32 devices in a mesh: sub: 8 (over z, y), crs: 4 (over x, core).
Axes of the slice: x: 2, y: 2, z: 4, core: 2. Of those that a mesh axis runs over, the one named last changes fastest.
Arguments:
- jump_data: float32 [8, 4, 6, 384], P('sub', 'crs'), may hold values from -6 to 6
- lumped_scale: float32 [8, 4, 384], P('sub', 'crs'), may hold values from 0.3 to 3
- schur_inverse: float32 [8, 4, 768, 768], P('sub', 'crs'), as said below
- coarse_coupling: float32 [8, 4, 24, 768], P('sub', 'crs'), may hold values from -0.4375 to 0.4375
- corner_inverse: float32 [1024, 1024], P(None, 'crs'), as said below
- own_dof: int32 [8, 4, 384], P('sub', 'crs'), may hold values from 0 to 767, as said below
- nbr_dof: int32 [8, 4, 384], P('sub', 'crs'), may hold values from 0 to 767, as said below
- live_count: int32 [8, 4], P('sub', 'crs'), may hold values from 1 to 384, as said below
- corner_index: int32 [8, 4, 24], P('sub', 'crs'), may hold values from 0 to 1023
Outputs:
- multipliers: float32 [8, 4, 6, 384], P('sub', 'crs')
- residual: float32 [8, 4, 6, 384], P('sub', 'crs')
The draws below stay inside these ranges and needn't reach their ends.
Inputs may be any that keep to these rules, and one draw needn't show every extreme that they name: `own_dof`: the 384 entries of one subdomain are distinct. `nbr_dof`: the 384 entries of one subdomain are distinct. `live_count`: some subdomain has all 384 slots live. `schur_inverse`: symmetric positive definite. `corner_inverse`: symmetric positive definite.
All inputs are finite; a program needn't handle non-finite values.
Results may differ from the reference program's by a relative error of at most 0.00021.
Values sent between devices are 32-bit elements; how exact they have to be, the bound alone decides.
No kernel may reach another device: no remote copies, remote signals or barrier semaphores. Data moves between devices by JAX's collectives and lax.ppermute only.
A program may use at most 64 MiB of HBM per device.

```python
import math
import jax
import jax.numpy as jnp
from jax import lax

IFACE = 768
LAM = 384
NCS = 24
CASES = 6
ITERS = 2
CHAIN = 8
SLABS = 4
NCORNER = 1024


def draw_schur_inverse(key, part):
    first, second = jax.random.split(jax.random.fold_in(key, 11))
    raw = jax.random.normal(first, (CHAIN, SLABS, IFACE, IFACE), jnp.float32)
    sym = (raw + jnp.swapaxes(raw, -1, -2)) * (0.25 / IFACE ** 0.5)
    diag = jax.random.uniform(second, (CHAIN, SLABS, IFACE), jnp.float32, 1.0, 2.0)
    return sym + diag[..., :, None] * jnp.eye(IFACE, dtype=jnp.float32)


def draw_corner_inverse(key, part):
    first, second = jax.random.split(jax.random.fold_in(key, 23))
    raw = jax.random.normal(first, (NCORNER, NCORNER), jnp.float32)
    sym = (raw + raw.T) * (0.25 / NCORNER ** 0.5)
    diag = jax.random.uniform(second, (NCORNER,), jnp.float32, 1.0, 2.0)
    return sym + jnp.diag(diag)


def draw_slots(key, salt):
    keys = jax.random.split(jax.random.fold_in(key, salt), CHAIN * SLABS)
    picks = jax.vmap(lambda k: jax.random.permutation(k, IFACE)[:LAM])(keys)
    return picks.reshape(CHAIN, SLABS, LAM).astype(jnp.int32)


def draw_own_dof(key, part):
    return draw_slots(key, 31)


def draw_nbr_dof(key, part):
    return draw_slots(key, 37)


def draw_live_count(key, part):
    first, second, third = jax.random.split(jax.random.fold_in(key, 41), 3)
    left = jax.random.randint(first, (CHAIN, SLABS), 0, LAM)
    right = jax.random.randint(second, (CHAIN, SLABS), 0, LAM)
    counts = 1 + left * right // LAM
    where_full = jax.random.randint(third, (), 0, CHAIN * SLABS)
    places = jnp.arange(CHAIN * SLABS, dtype=jnp.int32).reshape(CHAIN, SLABS)
    return jnp.where(places == where_full, LAM, counts).astype(jnp.int32)


def plant(array, rng, low, largest):
    place = [jax.random.randint(jax.random.fold_in(rng, axis), (), 0, length) for axis, length in enumerate(array.shape)]
    longest = array.shape.index(max(array.shape))
    beside = place[:longest] + [(place[longest] + 1) % array.shape[longest]] + place[longest + 1:]
    return array.at[tuple(place)].set(low).at[tuple(beside)].set(largest)


def block_scale(key, extent, cuts, smallest, top_value):
    gain = 1.0
    for dim, blocks in cuts:
        steps = jax.random.uniform(jax.random.fold_in(jax.random.fold_in(key, 6), dim), (blocks,), jnp.float32, smallest / len(cuts), top_value / len(cuts))
        gain = gain * jnp.repeat(jnp.exp(steps), extent[dim] // blocks).reshape((-1,) + (1,) * (len(extent) - 1 - dim))
    return gain


def normal_values(key, extent, scale, reach, cuts=(), kind=jnp.bfloat16):
    entries = jax.random.normal(key, extent, jnp.float32) * scale
    if len(cuts) > 0:
        entries = block_scale(key, extent, cuts, -0.22, 0.18) * entries
    return jnp.clip(entries, min=-reach, max=reach).astype(kind)


def setup_inputs(seed: int = 0) -> dict:
    key_of = jax.random.split(jax.random.key(seed), 10)
    return {
        "jump_data": normal_values(key_of[0], (CHAIN, SLABS, CASES, LAM), 1.0, 6.0, ((0, 8), (1, 4)), jnp.float32),
        "lumped_scale": jnp.clip(jnp.exp(math.log(3.0) - 2.3025851 * jax.random.uniform(key_of[1], (CHAIN, SLABS, LAM), jnp.float32) ** block_scale(key_of[1], (CHAIN, SLABS, LAM), ((0, 8), (1, 4)), -0.2, 0.2)), 0.3, 3.0),
        "schur_inverse": draw_schur_inverse(jax.random.fold_in(key_of[9], 71), 0),
        "coarse_coupling": normal_values(key_of[3], (CHAIN, SLABS, NCS, IFACE), (IFACE // 4) ** -0.5, 0.4375, ((0, 8), (1, 4)), jnp.float32),
        "corner_inverse": draw_corner_inverse(jax.random.fold_in(key_of[9], 71), 0),
        "own_dof": draw_own_dof(jax.random.fold_in(key_of[9], 71), 0),
        "nbr_dof": draw_nbr_dof(jax.random.fold_in(key_of[9], 71), 0),
        "live_count": draw_live_count(jax.random.fold_in(key_of[9], 71), 0),
        "corner_index": plant(jax.random.randint(key_of[8], (CHAIN, SLABS, NCS), 0, NCORNER), jax.random.fold_in(key_of[8], 1), 0, NCORNER - 1).astype(jnp.int32),
    }


def spread_rows(values, index):
    return jax.vmap(lambda v, i: jnp.zeros((CASES, IFACE), jnp.float32).at[:, i].add(v))(values, index)


def pick_rows(values, index):
    return jax.vmap(lambda v, i: v[:, i])(values, index)


def reference(jump_data, lumped_scale, schur_inverse, coarse_coupling, corner_inverse, own_dof, nbr_dof, live_count, corner_index):
    highest = lax.Precision.HIGHEST
    count = CHAIN * SLABS
    live = (jnp.arange(LAM, dtype=jnp.int32)[None, None, :] < live_count[:, :, None]).astype(jnp.float32)
    live_flat = live.reshape(count, LAM)
    own_flat = own_dof.reshape(count, LAM)
    nbr_flat = nbr_dof.reshape(count, LAM)
    flat_corner = corner_index.reshape(count * NCS)

    def operate(field):
        masked = field.reshape(count, CASES, LAM) * live_flat[:, None, :]
        own_load = spread_rows(masked, own_flat).reshape(CHAIN, SLABS, CASES, IFACE)
        next_load = spread_rows(masked, nbr_flat).reshape(CHAIN, SLABS, CASES, IFACE)
        load = own_load - jnp.roll(next_load, 1, axis=0)
        local_part = jnp.einsum("csij,csjk->csik", load, schur_inverse, precision=highest)
        corner_force = jnp.einsum("csij,csnj->csin", load, coarse_coupling, precision=highest)
        moved = jnp.transpose(corner_force, (2, 0, 1, 3)).reshape(CASES, count * NCS)
        corner_total = jnp.zeros((CASES, NCORNER), jnp.float32).at[:, flat_corner].add(moved)
        corner_solution = jnp.dot(corner_total, corner_inverse, precision=highest)
        picked = jnp.transpose(corner_solution[:, corner_index], (1, 2, 0, 3))
        displacement = local_part + jnp.einsum("csin,csnj->csij", picked, coarse_coupling, precision=highest)
        here = displacement.reshape(count, CASES, IFACE)
        beyond = jnp.roll(displacement, -1, axis=0).reshape(count, CASES, IFACE)
        image = (pick_rows(here, own_flat) - pick_rows(beyond, nbr_flat)) * live_flat[:, None, :]
        return image.reshape(CHAIN, SLABS, CASES, LAM)

    def inner(left, right):
        return jnp.sum(left * right, axis=(0, 1, 3))

    scale = lumped_scale[:, :, None, :]
    residual = jump_data * live[:, :, None, :]
    multipliers = jnp.zeros_like(residual)
    precon = scale * residual
    direction = precon
    norm_now = inner(residual, precon)
    for step in range(ITERS):
        image = operate(direction)
        alpha = (norm_now / inner(direction, image))[None, None, :, None]
        multipliers = multipliers + alpha * direction
        residual = residual - alpha * image
        if step + 1 < ITERS:
            precon = scale * residual
            norm_next = inner(residual, precon)
            direction = precon + (norm_next / norm_now)[None, None, :, None] * direction
            norm_now = norm_next
    return multipliers, residual
```

```python
import functools

import jax
import jax.numpy as jnp
from jax import lax
from jax.experimental import pallas as pl
from jax.experimental.pallas import tpu as pltpu
from jax.sharding import PartitionSpec as P

F32 = jnp.float32
BF16 = jnp.bfloat16
ROWS = 8
LANES = 128
SLOT = 32
GROUP = LANES // SLOT
VMEM_LIMIT = 40 << 20


def parts(x, count):
    out = []
    for _ in range(count):
        out.append(x.astype(BF16))
        x = x - out[-1].astype(F32)
    return out


def dot(a, b, transposed=False):
    dims = (((1,), (1 if transposed else 0,)), ((), ()))
    return lax.dot_general(a, b, dims, preferred_element_type=F32)


def moved(a, chosen, transposed=False):
    rows = a.shape[0]
    all_parts = dot(jnp.concatenate(parts(a, 3), axis=0), chosen, transposed)
    return all_parts[:rows] + all_parts[rows : 2 * rows] + all_parts[2 * rows :]


def product(a, high, low, transposed=False):
    rows = a.shape[0]
    top, rest = parts(a, 2)
    both = dot(jnp.concatenate([top, rest], axis=0), high, transposed)
    return both[:rows] + both[rows:] + dot(top, low, transposed)


def chosen_columns(index, count):
    shape = (count, index.shape[1])
    rows = lax.broadcasted_iota(jnp.int32, shape, 0)
    return jnp.where(rows == index, 1.0, 0.0).astype(BF16)


def row_sum(x):
    return jnp.sum(x, axis=1, keepdims=True)


def padded(x, rows):
    return jnp.concatenate([x, jnp.zeros((rows - x.shape[0], x.shape[1]), x.dtype)], axis=0)


def pack_kernel(live_ref, jump_ref, scale_ref, nbr_ref, out_ref):
    cases, records = jump_ref.shape[2:]
    live = lax.broadcasted_iota(jnp.int32, (1, records), 1) < live_ref[0, 0]
    live = live.astype(F32)
    out_ref[:cases] = jump_ref[0, 0] * live
    out_ref[cases : cases + 1] = scale_ref[0] * live
    out_ref[cases + 1 : cases + 2] = nbr_ref[0].astype(F32)


def unpacked(pack, cases):
    rows = lax.broadcasted_iota(jnp.int32, pack.shape, 0)
    residual = jnp.where(rows < cases, pack, 0.0)
    return residual, pack[cases : cases + 1], pack[cases + 1 : cases + 2].astype(jnp.int32)


def prepare_kernel(
    cases, pack_ref, schur_ref, coupling_ref, inverse_ref, own_ref,
    s_high, s_low, inv_high, inv_low, c_high, c_low, own_map, own_coupling, load_ref,
):
    s_high[...], s_low[...] = parts(schur_ref[0, 0], 2)
    inv_high[...], inv_low[...] = parts(inverse_ref[...], 2)
    coupling = coupling_ref[0, 0]
    block = padded(coupling, SLOT)
    c_high[...], c_low[...] = parts(jnp.concatenate([block] * GROUP, axis=0), 2)
    chosen = chosen_columns(own_ref[0], coupling.shape[1])
    own_map[...] = chosen
    own_coupling[...] = moved(coupling, chosen)
    residual, scale, _ = unpacked(pack_ref[...], cases)
    load_ref[...] = moved(residual * scale, chosen, True)


def forces(load, through, first, c_high, c_low, index_ref, cases, send_ref):
    force = product(load, c_high[...], c_low[...], True)
    lane = lax.broadcasted_iota(jnp.int32, force.shape, 1) % SLOT
    row = lax.broadcasted_iota(jnp.int32, force.shape, 0)
    force = jnp.where(lane == SLOT - 2, first, force)
    force = jnp.where(lane == SLOT - 1, row_sum(load * through), force)
    force = jnp.where(row == cases, index_ref[...], force)
    send_ref[...] = jnp.broadcast_to(force[None], send_ref.shape)


def first_kernel(
    cases, left_ref, pack_ref, load_ref, coupling_ref, own_coupling, index_ref,
    s_high, s_low, c_high, c_low, own_map,
    send_ref, right_ref, back_ref, left_map,
):
    left_residual, left_scale, left_index = unpacked(left_ref[...], cases)
    chosen = chosen_columns(left_index, coupling_ref.shape[3])
    left_map[...] = chosen
    load = load_ref[...] - moved(left_residual * left_scale, chosen, True)
    through = product(load, s_high[...], s_low[...])
    residual, scale, _ = unpacked(pack_ref[...], cases)
    norm = row_sum(residual * residual * scale)
    forces(load, through, norm, c_high, c_low, index_ref, cases, send_ref)
    right_ref[:ROWS] = moved(through, own_map[...])
    right_ref[ROWS:] = own_coupling[...]
    back_ref[:ROWS] = moved(through, chosen)
    back_ref[ROWS:] = moved(coupling_ref[0, 0], chosen)


def coarse_kernel(cases, place_ref, all_ref, inv_high, inv_low, x_ref, total_ref, sums_ref, index_ref):
    devices = all_ref.shape[0]
    corners = total_ref.shape[1]
    chunk = min(devices, LANES // GROUP)
    lane = lax.broadcasted_iota(jnp.int32, (ROWS, LANES), 1) // SLOT
    row = lax.broadcasted_iota(jnp.int32, (ROWS, 1), 0)
    step = min(corners, 1024)

    def add(at):
        pieces = []
        sums = jnp.zeros((ROWS, LANES), F32)
        for group in range(chunk // GROUP):
            piece = all_ref[at + group * GROUP]
            sums = sums + piece
            for e in range(1, GROUP):
                other = all_ref[at + group * GROUP + e]
                sums = sums + other
                piece = jnp.where(lane == e, other, piece)
            pieces.append(piece)
        flat = jnp.concatenate(pieces, axis=1)
        index = flat[cases : cases + 1].astype(jnp.int32)
        force = jnp.where(row < cases, flat, 0.0)
        total = [
            moved(force, chosen_columns(index - start, step), True)
            for start in range(0, corners, step)
        ]
        return sums, jnp.concatenate(total, axis=1)

    sums, total = add(0)
    sums_ref[...] = sums
    total_ref[...] = total
    if devices > chunk:

        @pl.loop(1, devices // chunk)
        def _(i):
            sums, total = add(i * chunk)
            sums_ref[...] += sums
            total_ref[...] += total

    x_ref[...] = product(total_ref[...], inv_high[...], inv_low[...])
    index = all_ref[place_ref[0], cases : cases + 1]
    for e in (1, 2):
        index = jnp.where(lane[:1] == e, all_ref[place_ref[e], cases : cases + 1], index)
    index_ref[...] = jnp.broadcast_to(index, index_ref.shape)


def picked_corners(place_ref, pieces, whole, index_ref):
    width = pieces[0].shape[1]
    for m, piece in enumerate(pieces):
        base = lax.rem(place_ref[3] + m, len(pieces)) * width
        whole[:, pl.ds(pl.multiple_of(base, width), width)] = piece[...]
    solution = whole[...]
    index = index_ref[:1].astype(jnp.int32)
    return solution, moved(solution, chosen_columns(index, solution.shape[1]))


def column(x, lane):
    return x[:, lane : lane + 1]


def second_kernel(
    cases, count, place_ref, *refs,
):
    pieces = refs[:count]
    (
        total_ref, sums_ref, index_ref, pack_ref, left_ref, right_ref, back_ref, from_left, from_right,
        own_map, left_map, s_high, s_low, c_high, c_low, corner_ref,
        send_ref, out_ref, keep_ref, spread_ref, scalar_ref, whole,
    ) = refs[count:]
    solution, picked = picked_corners(place_ref, pieces, whole, index_ref)
    blank = jnp.zeros((SLOT - (right_ref.shape[0] - ROWS), right_ref.shape[1]), F32)
    none = jnp.zeros((SLOT, right_ref.shape[1]), F32)
    own = jnp.concatenate([none, right_ref[ROWS:], blank, -from_right[ROWS:], blank, none], axis=0)
    other = jnp.concatenate([from_left[ROWS:], blank, -back_ref[ROWS:], blank, none, none], axis=0)
    spread_ref[...] = own
    both = product(picked, *parts(jnp.concatenate([own, other], axis=1), 2))
    records = right_ref.shape[1]
    residual, scale, _ = unpacked(pack_ref[...], cases)
    left_residual, left_scale, _ = unpacked(left_ref[...], cases)
    live = (scale > 0.0).astype(F32)
    left_live = (left_scale > 0.0).astype(F32)
    image = (right_ref[:ROWS] - from_right[:ROWS] + both[:, :records]) * live
    left_image = (from_left[:ROWS] - back_ref[:ROWS] + both[:, records:]) * left_live
    norm = column(sums_ref[...], SLOT - 2)
    curvature = column(sums_ref[...], SLOT - 1) + row_sum(total_ref[...] * solution)
    row = lax.broadcasted_iota(jnp.int32, (ROWS, 1), 0)
    alpha = jnp.where(row < cases, norm / curvature, 0.0)
    residual = residual - alpha * image
    left_residual = left_residual - alpha * left_image
    precon = scale * residual
    left_precon = left_scale * left_residual
    load = moved(precon, own_map[...], True) - moved(left_precon, left_map[...], True)
    through = product(load, s_high[...], s_low[...])
    forces(load, through, row_sum(residual * precon), c_high, c_low, corner_ref, cases, send_ref)
    out_ref[...] = moved(through, left_map[...])
    keep_ref[:ROWS] = moved(through, own_map[...])
    keep_ref[ROWS:] = image
    lane = lax.broadcasted_iota(jnp.int32, scalar_ref.shape, 1)
    scalar_ref[...] = jnp.where(lane == 0, norm, alpha)


def last_kernel(cases, count, place_ref, *refs):
    pieces = refs[:count]
    (
        total_ref, sums_ref, index_ref, pack_ref, from_right, keep_ref, spread_ref, scalar_ref,
        multipliers_ref, residual_ref, whole,
    ) = refs[count:]
    solution, picked = picked_corners(place_ref, pieces, whole, index_ref)
    residual, scale, _ = unpacked(pack_ref[...], cases)
    live = (scale > 0.0).astype(F32)
    coarse = product(picked, *parts(spread_ref[...], 2))
    image = (keep_ref[:ROWS] - from_right[...] + coarse) * live
    along = keep_ref[ROWS:]
    first_norm = column(scalar_ref[...], 0)
    first_alpha = column(scalar_ref[...], 1)
    norm = column(sums_ref[...], SLOT - 2)
    curvature = column(sums_ref[...], SLOT - 1) + row_sum(total_ref[...] * solution)
    ratio = norm / first_norm
    alpha = norm / (curvature - ratio * norm / first_alpha)
    direction = scale * residual
    multipliers = first_alpha * direction
    residual = residual - first_alpha * along
    direction = scale * residual + ratio * direction
    along = image + ratio * along
    multipliers = multipliers + alpha * direction
    residual = residual - alpha * along
    multipliers_ref[0, 0] = multipliers[:cases]
    residual_ref[0, 0] = residual[:cases]


VM = pl.BlockSpec(memory_space=pltpu.VMEM)
SM = pl.BlockSpec(memory_space=pltpu.SMEM)


def call(kernel, outs, given, scalars=0, scratch=()):
    return pl.pallas_call(
        kernel,
        out_shape=[jax.ShapeDtypeStruct(shape, kind) for shape, kind in outs],
        in_specs=[SM] * scalars + [VM] * (len(given) - scalars),
        out_specs=[VM] * len(outs),
        scratch_shapes=list(scratch),
        compiler_params=pltpu.CompilerParams(vmem_limit_bytes=VMEM_LIMIT),
    )(*given)


def passed_along(value, axis, steps):
    count = lax.axis_size(axis)
    pairs = [(source, (source + steps) % count) for source in range(count)]
    return lax.ppermute(value, axis, pairs)


def per_device(
    jump_data,
    lumped_scale,
    schur_inverse,
    coarse_coupling,
    corner_inverse,
    own_dof,
    nbr_dof,
    live_count,
    corner_index,
):
    cases, records = jump_data.shape[2:]
    held, iface = coarse_coupling.shape[2:]
    corners, width = corner_inverse.shape
    chain, slabs = lax.axis_size("sub"), lax.axis_size("crs")
    devices = chain * slabs
    here, slab = lax.axis_index("sub"), lax.axis_index("crs")
    place = jnp.stack(
        [
            (here + chain - 1) % chain * slabs + slab,
            here * slabs + slab,
            (here + 1) % chain * slabs + slab,
            slab,
        ]
    ).astype(jnp.int32)
    index = jnp.pad(corner_index[0, 0].astype(F32), (0, SLOT - held), constant_values=-1.0)
    index = jnp.tile(index, GROUP)[None]

    (pack,) = call(
        pack_kernel, [((ROWS, records), F32)], (live_count, jump_data, lumped_scale, nbr_dof), 1
    )
    left = passed_along(pack, "sub", 1)
    s_high, s_low, inv_high, inv_low, c_high, c_low, own_map, own_coupling, load = call(
        functools.partial(prepare_kernel, cases),
        [
            ((iface, iface), BF16),
            ((iface, iface), BF16),
            ((corners, width), BF16),
            ((corners, width), BF16),
            ((LANES, iface), BF16),
            ((LANES, iface), BF16),
            ((iface, records), BF16),
            ((held, records), F32),
            ((ROWS, iface), F32),
        ],
        (pack, schur_inverse, coarse_coupling, corner_inverse, own_dof),
    )
    send, right, back, left_map = call(
        functools.partial(first_kernel, cases),
        [
            ((devices, ROWS, LANES), F32),
            ((ROWS + held, records), F32),
            ((ROWS + held, records), F32),
            ((iface, records), BF16),
        ],
        (
            left, pack, load, coarse_coupling, own_coupling, index,
            s_high, s_low, c_high, c_low, own_map,
        ),
    )

    def coarse(send):
        gathered = lax.all_to_all(send, ("sub", "crs"), 0, 0)
        x, total, sums, near = call(
            functools.partial(coarse_kernel, cases),
            [
                ((ROWS, width), F32),
                ((ROWS, corners), F32),
                ((ROWS, LANES), F32),
                ((ROWS, LANES), F32),
            ],
            (place, gathered, inv_high, inv_low),
            1,
        )
        pieces = [x] + [passed_along(x, "crs", -m) for m in range(1, slabs)]
        return pieces, total, sums, near

    from_left = passed_along(right, "sub", 1)
    from_right = passed_along(back, "sub", -1)
    pieces, total, sums, near = coarse(send)
    whole = [pltpu.VMEM((ROWS, corners), F32)]
    send, out, keep, spread, scalars = call(
        functools.partial(second_kernel, cases, slabs),
        [
            ((devices, ROWS, LANES), F32),
            ((ROWS, records), F32),
            ((2 * ROWS, records), F32),
            ((LANES, records), F32),
            ((ROWS, LANES), F32),
        ],
        (
            place, *pieces, total, sums, near, pack, left, right, back, from_left, from_right,
            own_map, left_map, s_high, s_low, c_high, c_low, index,
        ),
        1,
        whole,
    )
    from_right = passed_along(out, "sub", -1)
    pieces, total, sums, near = coarse(send)
    shape = jump_data.shape
    return tuple(
        call(
            functools.partial(last_kernel, cases, slabs),
            [(shape, F32), (shape, F32)],
            (
                place, *pieces, total, sums, near, pack, from_right, keep, spread, scalars,
            ),
            1,
            whole,
        )
    )


def solution(mesh):
    return jax.shard_map(
        per_device,
        mesh=mesh,
        in_specs=(
            P("sub", "crs", None, None),
            P("sub", "crs", None),
            P("sub", "crs", None, None),
            P("sub", "crs", None, None),
            P(None, "crs"),
            P("sub", "crs", None),
            P("sub", "crs", None),
            P("sub", "crs"),
            P("sub", "crs", None),
        ),
        out_specs=(P("sub", "crs", None, None), P("sub", "crs", None, None)),
        check_vma=False,
    )
```

```python
import functools

import jax
import jax.numpy as jnp
from jax import lax
from jax.experimental import pallas as pl
from jax.experimental.pallas import tpu as pltpu
from jax.sharding import PartitionSpec as P

F32 = jnp.float32
BF16 = jnp.bfloat16
ROWS = 8
LANES = 128
SLOT = 32
GROUP = LANES // SLOT
VMEM_LIMIT = 24 << 20


def parts(x, count):
    out = []
    for _ in range(count):
        out.append(x.astype(BF16))
        x = x - out[-1].astype(F32)
    return out


def dot(a, b, transposed=False):
    dims = (((1,), (1 if transposed else 0,)), ((), ()))
    return lax.dot_general(a, b, dims, preferred_element_type=F32)


def moved(a, chosen, transposed=False):
    rows = a.shape[0]
    all_parts = dot(jnp.concatenate(parts(a, 3), axis=0), chosen, transposed)
    return all_parts[:rows] + all_parts[rows : 2 * rows] + all_parts[2 * rows :]


def moved_parts(high, low, chosen):
    both = dot(jnp.concatenate([high, low], axis=0), chosen)
    return both[: high.shape[0]] + both[high.shape[0] :]


def product(a, high, low, transposed=False):
    rows = a.shape[0]
    top, rest = parts(a, 2)
    both = dot(jnp.concatenate([top, rest], axis=0), high, transposed)
    return both[:rows] + both[rows:] + dot(top, low, transposed)


def chosen_columns(index, count):
    shape = (count, index.shape[1])
    rows = lax.broadcasted_iota(jnp.int32, shape, 0)
    return jnp.where(rows == index, 1.0, 0.0).astype(BF16)


def row_sum(x):
    return jnp.sum(x, axis=1, keepdims=True)


def padded(x, rows):
    return jnp.concatenate([x, jnp.zeros((rows - x.shape[0], x.shape[1]), x.dtype)], axis=0)


def fetched(pairs, sems):
    copies = [
        pltpu.make_async_copy(source, target, sems.at[i]) for i, (source, target) in enumerate(pairs)
    ]
    for copy in copies:
        copy.start()
    return copies


def pack_kernel(
    live_ref, place_ref, jump_hbm, scale_hbm, nbr_hbm, inverse_hbm, out_ref, half_ref, jump, scale, nbr, sems,
):
    cases, _, records = jump.shape
    copies = fetched(
        [
            (jump_hbm, jump),
            (scale_hbm, scale),
            (nbr_hbm, nbr),
            (half_of(place_ref[3], inverse_hbm), half_ref),
        ],
        sems,
    )
    for copy in copies:
        copy.wait()
    live = lax.broadcasted_iota(jnp.int32, (1, records), 1) < live_ref[0, 0]
    live = live.astype(F32)
    for case in range(cases):
        out_ref[case : case + 1] = jump[case] * live
    out_ref[cases : cases + 1] = scale[0] * live
    out_ref[cases + 1 : cases + 2] = nbr[0].astype(F32)


def unpacked(pack, cases):
    rows = lax.broadcasted_iota(jnp.int32, pack.shape, 0)
    residual = jnp.where(rows < cases, pack, 0.0)
    return residual, pack[cases : cases + 1], pack[cases + 1 : cases + 2].astype(jnp.int32)


def half_of(slab, inverse_hbm):
    rows = 2 * inverse_hbm.shape[1]
    first = jnp.minimum(slab // 2 * rows, inverse_hbm.shape[0] - rows)
    return inverse_hbm.at[pl.ds(pl.multiple_of(first, 8), rows)]


def prepare_kernel(
    cases, pack_ref, schur_hbm, coupling_hbm, own_hbm, corner_hbm,
    s_high, s_low, c_high, c_low, own_coupling, load_ref, index_ref, own_ref,
    schur, coupling, own, corner, sems,
):
    copies = fetched(
        [
            (own_hbm, own),
            (coupling_hbm, coupling),
            (corner_hbm, corner),
            (schur_hbm, schur),
        ],
        sems,
    )
    for copy in copies[:3]:
        copy.wait()
    held, iface = coupling.shape[2:]
    block = padded(coupling[0, 0], SLOT)
    c_high[...], c_low[...] = parts(block, 2)
    chosen = chosen_columns(own[0], iface)
    own_ref[...] = own[0]
    own_coupling[...] = moved_parts(c_high[...], c_low[...], chosen)[:held]
    residual, scale, _ = unpacked(pack_ref[...], cases)
    load_ref[...] = moved(residual * scale, chosen, True)
    lane = lax.broadcasted_iota(jnp.int32, (held, LANES), 1) % SLOT
    tiles = jnp.where(lane == lax.broadcasted_iota(jnp.int32, (held, LANES), 0), 1.0, 0.0)
    index = jnp.broadcast_to(corner[0].astype(F32), (ROWS, held))
    index_ref[...] = jnp.where(lane[:1] < held, moved(index, tiles.astype(BF16))[:1], -1.0)
    copies[3].wait()
    s_high[...], s_low[...] = parts(schur[0, 0], 2)


def forces(load, through, first, c_high, c_low, index_ref, cases, send_ref):
    high, low = [jnp.concatenate([c[...]] * GROUP, axis=0) for c in (c_high, c_low)]
    force = product(load, high, low, True)
    lane = lax.broadcasted_iota(jnp.int32, force.shape, 1) % SLOT
    row = lax.broadcasted_iota(jnp.int32, force.shape, 0)
    force = jnp.where(lane == SLOT - 2, first, force)
    force = jnp.where(lane == SLOT - 1, row_sum(load * through), force)
    force = jnp.where(row == cases, index_ref[...], force)
    send_ref[...] = jnp.broadcast_to(force[None], send_ref.shape)


def first_kernel(
    cases, left_ref, pack_ref, load_ref, own_coupling, index_ref,
    s_high, s_low, c_high, c_low, own_ref,
    send_ref, right_ref, back_ref,
):
    left_residual, left_scale, left_index = unpacked(left_ref[...], cases)
    chosen = chosen_columns(left_index, load_ref.shape[1])
    load = load_ref[...] - moved(left_residual * left_scale, chosen, True)
    through = product(load, s_high[...], s_low[...])
    residual, scale, _ = unpacked(pack_ref[...], cases)
    norm = row_sum(residual * residual * scale)
    forces(load, through, norm, c_high, c_low, index_ref, cases, send_ref)
    right_ref[:ROWS] = moved(through, chosen_columns(own_ref[...], load_ref.shape[1]))
    right_ref[ROWS:] = own_coupling[...]
    back_ref[:ROWS] = moved(through, chosen)
    held = own_coupling.shape[0]
    back_ref[ROWS:] = moved_parts(c_high[...], c_low[...], chosen)[:held]


def gathered_forces(cases, all_ref, corners, flip, sums_ref, total_ref):
    devices = all_ref.shape[0]
    chunk = min(devices, LANES // GROUP)
    lane = lax.broadcasted_iota(jnp.int32, (ROWS, LANES), 1) // SLOT
    row = lax.broadcasted_iota(jnp.int32, (ROWS, 1), 0)
    step = min(corners, 1024)

    def add(at):
        pieces = []
        sums = jnp.zeros((ROWS, LANES), F32)
        for group in range(chunk // GROUP):
            piece = all_ref[at + group * GROUP]
            sums = sums + piece
            for e in range(1, GROUP):
                other = all_ref[at + group * GROUP + e]
                sums = sums + other
                piece = jnp.where(lane == e, other, piece)
            pieces.append(piece)
        flat = jnp.concatenate(pieces, axis=1)
        index = flat[cases : cases + 1].astype(jnp.int32) ^ flip
        force = jnp.where(row < cases, flat, 0.0)
        total = [
            moved(force, chosen_columns(index - start, step), True)
            for start in range(0, corners, step)
        ]
        return sums, jnp.concatenate(total, axis=1)

    sums_ref[...], total_ref[...] = add(0)
    if devices > chunk:

        @pl.loop(1, devices // chunk)
        def _(i):
            sums, total = add(i * chunk)
            sums_ref[...] += sums
            total_ref[...] += total


def near_index(cases, place_ref, all_ref):
    lane = lax.broadcasted_iota(jnp.int32, (1, LANES), 1) // SLOT
    index = all_ref[place_ref[0], cases : cases + 1]
    for e in (1, 2):
        index = jnp.where(lane == e, all_ref[place_ref[e], cases : cases + 1], index)
    return index.astype(jnp.int32)


def coarse_kernel(cases, place_ref, all_ref, inverse_hbm, x_ref, total_ref, sums_ref, index_ref, inverse, sems):
    (copy,) = fetched([(inverse_hbm, inverse)], sems)
    gathered_forces(cases, all_ref, total_ref.shape[1], 0, sums_ref, total_ref)
    index_ref[...] = jnp.broadcast_to(near_index(cases, place_ref, all_ref), index_ref.shape)
    copy.wait()
    x_ref[...] = product(total_ref[...], *parts(inverse[...], 2))


def shared_coarse(cases, width, refs):
    place_ref, *pieces, total_ref, sums_ref, index_ref, whole = refs
    for m, piece in enumerate(pieces):
        base = lax.rem(place_ref[3] + m, len(pieces)) * width
        whole[:, pl.ds(pl.multiple_of(base, width), width)] = piece[...]
    return whole[...], total_ref[...], sums_ref[...], index_ref[:1]


def pair_kernel(
    cases, place_ref, all_ref, far_ref, inverse_hbm, _, x_ref, total_ref, sums_ref, index_ref, inverse, sems,
):
    width = inverse.shape[1]
    slab = place_ref[3]
    copies = fetched(
        [
            (
                inverse_hbm.at[pl.ds(pl.multiple_of((slab ^ j) * width, width), width)],
                inverse.at[pl.ds(j * width, width)],
            )
            for j in range(4)
        ],
        sems,
    )
    flip = slab * width
    gathered_forces(cases, all_ref, 4 * width, flip, sums_ref, total_ref)
    index = near_index(cases, place_ref, all_ref) ^ flip
    index_ref[...] = jnp.broadcast_to(index, index_ref.shape)
    total = total_ref[...]
    last = [
        far_ref[pl.ds(pl.multiple_of((slab % 2 ^ j) * width, width), width)] for j in range(2)
    ]
    third = product(total[:, 2 * width :], *parts(jnp.concatenate(last, axis=0), 2))
    for copy in copies:
        copy.wait()
    high, low = parts(inverse[...], 2)
    x_ref[:, :width] = product(total, high, low)
    x_ref[:, width : 2 * width] = jnp.zeros((ROWS, width), F32)
    across = product(total[:, :width], high[2 * width :], low[2 * width :], True)
    x_ref[:, 2 * width : 3 * width] = across[:, :width] + third
    x_ref[:, 3 * width :] = across[:, width:]


def paired_coarse(cases, width, refs):
    place_ref, x_ref, other_ref, total_ref, sums_ref, index_ref = refs
    other = [other_ref[:, (j ^ 1) * width : (j ^ 1) * width + width] for j in range(4)]
    solution = x_ref[...] + jnp.concatenate(other, axis=1)
    return solution, total_ref[...], sums_ref[...], index_ref[:1]


def column(x, lane):
    return x[:, lane : lane + 1]


def second_kernel(cases, coarse, given, *refs):
    (
        pack_ref, left_ref, right_ref, back_ref, from_left, from_right,
        s_high, s_low, c_high, c_low, corner_ref, own_ref,
        send_ref, out_ref, keep_ref, spread_ref, scalar_ref,
    ) = refs[given : given + 17]
    solution, total, sums, index = coarse(refs[:given] + refs[given + 17 :])
    picked = moved(solution, chosen_columns(index, solution.shape[1]))
    blank = jnp.zeros((SLOT - (right_ref.shape[0] - ROWS), right_ref.shape[1]), F32)
    none = jnp.zeros((SLOT, right_ref.shape[1]), F32)
    own = jnp.concatenate([none, right_ref[ROWS:], blank, -from_right[ROWS:], blank, none], axis=0)
    other = jnp.concatenate([from_left[ROWS:], blank, -back_ref[ROWS:], blank, none, none], axis=0)
    spread_ref[...] = own
    both = product(picked, *parts(jnp.concatenate([own, other], axis=1), 2))
    records = right_ref.shape[1]
    residual, scale, _ = unpacked(pack_ref[...], cases)
    left_residual, left_scale, left_index = unpacked(left_ref[...], cases)
    live = (scale > 0.0).astype(F32)
    left_live = (left_scale > 0.0).astype(F32)
    image = (right_ref[:ROWS] - from_right[:ROWS] + both[:, :records]) * live
    left_image = (from_left[:ROWS] - back_ref[:ROWS] + both[:, records:]) * left_live
    norm = column(sums, SLOT - 2)
    curvature = column(sums, SLOT - 1) + row_sum(total * solution)
    row = lax.broadcasted_iota(jnp.int32, (ROWS, 1), 0)
    alpha = jnp.where(row < cases, norm / curvature, 0.0)
    residual = residual - alpha * image
    left_residual = left_residual - alpha * left_image
    precon = scale * residual
    left_precon = left_scale * left_residual
    own_map = chosen_columns(own_ref[...], c_high.shape[1])
    left_map = chosen_columns(left_index, c_high.shape[1])
    load = moved(precon, own_map, True) - moved(left_precon, left_map, True)
    through = product(load, s_high[...], s_low[...])
    forces(load, through, row_sum(residual * precon), c_high, c_low, corner_ref, cases, send_ref)
    out_ref[...] = moved(through, left_map)
    keep_ref[:ROWS] = moved(through, own_map)
    keep_ref[ROWS:] = image
    lane = lax.broadcasted_iota(jnp.int32, scalar_ref.shape, 1)
    scalar_ref[...] = jnp.where(lane == 0, norm, alpha)


def last_kernel(cases, coarse, given, *refs):
    (
        pack_ref, from_right, keep_ref, spread_ref, scalar_ref, multipliers_ref, residual_ref,
    ) = refs[given : given + 7]
    solution, total, sums, index = coarse(refs[:given] + refs[given + 7 :])
    picked = moved(solution, chosen_columns(index, solution.shape[1]))
    residual, scale, _ = unpacked(pack_ref[...], cases)
    live = (scale > 0.0).astype(F32)
    spread = product(picked, *parts(spread_ref[...], 2))
    image = (keep_ref[:ROWS] - from_right[...] + spread) * live
    along = keep_ref[ROWS:]
    first_norm = column(scalar_ref[...], 0)
    first_alpha = column(scalar_ref[...], 1)
    norm = column(sums, SLOT - 2)
    curvature = column(sums, SLOT - 1) + row_sum(total * solution)
    ratio = norm / first_norm
    alpha = norm / (curvature - ratio * norm / first_alpha)
    direction = scale * residual
    multipliers = first_alpha * direction
    residual = residual - first_alpha * along
    direction = scale * residual + ratio * direction
    along = image + ratio * along
    multipliers = multipliers + alpha * direction
    residual = residual - alpha * along
    for case in range(cases):
        multipliers_ref[case] = multipliers[case : case + 1]
        residual_ref[case] = residual[case : case + 1]


VM = pl.BlockSpec(memory_space=pltpu.VMEM)
SM = pl.BlockSpec(memory_space=pltpu.SMEM)
HB = pl.BlockSpec(memory_space=pltpu.HBM)


def call(kernel, outs, given, specs, scratch=(), moved_bytes=None):
    specs = specs + [VM] * (len(given) - len(specs))
    given = [
        pltpu.with_memory_space_constraint(x, pltpu.HBM) if spec is HB else x
        for x, spec in zip(given, specs)
    ]
    return pl.pallas_call(
        kernel,
        out_shape=[jax.ShapeDtypeStruct(shape, kind) for shape, kind in outs],
        in_specs=specs,
        out_specs=[VM] * len(outs),
        scratch_shapes=list(scratch),
        cost_estimate=moved_bytes
        and pl.CostEstimate(flops=0, bytes_accessed=moved_bytes, transcendentals=0),
        compiler_params=pltpu.CompilerParams(vmem_limit_bytes=VMEM_LIMIT),
    )(*given)


def passed_along(value, axis, steps):
    count = lax.axis_size(axis)
    pairs = [(source, (source + steps) % count) for source in range(count)]
    return lax.ppermute(value, axis, pairs)


def exchanged(value, axis, bit):
    pairs = [(source, source ^ bit) for source in range(lax.axis_size(axis))]
    return lax.ppermute(value, axis, pairs)


def per_device(
    jump_data,
    lumped_scale,
    schur_inverse,
    coarse_coupling,
    corner_inverse,
    own_dof,
    nbr_dof,
    live_count,
    corner_index,
):
    cases, records = jump_data.shape[2:]
    held, iface = coarse_coupling.shape[2:]
    corners, width = corner_inverse.shape
    chain, slabs = lax.axis_size("sub"), lax.axis_size("crs")
    devices = chain * slabs
    here, slab = lax.axis_index("sub"), lax.axis_index("crs")
    place = jnp.stack(
        [
            (here + chain - 1) % chain * slabs + slab,
            here * slabs + slab,
            (here + 1) % chain * slabs + slab,
            slab,
        ]
    ).astype(jnp.int32)

    def buffers(*arrays):
        return [pltpu.VMEM(a.shape, a.dtype) for a in arrays] + [
            pltpu.SemaphoreType.DMA((len(arrays),))
        ]

    jump = jump_data.reshape(cases, 1, records)
    first = (jump, lumped_scale, nbr_dof)
    pack, half = call(
        pack_kernel,
        [((ROWS, records), F32), ((2 * width, width), F32)],
        (live_count, place, *first, corner_inverse),
        [SM, SM] + [HB] * 4,
        [*buffers(*first)[:-1], pltpu.SemaphoreType.DMA((4,))],
    )
    left = passed_along(pack, "sub", 1)
    fetched_here = (schur_inverse, coarse_coupling, own_dof, corner_index)
    s_high, s_low, c_high, c_low, own_coupling, load, index, own = call(
        functools.partial(prepare_kernel, cases),
        [
            ((iface, iface), BF16),
            ((iface, iface), BF16),
            ((SLOT, iface), BF16),
            ((SLOT, iface), BF16),
            ((held, records), F32),
            ((ROWS, iface), F32),
            ((1, LANES), F32),
            ((1, records), jnp.int32),
        ],
        (pack, *fetched_here),
        [VM] + [HB] * 4,
        buffers(*fetched_here),
        32 << 20,
    )
    is_paired = slabs == 4 and width & (width - 1) == 0
    if is_paired:
        far = exchanged(half, "crs", 2)
    send, right, back = call(
        functools.partial(first_kernel, cases),
        [
            ((devices, ROWS, LANES), F32),
            ((ROWS + held, records), F32),
            ((ROWS + held, records), F32),
        ],
        (left, pack, load, own_coupling, index, s_high, s_low, c_high, c_low, own),
        [],
    )

    def gathered(send, beside):
        everyone = lax.all_to_all(send, ("sub", "crs"), 0, 0)
        row = (ROWS, corners)
        outs = [(row, F32), ((ROWS, LANES), F32), ((ROWS, LANES), jnp.int32)]
        if is_paired:
            x, *others = call(
                functools.partial(pair_kernel, cases),
                [(row, F32), *outs],
                (place, everyone, far, corner_inverse, beside),
                [SM, VM, VM, HB, VM],
                [pltpu.VMEM((corners, width), F32), pltpu.SemaphoreType.DMA((4,))],
            )
            return (
                (place, x, exchanged(x, "crs", 1), *others),
                [SM] + [VM] * 5,
                [],
                functools.partial(paired_coarse, cases, width),
            )
        x, *others = call(
            functools.partial(coarse_kernel, cases),
            [((ROWS, width), F32), *outs],
            (place, everyone, corner_inverse),
            [SM, VM, HB],
            buffers(corner_inverse),
        )
        pieces = [x] + [passed_along(x, "crs", -m) for m in range(1, slabs)]
        return (
            (place, *pieces, *others),
            [SM] + [VM] * (len(pieces) + len(others)),
            [pltpu.VMEM(row, F32)],
            functools.partial(shared_coarse, cases, width),
        )

    from_left = passed_along(right, "sub", 1)
    from_right = passed_along(back, "sub", -1)
    given, specs, scratch, coarse = gathered(send, from_right)
    send, out, keep, spread, scalars = call(
        functools.partial(second_kernel, cases, coarse, len(given)),
        [
            ((devices, ROWS, LANES), F32),
            ((ROWS, records), F32),
            ((2 * ROWS, records), F32),
            ((LANES, records), F32),
            ((ROWS, LANES), F32),
        ],
        (
            *given, pack, left, right, back, from_left, from_right,
            s_high, s_low, c_high, c_low, index, own,
        ),
        specs,
        scratch,
    )
    from_right = passed_along(out, "sub", -1)
    given, specs, scratch, coarse = gathered(send, from_right)
    outs = call(
        functools.partial(last_kernel, cases, coarse, len(given)),
        [(jump.shape, F32), (jump.shape, F32)],
        (*given, pack, from_right, keep, spread, scalars),
        specs,
        scratch,
    )
    return tuple(out.reshape(jump_data.shape) for out in outs)


def solution(mesh):
    return jax.shard_map(
        per_device,
        mesh=mesh,
        in_specs=(
            P("sub", "crs", None, None),
            P("sub", "crs", None),
            P("sub", "crs", None, None),
            P("sub", "crs", None, None),
            P(None, "crs"),
            P("sub", "crs", None),
            P("sub", "crs", None),
            P("sub", "crs"),
            P("sub", "crs", None),
        ),
        out_specs=(P("sub", "crs", None, None), P("sub", "crs", None, None)),
        check_vma=False,
    )
```

```python
import functools

import jax
import jax.numpy as jnp
from jax import lax
from jax.experimental import pallas as pl
from jax.experimental.pallas import tpu as pltpu
from jax.sharding import PartitionSpec as P

F32 = jnp.float32
BF16 = jnp.bfloat16
ROWS = 8
LANES = 128
SLOT = 32
GROUP = LANES // SLOT
VMEM_LIMIT = 24 << 20


def parts(x, count):
    out = []
    for _ in range(count):
        out.append(x.astype(BF16))
        x = x - out[-1].astype(F32)
    return out


def dot(a, b, transposed=False):
    dims = (((1,), (1 if transposed else 0,)), ((), ()))
    return lax.dot_general(a, b, dims, preferred_element_type=F32)


def moved(a, chosen, transposed=False):
    rows = a.shape[0]
    all_parts = dot(jnp.concatenate(parts(a, 3), axis=0), chosen, transposed)
    return all_parts[:rows] + all_parts[rows : 2 * rows] + all_parts[2 * rows :]


def moved_parts(high, low, chosen):
    both = dot(jnp.concatenate([high, low], axis=0), chosen)
    return both[: high.shape[0]] + both[high.shape[0] :]


def product(a, high, low, transposed=False):
    rows = a.shape[0]
    top, rest = parts(a, 2)
    both = dot(jnp.concatenate([top, rest], axis=0), high, transposed)
    return both[:rows] + both[rows:] + dot(top, low, transposed)


def chosen_columns(index, count):
    shape = (count, index.shape[1])
    rows = lax.broadcasted_iota(jnp.int32, shape, 0)
    return jnp.where(rows == index, 1.0, 0.0).astype(BF16)


def row_sum(x):
    return jnp.sum(x, axis=1, keepdims=True)


def padded(x, rows):
    return jnp.concatenate([x, jnp.zeros((rows - x.shape[0], x.shape[1]), x.dtype)], axis=0)


def fetched(pairs, sems):
    copies = [
        pltpu.make_async_copy(source, target, sems.at[i]) for i, (source, target) in enumerate(pairs)
    ]
    for copy in copies:
        copy.start()
    return copies


def pack_kernel(
    live_ref, jump_hbm, scale_hbm, nbr_hbm, inverse_hbm, out_ref, half_ref, jump, scale, nbr, sems,
):
    cases, _, records = jump.shape
    copies = fetched(
        [
            (jump_hbm, jump),
            (scale_hbm, scale),
            (nbr_hbm, nbr),
            (half_of(lax.axis_index("crs"), inverse_hbm), half_ref),
        ],
        sems,
    )
    for copy in copies:
        copy.wait()
    live = lax.broadcasted_iota(jnp.int32, (1, records), 1) < live_ref[0, 0]
    live = live.astype(F32)
    for case in range(cases):
        out_ref[case : case + 1] = jump[case] * live
    out_ref[cases : cases + 1] = scale[0] * live
    out_ref[cases + 1 : cases + 2] = nbr[0].astype(F32)


def unpacked(pack, cases):
    rows = lax.broadcasted_iota(jnp.int32, pack.shape, 0)
    residual = jnp.where(rows < cases, pack, 0.0)
    return residual, pack[cases : cases + 1], pack[cases + 1 : cases + 2].astype(jnp.int32)


def near_devices():
    chain, slabs = lax.axis_size("sub"), lax.axis_size("crs")
    here, slab = lax.axis_index("sub"), lax.axis_index("crs")
    return [lax.rem(here + step, chain) * slabs + slab for step in (chain - 1, 0, 1)]


def is_paired(width):
    return lax.axis_size("crs") == 4 and width & (width - 1) == 0


def block_at(slab, j, width):
    return slab ^ j if is_paired(width) else j


def half_of(slab, inverse_hbm):
    rows = 2 * inverse_hbm.shape[1]
    first = jnp.minimum(slab // 2 * rows, inverse_hbm.shape[0] - rows)
    return inverse_hbm.at[pl.ds(pl.multiple_of(first, 8), rows)]


def prepare_kernel(
    cases, pack_ref, schur_hbm, coupling_hbm, own_hbm, corner_hbm, inverse_hbm,
    s_high, s_low, c_high, c_low, own_coupling, load_ref, index_ref, own_ref, inv_high, inv_low,
    schur, coupling, own, corner, inverse, sems,
):
    copies = fetched(
        [
            (own_hbm, own),
            (coupling_hbm, coupling),
            (corner_hbm, corner),
            (inverse_hbm, inverse),
            (schur_hbm, schur),
        ],
        sems,
    )
    for copy in copies[:3]:
        copy.wait()
    held, iface = coupling.shape[2:]
    block = padded(coupling[0, 0], SLOT)
    c_high[...], c_low[...] = parts(block, 2)
    chosen = chosen_columns(own[0], iface)
    own_ref[...] = own[0]
    own_coupling[...] = moved_parts(c_high[...], c_low[...], chosen)[:held]
    residual, scale, _ = unpacked(pack_ref[...], cases)
    load_ref[...] = moved(residual * scale, chosen, True)
    lane = lax.broadcasted_iota(jnp.int32, (held, LANES), 1) % SLOT
    tiles = jnp.where(lane == lax.broadcasted_iota(jnp.int32, (held, LANES), 0), 1.0, 0.0)
    index = jnp.broadcast_to(corner[0].astype(F32), (ROWS, held))
    index_ref[...] = jnp.where(lane[:1] < held, moved(index, tiles.astype(BF16))[:1], -1.0)
    copies[3].wait()
    slab = lax.axis_index("crs")
    blocks = lax.axis_size("crs")
    width = inverse.shape[1]
    for j in range(blocks):
        rows = pl.ds(pl.multiple_of(block_at(slab, j, width) * width, width), width)
        high, low = parts(inverse[rows], 2)
        inv_high[j * width : (j + 1) * width] = high
        inv_low[j * width : (j + 1) * width] = low
    copies[4].wait()
    s_high[...], s_low[...] = parts(schur[0, 0], 2)


def forces(load, through, first, c_high, c_low, index_ref, cases, send_ref):
    high, low = [jnp.concatenate([c[...]] * GROUP, axis=0) for c in (c_high, c_low)]
    force = product(load, high, low, True)
    lane = lax.broadcasted_iota(jnp.int32, force.shape, 1) % SLOT
    row = lax.broadcasted_iota(jnp.int32, force.shape, 0)
    force = jnp.where(lane == SLOT - 2, first, force)
    force = jnp.where(lane == SLOT - 1, row_sum(load * through), force)
    force = jnp.where(row == cases, index_ref[...], force)
    send_ref[...] = jnp.broadcast_to(force[None], send_ref.shape)


def first_kernel(
    cases, left_ref, pack_ref, load_ref, own_coupling, index_ref,
    s_high, s_low, c_high, c_low, own_ref,
    send_ref, right_ref, back_ref,
):
    left_residual, left_scale, left_index = unpacked(left_ref[...], cases)
    chosen = chosen_columns(left_index, load_ref.shape[1])
    load = load_ref[...] - moved(left_residual * left_scale, chosen, True)
    through = product(load, s_high[...], s_low[...])
    residual, scale, _ = unpacked(pack_ref[...], cases)
    norm = row_sum(residual * residual * scale)
    forces(load, through, norm, c_high, c_low, index_ref, cases, send_ref)
    right_ref[:ROWS] = moved(through, chosen_columns(own_ref[...], load_ref.shape[1]))
    right_ref[ROWS:] = own_coupling[...]
    back_ref[:ROWS] = moved(through, chosen)
    held = own_coupling.shape[0]
    back_ref[ROWS:] = moved_parts(c_high[...], c_low[...], chosen)[:held]


def gathered_forces(cases, all_ref, corners, flip, sums_ref, total_ref):
    devices = all_ref.shape[0]
    chunk = min(devices, LANES // GROUP)
    lane = lax.broadcasted_iota(jnp.int32, (ROWS, LANES), 1) // SLOT
    row = lax.broadcasted_iota(jnp.int32, (ROWS, 1), 0)
    step = min(corners, 1024)

    def add(at):
        pieces = []
        sums = jnp.zeros((ROWS, LANES), F32)
        for group in range(chunk // GROUP):
            piece = all_ref[at + group * GROUP]
            sums = sums + piece
            for e in range(1, GROUP):
                other = all_ref[at + group * GROUP + e]
                sums = sums + other
                piece = jnp.where(lane == e, other, piece)
            pieces.append(piece)
        flat = jnp.concatenate(pieces, axis=1)
        index = flat[cases : cases + 1].astype(jnp.int32) ^ flip
        force = jnp.where(row < cases, flat, 0.0)
        total = [
            moved(force, chosen_columns(index - start, step), True)
            for start in range(0, corners, step)
        ]
        return sums, jnp.concatenate(total, axis=1)

    sums_ref[...], total_ref[...] = add(0)
    if devices > chunk:

        @pl.loop(1, devices // chunk)
        def _(i):
            sums, total = add(i * chunk)
            sums_ref[...] += sums
            total_ref[...] += total


def near_index(cases, all_ref):
    lane = lax.broadcasted_iota(jnp.int32, (1, LANES), 1) // SLOT
    left, *others = near_devices()
    index = all_ref[left, cases : cases + 1]
    for e, device in enumerate(others, 1):
        index = jnp.where(lane == e, all_ref[device, cases : cases + 1], index)
    return index.astype(jnp.int32)


def coarse_kernel(cases, all_ref, inv_high, inv_low, x_ref, total_ref, sums_ref, index_ref):
    gathered_forces(cases, all_ref, total_ref.shape[1], 0, sums_ref, total_ref)
    index_ref[...] = jnp.broadcast_to(near_index(cases, all_ref), index_ref.shape)
    x_ref[...] = product(total_ref[...], inv_high[...], inv_low[...])


def shared_coarse(cases, width, refs):
    *pieces, total_ref, sums_ref, index_ref, whole = refs
    for m, piece in enumerate(pieces):
        base = lax.rem(lax.axis_index("crs") + m, len(pieces)) * width
        whole[:, pl.ds(pl.multiple_of(base, width), width)] = piece[...]
    return whole[...], total_ref[...], sums_ref[...], index_ref[:1]


def pair_kernel(
    cases, all_ref, far_ref, inv_high, inv_low, _, schur_hbm, x_ref, total_ref, sums_ref, index_ref, *later,
):
    copies = fetched([(schur_hbm, later[0])], later[1]) if later else []
    width = inv_high.shape[1]
    slab = lax.axis_index("crs")
    flip = slab * width
    gathered_forces(cases, all_ref, 4 * width, flip, sums_ref, total_ref)
    index = near_index(cases, all_ref) ^ flip
    index_ref[...] = jnp.broadcast_to(index, index_ref.shape)
    total = total_ref[...]
    last = [
        far_ref[pl.ds(pl.multiple_of((slab % 2 ^ j) * width, width), width)] for j in range(2)
    ]
    third = product(total[:, 2 * width :], *parts(jnp.concatenate(last, axis=0), 2))
    x_ref[:, :width] = product(total, inv_high[...], inv_low[...])
    x_ref[:, width : 2 * width] = jnp.zeros((ROWS, width), F32)
    across = product(total[:, :width], inv_high[2 * width :], inv_low[2 * width :], True)
    x_ref[:, 2 * width : 3 * width] = across[:, :width] + third
    x_ref[:, 3 * width :] = across[:, width:]
    for copy in copies:
        copy.wait()


def paired_coarse(cases, width, refs):
    x_ref, other_ref, total_ref, sums_ref, index_ref = refs
    other = [other_ref[:, (j ^ 1) * width : (j ^ 1) * width + width] for j in range(4)]
    solution = x_ref[...] + jnp.concatenate(other, axis=1)
    return solution, total_ref[...], sums_ref[...], index_ref[:1]


def column(x, lane):
    return x[:, lane : lane + 1]


def second_kernel(cases, coarse, given, *refs):
    (
        pack_ref, left_ref, right_ref, back_ref, from_left, from_right,
        schur_ref, c_high, c_low, corner_ref, own_ref,
        send_ref, out_ref, keep_ref, spread_ref, scalar_ref,
    ) = refs[given : given + 16]
    solution, total, sums, index = coarse(refs[:given] + refs[given + 16 :])
    picked = moved(solution, chosen_columns(index, solution.shape[1]))
    blank = jnp.zeros((SLOT - (right_ref.shape[0] - ROWS), right_ref.shape[1]), F32)
    none = jnp.zeros((SLOT, right_ref.shape[1]), F32)
    own = jnp.concatenate([none, right_ref[ROWS:], blank, -from_right[ROWS:], blank, none], axis=0)
    other = jnp.concatenate([from_left[ROWS:], blank, -back_ref[ROWS:], blank, none, none], axis=0)
    spread_ref[...] = own
    both = product(picked, *parts(jnp.concatenate([own, other], axis=1), 2))
    records = right_ref.shape[1]
    residual, scale, _ = unpacked(pack_ref[...], cases)
    left_residual, left_scale, left_index = unpacked(left_ref[...], cases)
    live = (scale > 0.0).astype(F32)
    left_live = (left_scale > 0.0).astype(F32)
    image = (right_ref[:ROWS] - from_right[:ROWS] + both[:, :records]) * live
    left_image = (from_left[:ROWS] - back_ref[:ROWS] + both[:, records:]) * left_live
    norm = column(sums, SLOT - 2)
    curvature = column(sums, SLOT - 1) + row_sum(total * solution)
    row = lax.broadcasted_iota(jnp.int32, (ROWS, 1), 0)
    alpha = jnp.where(row < cases, norm / curvature, 0.0)
    residual = residual - alpha * image
    left_residual = left_residual - alpha * left_image
    precon = scale * residual
    left_precon = left_scale * left_residual
    own_map = chosen_columns(own_ref[...], c_high.shape[1])
    left_map = chosen_columns(left_index, c_high.shape[1])
    load = moved(precon, own_map, True) - moved(left_precon, left_map, True)
    through = product(load, *parts(schur_ref[0, 0], 2))
    forces(load, through, row_sum(residual * precon), c_high, c_low, corner_ref, cases, send_ref)
    out_ref[...] = moved(through, left_map)
    keep_ref[:ROWS] = moved(through, own_map)
    keep_ref[ROWS:] = image
    lane = lax.broadcasted_iota(jnp.int32, scalar_ref.shape, 1)
    scalar_ref[...] = jnp.where(lane == 0, norm, alpha)


def last_kernel(cases, coarse, given, *refs):
    (
        pack_ref, from_right, keep_ref, spread_ref, scalar_ref, multipliers_ref, residual_ref,
    ) = refs[given : given + 7]
    solution, total, sums, index = coarse(refs[:given] + refs[given + 7 :])
    picked = moved(solution, chosen_columns(index, solution.shape[1]))
    residual, scale, _ = unpacked(pack_ref[...], cases)
    live = (scale > 0.0).astype(F32)
    spread = product(picked, *parts(spread_ref[...], 2))
    image = (keep_ref[:ROWS] - from_right[...] + spread) * live
    along = keep_ref[ROWS:]
    first_norm = column(scalar_ref[...], 0)
    first_alpha = column(scalar_ref[...], 1)
    norm = column(sums, SLOT - 2)
    curvature = column(sums, SLOT - 1) + row_sum(total * solution)
    ratio = norm / first_norm
    alpha = norm / (curvature - ratio * norm / first_alpha)
    direction = scale * residual
    multipliers = first_alpha * direction
    residual = residual - first_alpha * along
    direction = scale * residual + ratio * direction
    along = image + ratio * along
    multipliers = multipliers + alpha * direction
    residual = residual - alpha * along
    for case in range(cases):
        multipliers_ref[case] = multipliers[case : case + 1]
        residual_ref[case] = residual[case : case + 1]


VM = pl.BlockSpec(memory_space=pltpu.VMEM)
SM = pl.BlockSpec(memory_space=pltpu.SMEM)
HB = pl.BlockSpec(memory_space=pltpu.HBM)


def call(kernel, outs, given, specs, scratch=(), moved_bytes=None):
    specs = specs + [VM] * (len(given) - len(specs))
    given = [
        pltpu.with_memory_space_constraint(x, pltpu.HBM) if spec is HB else x
        for x, spec in zip(given, specs)
    ]
    return pl.pallas_call(
        kernel,
        out_shape=[jax.ShapeDtypeStruct(shape, kind) for shape, kind in outs],
        in_specs=specs,
        out_specs=[VM] * len(outs),
        scratch_shapes=list(scratch),
        cost_estimate=moved_bytes
        and pl.CostEstimate(flops=0, bytes_accessed=moved_bytes, transcendentals=0),
        compiler_params=pltpu.CompilerParams(vmem_limit_bytes=VMEM_LIMIT),
    )(*given)


def passed_along(value, axis, steps):
    count = lax.axis_size(axis)
    pairs = [(source, (source + steps) % count) for source in range(count)]
    return lax.ppermute(value, axis, pairs)


def exchanged(value, axis, bit):
    pairs = [(source, source ^ bit) for source in range(lax.axis_size(axis))]
    return lax.ppermute(value, axis, pairs)


def per_device(
    jump_data,
    lumped_scale,
    schur_inverse,
    coarse_coupling,
    corner_inverse,
    own_dof,
    nbr_dof,
    live_count,
    corner_index,
):
    cases, records = jump_data.shape[2:]
    held, iface = coarse_coupling.shape[2:]
    corners, width = corner_inverse.shape
    chain, slabs = lax.axis_size("sub"), lax.axis_size("crs")
    devices = chain * slabs

    def buffers(*arrays):
        return [pltpu.VMEM(a.shape, a.dtype) for a in arrays] + [
            pltpu.SemaphoreType.DMA((len(arrays),))
        ]

    jump = jump_data.reshape(cases, 1, records)
    first = (jump, lumped_scale, nbr_dof)
    pack, half = call(
        pack_kernel,
        [((ROWS, records), F32), ((2 * width, width), F32)],
        (live_count, *first, corner_inverse),
        [SM] + [HB] * 4,
        [*buffers(*first)[:-1], pltpu.SemaphoreType.DMA((4,))],
    )
    left = passed_along(pack, "sub", 1)
    fetched_here = (schur_inverse, coarse_coupling, own_dof, corner_index, corner_inverse)
    s_high, s_low, c_high, c_low, own_coupling, load, index, own, inv_high, inv_low = call(
        functools.partial(prepare_kernel, cases),
        [
            ((iface, iface), BF16),
            ((iface, iface), BF16),
            ((SLOT, iface), BF16),
            ((SLOT, iface), BF16),
            ((held, records), F32),
            ((ROWS, iface), F32),
            ((1, LANES), F32),
            ((1, records), jnp.int32),
            ((corners, width), BF16),
            ((corners, width), BF16),
        ],
        (pack, *fetched_here),
        [VM] + [HB] * 5,
        buffers(*fetched_here),
        32 << 20,
    )
    if is_paired(width):
        far = exchanged(half, "crs", 2)
    send, right, back = call(
        functools.partial(first_kernel, cases),
        [
            ((devices, ROWS, LANES), F32),
            ((ROWS + held, records), F32),
            ((ROWS + held, records), F32),
        ],
        (left, pack, load, own_coupling, index, s_high, s_low, c_high, c_low, own),
        [],
    )

    def gathered(send, beside, *later):
        everyone = lax.all_to_all(send, ("sub", "crs"), 0, 0)
        row = (ROWS, corners)
        outs = [(row, F32), ((ROWS, LANES), F32), ((ROWS, LANES), jnp.int32)]
        if is_paired(width):
            x, total, sums, near, *fetched = call(
                functools.partial(pair_kernel, cases),
                [(row, F32), *outs, *((v.shape, v.dtype) for v in later)],
                (everyone, far, inv_high, inv_low, beside, schur_inverse),
                [VM] * 5 + [HB],
                [pltpu.SemaphoreType.DMA((1,)) for _ in later],
            )
            return (
                (x, exchanged(x, "crs", 1), total, sums, near),
                [VM] * 5,
                [],
                functools.partial(paired_coarse, cases, width),
                *fetched,
            )
        x, *others = call(
            functools.partial(coarse_kernel, cases),
            [((ROWS, width), F32), *outs],
            (everyone, inv_high, inv_low),
            [],
        )
        pieces = [x] + [passed_along(x, "crs", -m) for m in range(1, slabs)]
        return (
            (*pieces, *others),
            [VM] * (len(pieces) + len(others)),
            [pltpu.VMEM(row, F32)],
            functools.partial(shared_coarse, cases, width),
            *later,
        )

    from_left = passed_along(right, "sub", 1)
    from_right = passed_along(back, "sub", -1)
    given, specs, scratch, coarse, schur = gathered(send, from_right, schur_inverse)
    send, out, keep, spread, scalars = call(
        functools.partial(second_kernel, cases, coarse, len(given)),
        [
            ((devices, ROWS, LANES), F32),
            ((ROWS, records), F32),
            ((2 * ROWS, records), F32),
            ((LANES, records), F32),
            ((ROWS, LANES), F32),
        ],
        (
            *given, pack, left, right, back, from_left, from_right,
            schur, c_high, c_low, index, own,
        ),
        specs,
        scratch,
    )
    from_right = passed_along(out, "sub", -1)
    given, specs, scratch, coarse = gathered(send, from_right)
    outs = call(
        functools.partial(last_kernel, cases, coarse, len(given)),
        [(jump.shape, F32), (jump.shape, F32)],
        (*given, pack, from_right, keep, spread, scalars),
        specs,
        scratch,
    )
    return tuple(out.reshape(jump_data.shape) for out in outs)


def solution(mesh):
    return jax.shard_map(
        per_device,
        mesh=mesh,
        in_specs=(
            P("sub", "crs", None, None),
            P("sub", "crs", None),
            P("sub", "crs", None, None),
            P("sub", "crs", None, None),
            P(None, "crs"),
            P("sub", "crs", None),
            P("sub", "crs", None),
            P("sub", "crs"),
            P("sub", "crs", None),
        ),
        out_specs=(P("sub", "crs", None, None), P("sub", "crs", None, None)),
        check_vma=False,
    )
```

```python
import functools

import jax
import jax.numpy as jnp
from jax import lax
from jax.experimental import pallas as pl
from jax.experimental.pallas import tpu as pltpu
from jax.sharding import PartitionSpec as P

F32 = jnp.float32
BF16 = jnp.bfloat16
ROWS = 8
LANES = 128
SLOT = 32
GROUP = LANES // SLOT
FOLD = ROWS // GROUP
VMEM_LIMIT = 24 << 20


def parts(x, count):
    out = []
    for _ in range(count):
        out.append(x.astype(BF16))
        x = x - out[-1].astype(F32)
    return out


def dot(a, b, transposed=False):
    dims = (((1,), (1 if transposed else 0,)), ((), ()))
    return lax.dot_general(a, b, dims, preferred_element_type=F32)


def moved(a, chosen, transposed=False):
    rows = a.shape[0]
    all_parts = dot(jnp.concatenate(parts(a, 3), axis=0), chosen, transposed)
    return all_parts[:rows] + all_parts[rows : 2 * rows] + all_parts[2 * rows :]


def moved_parts(high, low, chosen):
    both = dot(jnp.concatenate([high, low], axis=0), chosen)
    return both[: high.shape[0]] + both[high.shape[0] :]


def product(a, high, low, transposed=False):
    rows = a.shape[0]
    top, rest = parts(a, 2)
    both = dot(jnp.concatenate([top, rest], axis=0), high, transposed)
    return both[:rows] + both[rows:] + dot(top, low, transposed)


def chosen_columns(index, count):
    shape = (count, index.shape[1])
    rows = lax.broadcasted_iota(jnp.int32, shape, 0)
    return jnp.where(rows == index, 1.0, 0.0).astype(BF16)


def row_sum(x):
    return jnp.sum(x, axis=1, keepdims=True)


def padded(x, rows):
    return jnp.concatenate([x, jnp.zeros((rows - x.shape[0], x.shape[1]), x.dtype)], axis=0)


def fetched(pairs, sems):
    copies = [
        pltpu.make_async_copy(source, target, sems.at[i]) for i, (source, target) in enumerate(pairs)
    ]
    for copy in copies:
        copy.start()
    return copies


def pack_kernel(
    live_ref, jump_hbm, scale_hbm, nbr_hbm, inverse_hbm, out_ref, half_ref, jump, scale, nbr, sems,
):
    cases, _, records = jump.shape
    copies = fetched(
        [
            (jump_hbm, jump),
            (scale_hbm, scale),
            (nbr_hbm, nbr),
            (half_of(lax.axis_index("crs"), inverse_hbm), half_ref),
        ],
        sems,
    )
    for copy in copies:
        copy.wait()
    live = lax.broadcasted_iota(jnp.int32, (1, records), 1) < live_ref[0, 0]
    live = live.astype(F32)
    for case in range(cases):
        out_ref[case : case + 1] = jump[case] * live
    out_ref[cases : cases + 1] = scale[0] * live
    out_ref[cases + 1 : cases + 2] = nbr[0].astype(F32)


def unpacked(pack, cases):
    rows = lax.broadcasted_iota(jnp.int32, pack.shape, 0)
    residual = jnp.where(rows < cases, pack, 0.0)
    return residual, pack[cases : cases + 1], pack[cases + 1 : cases + 2].astype(jnp.int32)


def near_devices():
    chain, slabs = lax.axis_size("sub"), lax.axis_size("crs")
    here, slab = lax.axis_index("sub"), lax.axis_index("crs")
    return [lax.rem(here + step, chain) * slabs + slab for step in (chain - 1, 0, 1)]


def is_paired(width):
    return lax.axis_size("crs") == 4 and width & (width - 1) == 0


def block_at(slab, j, width):
    return slab ^ j if is_paired(width) else j


def by_turns(count):
    return count % 2 == 0


def dealt(right, left):
    if not by_turns(lax.axis_size("sub")):
        return right, left
    even = lax.rem(lax.axis_index("sub"), 2) == 0
    return jnp.where(even, right, left), jnp.where(even, left, right)


def half_of(slab, inverse_hbm):
    rows = 2 * inverse_hbm.shape[1]
    first = jnp.minimum(slab // 2 * rows, inverse_hbm.shape[0] - rows)
    return inverse_hbm.at[pl.ds(pl.multiple_of(first, 8), rows)]


def prepare_kernel(
    cases, pack_ref, schur_hbm, coupling_hbm, own_hbm, corner_hbm, inverse_hbm,
    s_high, s_low, c_high, c_low, own_coupling, load_ref, index_ref, own_ref, inv_high, inv_low,
    schur, coupling, own, corner, inverse, sems,
):
    copies = fetched(
        [
            (own_hbm, own),
            (coupling_hbm, coupling),
            (corner_hbm, corner),
            (inverse_hbm, inverse),
            (schur_hbm, schur),
        ],
        sems,
    )
    for copy in copies[:3]:
        copy.wait()
    held, iface = coupling.shape[2:]
    block = padded(coupling[0, 0], SLOT)
    c_high[...], c_low[...] = parts(block, 2)
    chosen = chosen_columns(own[0], iface)
    own_ref[...] = own[0]
    own_coupling[...] = moved_parts(c_high[...], c_low[...], chosen)[:held]
    residual, scale, _ = unpacked(pack_ref[...], cases)
    load_ref[...] = moved(residual * scale, chosen, True)
    lane = lax.broadcasted_iota(jnp.int32, (held, LANES), 1) % SLOT
    tiles = jnp.where(lane == lax.broadcasted_iota(jnp.int32, (held, LANES), 0), 1.0, 0.0)
    index = jnp.broadcast_to(corner[0].astype(F32), (ROWS, held))
    index_ref[...] = jnp.where(lane[:1] < held, moved(index, tiles.astype(BF16))[:1], -1.0)
    copies[3].wait()
    slab = lax.axis_index("crs")
    blocks = lax.axis_size("crs")
    width = inverse.shape[1]
    for j in range(blocks):
        rows = pl.ds(pl.multiple_of(block_at(slab, j, width) * width, width), width)
        high, low = parts(inverse[rows], 2)
        inv_high[j * width : (j + 1) * width] = high
        inv_low[j * width : (j + 1) * width] = low
    copies[4].wait()
    s_high[...], s_low[...] = parts(schur[0, 0], 2)


def forces(load, through, first, c_high, c_low, index_ref, cases, send_hbm, send, sems):
    high, low = [jnp.concatenate([c[...]] * GROUP, axis=0) for c in (c_high, c_low)]
    force = product(load, high, low, True)
    lane = lax.broadcasted_iota(jnp.int32, force.shape, 1) % SLOT
    row = lax.broadcasted_iota(jnp.int32, force.shape, 0)
    force = jnp.where(lane == SLOT - 2, first, force)
    force = jnp.where(lane == SLOT - 1, row_sum(load * through), force)
    force = jnp.where(row == cases, index_ref[...], force)
    block = lax.broadcasted_iota(jnp.int32, force.shape, 1) // SLOT
    force = jnp.where(row // FOLD == block, force, 0.0)
    folded = sum(force[b * FOLD : (b + 1) * FOLD] for b in range(GROUP))
    send[...] = jnp.broadcast_to(folded[None], send.shape)
    (copy,) = fetched([(send, send_hbm)], sems)
    return copy


def unfolded(four):
    block = lax.broadcasted_iota(jnp.int32, four.shape, 1) // SLOT
    place = lax.broadcasted_iota(jnp.int32, four.shape, 0) // FOLD
    out = four
    for k in range(1, GROUP):
        turned = pltpu.roll(pltpu.roll(four, SLOT * k, 1), ROWS - FOLD * k, 0)
        out = jnp.where((block - place) % GROUP == k, turned, out)
    return out


def first_kernel(
    cases, left_ref, pack_ref, load_ref, own_coupling, index_ref,
    s_high, s_low, c_high, c_low, own_ref,
    send_hbm, right_ref, back_ref, one_ref, two_ref, send, sems,
):
    left_residual, left_scale, left_index = unpacked(left_ref[...], cases)
    chosen = chosen_columns(left_index, load_ref.shape[1])
    load = load_ref[...] - moved(left_residual * left_scale, chosen, True)
    through = product(load, s_high[...], s_low[...])
    residual, scale, _ = unpacked(pack_ref[...], cases)
    norm = row_sum(residual * residual * scale)
    copy = forces(load, through, norm, c_high, c_low, index_ref, cases, send_hbm, send, sems)
    right_ref[:ROWS] = moved(through, chosen_columns(own_ref[...], load_ref.shape[1]))
    right_ref[ROWS:] = own_coupling[...]
    back_ref[:ROWS] = moved(through, chosen)
    held = own_coupling.shape[0]
    back_ref[ROWS:] = moved_parts(c_high[...], c_low[...], chosen)[:held]
    one_ref[...], two_ref[...] = dealt(right_ref[...], back_ref[...])
    copy.wait()


def gathered_forces(cases, all_ref, corners, flip, sums_ref, total_ref):
    devices = all_ref.shape[0]
    chunk = min(devices, LANES // GROUP)
    row = lax.broadcasted_iota(jnp.int32, (ROWS, 1), 0)
    step = min(corners, 1024)

    def add(at):
        pieces = [
            unfolded(jnp.concatenate([all_ref[at + group + e] for e in range(GROUP)], axis=0))
            for group in range(0, chunk, GROUP)
        ]
        sums = sum(pieces)
        for turn in (SLOT, 2 * SLOT):
            sums = sums + pltpu.roll(sums, turn, 1)
        flat = jnp.concatenate(pieces, axis=1)
        index = flat[cases : cases + 1].astype(jnp.int32) ^ flip
        force = jnp.where(row < cases, flat, 0.0)
        total = [
            moved(force, chosen_columns(index - start, step), True)
            for start in range(0, corners, step)
        ]
        return sums, jnp.concatenate(total, axis=1)

    sums_ref[...], total_ref[...] = add(0)
    if devices > chunk:

        @pl.loop(1, devices // chunk)
        def _(i):
            sums, total = add(i * chunk)
            sums_ref[...] += sums
            total_ref[...] += total


def near_index(cases, all_ref):
    lane = lax.broadcasted_iota(jnp.int32, (1, LANES), 1) // SLOT
    index = jnp.zeros((1, LANES), F32)
    for e, device in enumerate(near_devices()):
        rows = jnp.concatenate([all_ref[device]] * GROUP, axis=0)
        rows = pltpu.roll(rows, SLOT * (e - cases // FOLD) % LANES, 1)
        index = jnp.where(lane == e, rows[cases % FOLD : cases % FOLD + 1], index)
    return index.astype(jnp.int32)


def coarse_kernel(cases, all_ref, inv_high, inv_low, x_ref, total_ref, sums_ref, index_ref):
    gathered_forces(cases, all_ref, total_ref.shape[1], 0, sums_ref, total_ref)
    index_ref[...] = jnp.broadcast_to(near_index(cases, all_ref), index_ref.shape)
    x_ref[...] = product(total_ref[...], inv_high[...], inv_low[...])


def shared_coarse(cases, width, refs):
    *pieces, total_ref, sums_ref, index_ref, whole = refs
    for m, piece in enumerate(pieces):
        base = lax.rem(lax.axis_index("crs") + m, len(pieces)) * width
        whole[:, pl.ds(pl.multiple_of(base, width), width)] = piece[...]
    return whole[...], total_ref[...], sums_ref[...], index_ref[:1]


def pair_kernel(
    cases, all_ref, far_ref, inv_high, inv_low, schur_hbm, x_ref, total_ref, sums_ref, index_ref, *later,
):
    copies = fetched([(schur_hbm, later[0])], later[1]) if later else []
    width = inv_high.shape[1]
    slab = lax.axis_index("crs")
    flip = slab * width

    @pl.when(slab >= 0)
    def _():
        gathered_forces(cases, all_ref, 4 * width, flip, sums_ref, total_ref)
        index = near_index(cases, all_ref) ^ flip
        index_ref[...] = jnp.broadcast_to(index, index_ref.shape)
        total = total_ref[...]
        last = [
            far_ref[pl.ds(pl.multiple_of((slab % 2 ^ j) * width, width), width)] for j in range(2)
        ]
        third = product(total[:, 2 * width :], *parts(jnp.concatenate(last, axis=0), 2))
        x_ref[:, :width] = product(total, inv_high[...], inv_low[...])
        x_ref[:, width : 2 * width] = jnp.zeros((ROWS, width), F32)
        across = product(total[:, :width], inv_high[2 * width :], inv_low[2 * width :], True)
        x_ref[:, 2 * width : 3 * width] = across[:, :width] + third
        x_ref[:, 3 * width :] = across[:, width:]

    for copy in copies:
        copy.wait()


def paired_coarse(cases, width, refs):
    x_ref, other_ref, total_ref, sums_ref, index_ref = refs
    other = [other_ref[:, (j ^ 1) * width : (j ^ 1) * width + width] for j in range(4)]
    solution = x_ref[...] + jnp.concatenate(other, axis=1)
    return solution, total_ref[...], sums_ref[...], index_ref[:1]


def column(x, lane):
    return x[:, lane : lane + 1]


def second_kernel(cases, coarse, given, *refs):
    (
        pack_ref, left_ref, right_ref, back_ref, one_ref, two_ref,
        schur_ref, c_high, c_low, corner_ref, own_ref,
        send_hbm, out_ref, keep_ref, spread_ref, scalar_ref, send, sems,
    ) = refs[given : given + 18]
    solution, total, sums, index = coarse(refs[:given] + refs[given + 18 :])
    picked = moved(solution, chosen_columns(index, solution.shape[1]))
    from_right, from_left = dealt(one_ref[...], two_ref[...])
    blank = jnp.zeros((SLOT - (right_ref.shape[0] - ROWS), right_ref.shape[1]), F32)
    none = jnp.zeros((SLOT, right_ref.shape[1]), F32)
    own = jnp.concatenate([none, right_ref[ROWS:], blank, -from_right[ROWS:], blank, none], axis=0)
    other = jnp.concatenate([from_left[ROWS:], blank, -back_ref[ROWS:], blank, none, none], axis=0)
    spread_ref[...] = own
    both = product(picked, *parts(jnp.concatenate([own, other], axis=1), 2))
    records = right_ref.shape[1]
    residual, scale, _ = unpacked(pack_ref[...], cases)
    left_residual, left_scale, left_index = unpacked(left_ref[...], cases)
    live = (scale > 0.0).astype(F32)
    left_live = (left_scale > 0.0).astype(F32)
    image = (right_ref[:ROWS] - from_right[:ROWS] + both[:, :records]) * live
    left_image = (from_left[:ROWS] - back_ref[:ROWS] + both[:, records:]) * left_live
    norm = column(sums, SLOT - 2)
    curvature = column(sums, SLOT - 1) + row_sum(total * solution)
    row = lax.broadcasted_iota(jnp.int32, (ROWS, 1), 0)
    alpha = jnp.where(row < cases, norm / curvature, 0.0)
    residual = residual - alpha * image
    left_residual = left_residual - alpha * left_image
    precon = scale * residual
    left_precon = left_scale * left_residual
    own_map = chosen_columns(own_ref[...], c_high.shape[1])
    left_map = chosen_columns(left_index, c_high.shape[1])
    load = moved(precon, own_map, True) - moved(left_precon, left_map, True)
    through = product(load, *parts(schur_ref[0, 0], 2))
    norm_here = row_sum(residual * precon)
    copy = forces(load, through, norm_here, c_high, c_low, corner_ref, cases, send_hbm, send, sems)
    out_ref[...] = moved(through, left_map)
    keep_ref[:ROWS] = moved(through, own_map)
    keep_ref[ROWS:] = image
    lane = lax.broadcasted_iota(jnp.int32, scalar_ref.shape, 1)
    scalar_ref[...] = jnp.where(lane == 0, norm, alpha)
    copy.wait()


def last_kernel(cases, coarse, given, *refs):
    (
        pack_ref, from_right, keep_ref, spread_ref, scalar_ref, multipliers_ref, residual_ref,
    ) = refs[given : given + 7]
    solution, total, sums, index = coarse(refs[:given] + refs[given + 7 :])
    picked = moved(solution, chosen_columns(index, solution.shape[1]))
    residual, scale, _ = unpacked(pack_ref[...], cases)
    live = (scale > 0.0).astype(F32)
    spread = product(picked, *parts(spread_ref[...], 2))
    image = (keep_ref[:ROWS] - from_right[...] + spread) * live
    along = keep_ref[ROWS:]
    first_norm = column(scalar_ref[...], 0)
    first_alpha = column(scalar_ref[...], 1)
    norm = column(sums, SLOT - 2)
    curvature = column(sums, SLOT - 1) + row_sum(total * solution)
    ratio = norm / first_norm
    alpha = norm / (curvature - ratio * norm / first_alpha)
    direction = scale * residual
    multipliers = first_alpha * direction
    residual = residual - first_alpha * along
    direction = scale * residual + ratio * direction
    along = image + ratio * along
    multipliers = multipliers + alpha * direction
    residual = residual - alpha * along
    for case in range(cases):
        multipliers_ref[case] = multipliers[case : case + 1]
        residual_ref[case] = residual[case : case + 1]


VM = pl.BlockSpec(memory_space=pltpu.VMEM)
SM = pl.BlockSpec(memory_space=pltpu.SMEM)
HB = pl.BlockSpec(memory_space=pltpu.HBM)


def call(kernel, outs, given, specs, scratch=(), moved_bytes=None, stored=0):
    specs = specs + [VM] * (len(given) - len(specs))
    given = [
        pltpu.with_memory_space_constraint(x, pltpu.HBM) if spec is HB else x
        for x, spec in zip(given, specs)
    ]
    return pl.pallas_call(
        kernel,
        out_shape=[jax.ShapeDtypeStruct(shape, kind) for shape, kind in outs],
        in_specs=specs,
        out_specs=[HB] * stored + [VM] * (len(outs) - stored),
        scratch_shapes=list(scratch),
        cost_estimate=moved_bytes
        and pl.CostEstimate(flops=0, bytes_accessed=moved_bytes, transcendentals=0),
        compiler_params=pltpu.CompilerParams(vmem_limit_bytes=VMEM_LIMIT),
    )(*given)


def passed_along(value, axis, steps):
    count = lax.axis_size(axis)
    pairs = [(source, (source + steps) % count) for source in range(count)]
    return lax.ppermute(value, axis, pairs)


def exchanged(value, axis, bit):
    pairs = [(source, source ^ bit) for source in range(lax.axis_size(axis))]
    return lax.ppermute(value, axis, pairs)


def per_device(
    jump_data,
    lumped_scale,
    schur_inverse,
    coarse_coupling,
    corner_inverse,
    own_dof,
    nbr_dof,
    live_count,
    corner_index,
):
    cases, records = jump_data.shape[2:]
    held, iface = coarse_coupling.shape[2:]
    corners, width = corner_inverse.shape
    chain, slabs = lax.axis_size("sub"), lax.axis_size("crs")
    devices = chain * slabs

    def buffers(*arrays):
        return [pltpu.VMEM(a.shape, a.dtype) for a in arrays] + [
            pltpu.SemaphoreType.DMA((len(arrays),))
        ]

    jump = jump_data.reshape(cases, 1, records)
    first = (jump, lumped_scale, nbr_dof)
    pack, half = call(
        pack_kernel,
        [((ROWS, records), F32), ((2 * width, width), F32)],
        (live_count, *first, corner_inverse),
        [SM] + [HB] * 4,
        [*buffers(*first)[:-1], pltpu.SemaphoreType.DMA((4,))],
    )
    if is_paired(width):
        far = exchanged(half, "crs", 2)
    left = passed_along(pack, "sub", 1)
    fetched_here = (schur_inverse, coarse_coupling, own_dof, corner_index, corner_inverse)
    s_high, s_low, c_high, c_low, own_coupling, load, index, own, inv_high, inv_low = call(
        functools.partial(prepare_kernel, cases),
        [
            ((iface, iface), BF16),
            ((iface, iface), BF16),
            ((SLOT, iface), BF16),
            ((SLOT, iface), BF16),
            ((held, records), F32),
            ((ROWS, iface), F32),
            ((1, LANES), F32),
            ((1, records), jnp.int32),
            ((corners, width), BF16),
            ((corners, width), BF16),
        ],
        (pack, *fetched_here),
        [VM] + [HB] * 5,
        buffers(*fetched_here),
        32 << 20,
    )
    outgoing = [pltpu.VMEM((devices, FOLD, LANES), F32), pltpu.SemaphoreType.DMA((1,))]
    send, right, back, one, two = call(
        functools.partial(first_kernel, cases),
        [((devices, FOLD, LANES), F32)] + [((ROWS + held, records), F32)] * 4,
        (left, pack, load, own_coupling, index, s_high, s_low, c_high, c_low, own),
        [],
        outgoing,
        stored=1,
    )

    def gathered(send, beside, *later):
        everyone = lax.all_to_all(send, ("sub", "crs"), 0, 0)
        row = (ROWS, corners)
        outs = [(row, F32), ((ROWS, LANES), F32), ((ROWS, LANES), jnp.int32)]
        if is_paired(width):
            x, total, sums, near, *fetched = call(
                functools.partial(pair_kernel, cases),
                [(row, F32), *outs, *((v.shape, v.dtype) for v in later)],
                (everyone, far, inv_high, inv_low, schur_inverse),
                [VM] * 4 + [HB],
                [pltpu.SemaphoreType.DMA((1,)) for _ in later],
            )
            x, _ = lax.optimization_barrier((x, beside))
            return (
                (x, exchanged(x, "crs", 1), total, sums, near),
                [VM] * 5,
                [],
                functools.partial(paired_coarse, cases, width),
                *fetched,
            )
        x, *others = call(
            functools.partial(coarse_kernel, cases),
            [((ROWS, width), F32), *outs],
            (everyone, inv_high, inv_low),
            [],
        )
        pieces = [x] + [passed_along(x, "crs", -m) for m in range(1, slabs)]
        return (
            (*pieces, *others),
            [VM] * (len(pieces) + len(others)),
            [pltpu.VMEM(row, F32)],
            functools.partial(shared_coarse, cases, width),
            *later,
        )

    if by_turns(chain):
        rounds = [[(c, (c + 1) % chain) for c in range(start, chain, 2)] for start in (0, 1)]
        rounds = [pairs + [(b, a) for a, b in pairs] for pairs in rounds]
        two = lax.ppermute(two, "sub", rounds[1])
        one = lax.ppermute(one, "sub", rounds[0])
    else:
        one, two = passed_along(two, "sub", -1), passed_along(one, "sub", 1)
    given, specs, scratch, coarse, schur = gathered(send, two, schur_inverse)
    send, out, keep, spread, scalars = call(
        functools.partial(second_kernel, cases, coarse, len(given)),
        [
            ((devices, FOLD, LANES), F32),
            ((ROWS, records), F32),
            ((2 * ROWS, records), F32),
            ((LANES, records), F32),
            ((ROWS, LANES), F32),
        ],
        (
            *given, pack, left, right, back, one, two,
            schur, c_high, c_low, index, own,
        ),
        specs,
        outgoing + scratch,
        stored=1,
    )
    from_right = passed_along(out, "sub", -1)
    given, specs, scratch, coarse = gathered(send, from_right)
    outs = call(
        functools.partial(last_kernel, cases, coarse, len(given)),
        [(jump.shape, F32), (jump.shape, F32)],
        (*given, pack, from_right, keep, spread, scalars),
        specs,
        scratch,
    )
    return tuple(out.reshape(jump_data.shape) for out in outs)


def solution(mesh):
    return jax.shard_map(
        per_device,
        mesh=mesh,
        in_specs=(
            P("sub", "crs", None, None),
            P("sub", "crs", None),
            P("sub", "crs", None, None),
            P("sub", "crs", None, None),
            P(None, "crs"),
            P("sub", "crs", None),
            P("sub", "crs", None),
            P("sub", "crs"),
            P("sub", "crs", None),
        ),
        out_specs=(P("sub", "crs", None, None), P("sub", "crs", None, None)),
        check_vma=False,
    )
```

```python
import functools

import jax
import jax.numpy as jnp
from jax import lax
from jax.experimental import pallas as pl
from jax.experimental.pallas import tpu as pltpu
from jax.sharding import PartitionSpec as P

F32 = jnp.float32
BF16 = jnp.bfloat16
ROWS = 8
LANES = 128
SLOT = 32
GROUP = LANES // SLOT
FOLD = ROWS // GROUP
VMEM_LIMIT = 24 << 20


def parts(x, count):
    out = []
    for _ in range(count):
        out.append(x.astype(BF16))
        x = x - out[-1].astype(F32)
    return out


def dot(a, b, transposed=False):
    dims = (((1,), (1 if transposed else 0,)), ((), ()))
    return lax.dot_general(a, b, dims, preferred_element_type=F32)


def moved(a, chosen, transposed=False):
    rows = a.shape[0]
    all_parts = dot(jnp.concatenate(parts(a, 3), axis=0), chosen, transposed)
    return all_parts[:rows] + all_parts[rows : 2 * rows] + all_parts[2 * rows :]


def moved_parts(high, low, chosen):
    both = dot(jnp.concatenate([high, low], axis=0), chosen)
    return both[: high.shape[0]] + both[high.shape[0] :]


def product(a, high, low, transposed=False):
    rows = a.shape[0]
    top, rest = parts(a, 2)
    both = dot(jnp.concatenate([top, rest], axis=0), high, transposed)
    return both[:rows] + both[rows:] + dot(top, low, transposed)


def chosen_columns(index, count):
    shape = (count, index.shape[1])
    rows = lax.broadcasted_iota(jnp.int32, shape, 0)
    return jnp.where(rows == index, 1.0, 0.0).astype(BF16)


def row_sum(x):
    return jnp.sum(x, axis=1, keepdims=True)


def padded(x, rows):
    return jnp.concatenate([x, jnp.zeros((rows - x.shape[0], x.shape[1]), x.dtype)], axis=0)


def fetched(pairs, sems):
    copies = [
        pltpu.make_async_copy(source, target, sems.at[i]) for i, (source, target) in enumerate(pairs)
    ]
    for copy in copies:
        copy.start()
    return copies


def always(body):
    pl.when(lax.axis_index("crs") >= 0)(body)


def pack_kernel(
    live_ref, jump_hbm, scale_hbm, nbr_hbm, inverse_hbm, out_ref, half_ref, jump, scale, nbr, sems,
):
    cases, _, records = jump.shape
    copies = fetched(
        [
            (jump_hbm, jump),
            (scale_hbm, scale),
            (nbr_hbm, nbr),
            (half_of(lax.axis_index("crs"), inverse_hbm), half_ref),
        ],
        sems,
    )
    for copy in copies:
        copy.wait()
    live = lax.broadcasted_iota(jnp.int32, (1, records), 1) < live_ref[0, 0]
    live = live.astype(F32)
    for case in range(cases):
        out_ref[case : case + 1] = jump[case] * live
    out_ref[cases : cases + 1] = scale[0] * live
    out_ref[cases + 1 : cases + 2] = nbr[0].astype(F32)


def unpacked(pack, cases):
    rows = lax.broadcasted_iota(jnp.int32, pack.shape, 0)
    residual = jnp.where(rows < cases, pack, 0.0)
    return residual, pack[cases : cases + 1], pack[cases + 1 : cases + 2].astype(jnp.int32)


def near_devices():
    chain, slabs = lax.axis_size("sub"), lax.axis_size("crs")
    here, slab = lax.axis_index("sub"), lax.axis_index("crs")
    return [lax.rem(here + step, chain) * slabs + slab for step in (chain - 1, 0, 1)]


def is_paired(width):
    return lax.axis_size("crs") == 4 and width & (width - 1) == 0


def block_at(slab, j, width):
    return slab ^ j if is_paired(width) else j


def by_turns(count):
    return count % 2 == 0


def dealt(right, left):
    if not by_turns(lax.axis_size("sub")):
        return right, left
    even = lax.rem(lax.axis_index("sub"), 2) == 0
    return jnp.where(even, right, left), jnp.where(even, left, right)


def half_of(slab, inverse_hbm):
    rows = 2 * inverse_hbm.shape[1]
    first = jnp.minimum(slab // 2 * rows, inverse_hbm.shape[0] - rows)
    return inverse_hbm.at[pl.ds(pl.multiple_of(first, 8), rows)]


def prepare_kernel(
    cases, pack_ref, schur_hbm, coupling_hbm, own_hbm, corner_hbm,
    s_high, s_low, c_high, c_low, own_coupling, load_ref, index_ref, own_ref,
    schur, coupling, own, corner, sems,
):
    copies = fetched(
        [
            (own_hbm, own),
            (coupling_hbm, coupling),
            (corner_hbm, corner),
            (schur_hbm, schur),
        ],
        sems,
    )
    for copy in copies[:3]:
        copy.wait()
    held, iface = coupling.shape[2:]
    block = padded(coupling[0, 0], SLOT)
    c_high[...], c_low[...] = parts(block, 2)
    chosen = chosen_columns(own[0], iface)
    own_ref[...] = own[0]
    own_coupling[...] = moved_parts(c_high[...], c_low[...], chosen)[:held]
    residual, scale, _ = unpacked(pack_ref[...], cases)
    load_ref[...] = moved(residual * scale, chosen, True)
    lane = lax.broadcasted_iota(jnp.int32, (held, LANES), 1) % SLOT
    tiles = jnp.where(lane == lax.broadcasted_iota(jnp.int32, (held, LANES), 0), 1.0, 0.0)
    index = jnp.broadcast_to(corner[0].astype(F32), (ROWS, held))
    index_ref[...] = jnp.where(lane[:1] < held, moved(index, tiles.astype(BF16))[:1], -1.0)
    copies[3].wait()
    s_high[...], s_low[...] = parts(schur[0, 0], 2)


def inverse_kernel(inverse_hbm, inv_high, inv_low, inverse, sems):
    blocks, width = lax.axis_size("crs"), inverse.shape[1]
    pairs = []
    for j in range(blocks):
        rows = pl.ds(pl.multiple_of(block_at(lax.axis_index("crs"), j, width) * width, width), width)
        pairs.append((inverse_hbm.at[rows], inverse.at[pl.ds(j * width, width)]))
    for copy in fetched(pairs, sems):
        copy.wait()
    inv_high[...], inv_low[...] = parts(inverse[...], 2)


def terms_kernel(top_ref, left_index, own_ref, schur_hbm, s_high, s_low, own_map, left_map, rest, sems):
    rows, iface = top_ref.shape
    (copy,) = fetched([(schur_hbm.at[0, 0, pl.ds(rows, iface - rows)], rest)], sems)

    @always
    def _():
        s_high[:rows], s_low[:rows] = parts(top_ref[...], 2)
        own_map[...] = chosen_columns(own_ref[...], iface)
        left_map[...] = chosen_columns(left_index[...], iface)

    copy.wait()
    s_high[rows:], s_low[rows:] = parts(rest[...], 2)


def forces(load, through, first, c_high, c_low, index_ref, cases, send_hbm, send, sems):
    high, low = [jnp.concatenate([c[...]] * GROUP, axis=0) for c in (c_high, c_low)]
    force = product(load, high, low, True)
    lane = lax.broadcasted_iota(jnp.int32, force.shape, 1) % SLOT
    row = lax.broadcasted_iota(jnp.int32, force.shape, 0)
    force = jnp.where(lane == SLOT - 2, first, force)
    force = jnp.where(lane == SLOT - 1, row_sum(load * through), force)
    force = jnp.where(row == cases, index_ref[...], force)
    block = lax.broadcasted_iota(jnp.int32, force.shape, 1) // SLOT
    force = jnp.where(row // FOLD == block, force, 0.0)
    folded = sum(force[b * FOLD : (b + 1) * FOLD] for b in range(GROUP))
    send[...] = jnp.broadcast_to(folded[None], send.shape)
    (copy,) = fetched([(send, send_hbm)], sems)
    return copy


def unfolded(four):
    block = lax.broadcasted_iota(jnp.int32, four.shape, 1) // SLOT
    place = lax.broadcasted_iota(jnp.int32, four.shape, 0) // FOLD
    out = four
    for k in range(1, GROUP):
        turned = pltpu.roll(pltpu.roll(four, SLOT * k, 1), ROWS - FOLD * k, 0)
        out = jnp.where((block - place) % GROUP == k, turned, out)
    return out


def first_kernel(
    cases, left_ref, pack_ref, load_ref, own_coupling, index_ref,
    s_high, s_low, c_high, c_low, own_ref,
    send_hbm, right_ref, back_ref, one_ref, two_ref, index_out, send, sems,
):
    left_residual, left_scale, left_index = unpacked(left_ref[...], cases)
    index_out[...] = left_index
    chosen = chosen_columns(left_index, load_ref.shape[1])
    load = load_ref[...] - moved(left_residual * left_scale, chosen, True)
    through = product(load, s_high[...], s_low[...])
    residual, scale, _ = unpacked(pack_ref[...], cases)
    norm = row_sum(residual * residual * scale)
    copy = forces(load, through, norm, c_high, c_low, index_ref, cases, send_hbm, send, sems)

    @always
    def _():
        right_ref[:ROWS] = moved(through, chosen_columns(own_ref[...], load_ref.shape[1]))
        right_ref[ROWS:] = own_coupling[...]
        back_ref[:ROWS] = moved(through, chosen)
        held = own_coupling.shape[0]
        back_ref[ROWS:] = moved_parts(c_high[...], c_low[...], chosen)[:held]
        one_ref[...], two_ref[...] = dealt(right_ref[...], back_ref[...])

    copy.wait()


def gathered_forces(cases, all_ref, corners, flip, sums_ref, total_ref):
    devices = all_ref.shape[0]
    chunk = min(devices, LANES // GROUP)
    row = lax.broadcasted_iota(jnp.int32, (ROWS, 1), 0)
    step = min(corners, 1024)

    def add(at):
        pieces = [
            unfolded(jnp.concatenate([all_ref[at + group + e] for e in range(GROUP)], axis=0))
            for group in range(0, chunk, GROUP)
        ]
        sums = sum(pieces)
        for turn in (SLOT, 2 * SLOT):
            sums = sums + pltpu.roll(sums, turn, 1)
        flat = jnp.concatenate(pieces, axis=1)
        index = flat[cases : cases + 1].astype(jnp.int32) ^ flip
        force = jnp.where(row < cases, flat, 0.0)
        total = [
            moved(force, chosen_columns(index - start, step), True)
            for start in range(0, corners, step)
        ]
        return sums, jnp.concatenate(total, axis=1)

    sums_ref[...], total_ref[...] = add(0)
    if devices > chunk:

        @pl.loop(1, devices // chunk)
        def _(i):
            sums, total = add(i * chunk)
            sums_ref[...] += sums
            total_ref[...] += total


def near_index(cases, all_ref):
    lane = lax.broadcasted_iota(jnp.int32, (1, LANES), 1) // SLOT
    index = jnp.zeros((1, LANES), F32)
    for e, device in enumerate(near_devices()):
        rows = jnp.concatenate([all_ref[device]] * GROUP, axis=0)
        rows = pltpu.roll(rows, SLOT * (e - cases // FOLD) % LANES, 1)
        index = jnp.where(lane == e, rows[cases % FOLD : cases % FOLD + 1], index)
    return index.astype(jnp.int32)


def coarse_kernel(cases, all_ref, inv_high, inv_low, x_ref, total_ref, sums_ref, index_ref):
    gathered_forces(cases, all_ref, total_ref.shape[1], 0, sums_ref, total_ref)
    index_ref[...] = jnp.broadcast_to(near_index(cases, all_ref), index_ref.shape)
    x_ref[...] = product(total_ref[...], inv_high[...], inv_low[...])


def shared_coarse(cases, width, refs):
    *pieces, total_ref, sums_ref, index_ref, whole = refs
    for m, piece in enumerate(pieces):
        base = lax.rem(lax.axis_index("crs") + m, len(pieces)) * width
        whole[:, pl.ds(pl.multiple_of(base, width), width)] = piece[...]
    return whole[...], total_ref[...], sums_ref[...], index_ref[:1]


def pair_kernel(
    cases, all_ref, far_ref, inv_high, inv_low, schur_hbm, x_ref, total_ref, sums_ref, index_ref, *later,
):
    copies = fetched([(schur_hbm.at[0, 0, : later[0].shape[0]], later[0])], later[1]) if later else []
    width = inv_high.shape[1]
    slab = lax.axis_index("crs")
    flip = slab * width

    @always
    def _():
        gathered_forces(cases, all_ref, 4 * width, flip, sums_ref, total_ref)
        index = near_index(cases, all_ref) ^ flip
        index_ref[...] = jnp.broadcast_to(index, index_ref.shape)
        total = total_ref[...]
        last = [
            far_ref[pl.ds(pl.multiple_of((slab % 2 ^ j) * width, width), width)] for j in range(2)
        ]
        third = product(total[:, 2 * width :], *parts(jnp.concatenate(last, axis=0), 2))
        x_ref[:, :width] = product(total, inv_high[...], inv_low[...])
        x_ref[:, width : 2 * width] = jnp.zeros((ROWS, width), F32)
        across = product(total[:, :width], inv_high[2 * width :], inv_low[2 * width :], True)
        x_ref[:, 2 * width : 3 * width] = across[:, :width] + third
        x_ref[:, 3 * width :] = across[:, width:]

    for copy in copies:
        copy.wait()


def paired_coarse(cases, width, refs):
    x_ref, other_ref, total_ref, sums_ref, index_ref = refs
    other = [other_ref[:, (j ^ 1) * width : (j ^ 1) * width + width] for j in range(4)]
    solution = x_ref[...] + jnp.concatenate(other, axis=1)
    return solution, total_ref[...], sums_ref[...], index_ref[:1]


def column(x, lane):
    return x[:, lane : lane + 1]


def second_kernel(cases, coarse, given, *refs):
    (
        pack_ref, left_ref, right_ref, back_ref, one_ref, two_ref,
        s_high, s_low, own_map, left_map, c_high, c_low, corner_ref,
        send_hbm, out_ref, keep_ref, spread_ref, scalar_ref, send, sems,
    ) = refs[given : given + 20]
    solution, total, sums, index = coarse(refs[:given] + refs[given + 20 :])
    picked = moved(solution, chosen_columns(index, solution.shape[1]))
    from_right, from_left = dealt(one_ref[...], two_ref[...])
    blank = jnp.zeros((SLOT - (right_ref.shape[0] - ROWS), right_ref.shape[1]), F32)
    none = jnp.zeros((SLOT, right_ref.shape[1]), F32)
    own = jnp.concatenate([none, right_ref[ROWS:], blank, -from_right[ROWS:], blank, none], axis=0)
    other = jnp.concatenate([from_left[ROWS:], blank, -back_ref[ROWS:], blank, none, none], axis=0)
    spread_ref[...] = own
    both = product(picked, *parts(jnp.concatenate([own, other], axis=1), 2))
    records = right_ref.shape[1]
    residual, scale, _ = unpacked(pack_ref[...], cases)
    left_residual, left_scale, _ = unpacked(left_ref[...], cases)
    live = (scale > 0.0).astype(F32)
    left_live = (left_scale > 0.0).astype(F32)
    image = (right_ref[:ROWS] - from_right[:ROWS] + both[:, :records]) * live
    left_image = (from_left[:ROWS] - back_ref[:ROWS] + both[:, records:]) * left_live
    norm = column(sums, SLOT - 2)
    curvature = column(sums, SLOT - 1) + row_sum(total * solution)
    row = lax.broadcasted_iota(jnp.int32, (ROWS, 1), 0)
    alpha = jnp.where(row < cases, norm / curvature, 0.0)
    residual = residual - alpha * image
    left_residual = left_residual - alpha * left_image
    precon = scale * residual
    left_precon = left_scale * left_residual
    load = moved(precon, own_map[...], True) - moved(left_precon, left_map[...], True)
    through = product(load, s_high[...], s_low[...])
    norm_here = row_sum(residual * precon)
    copy = forces(load, through, norm_here, c_high, c_low, corner_ref, cases, send_hbm, send, sems)

    @always
    def _():
        out_ref[...] = moved(through, left_map[...])
        keep_ref[:ROWS] = moved(through, own_map[...])
        keep_ref[ROWS:] = image
        lane = lax.broadcasted_iota(jnp.int32, scalar_ref.shape, 1)
        scalar_ref[...] = jnp.where(lane == 0, norm, alpha)

    copy.wait()


def last_kernel(cases, coarse, given, *refs):
    (
        pack_ref, from_right, keep_ref, spread_ref, scalar_ref, multipliers_ref, residual_ref,
    ) = refs[given : given + 7]
    solution, total, sums, index = coarse(refs[:given] + refs[given + 7 :])
    picked = moved(solution, chosen_columns(index, solution.shape[1]))
    residual, scale, _ = unpacked(pack_ref[...], cases)
    live = (scale > 0.0).astype(F32)
    spread = product(picked, *parts(spread_ref[...], 2))
    image = (keep_ref[:ROWS] - from_right[...] + spread) * live
    along = keep_ref[ROWS:]
    first_norm = column(scalar_ref[...], 0)
    first_alpha = column(scalar_ref[...], 1)
    norm = column(sums, SLOT - 2)
    curvature = column(sums, SLOT - 1) + row_sum(total * solution)
    ratio = norm / first_norm
    alpha = norm / (curvature - ratio * norm / first_alpha)
    direction = scale * residual
    multipliers = first_alpha * direction
    residual = residual - first_alpha * along
    direction = scale * residual + ratio * direction
    along = image + ratio * along
    multipliers = multipliers + alpha * direction
    residual = residual - alpha * along
    for case in range(cases):
        multipliers_ref[case] = multipliers[case : case + 1]
        residual_ref[case] = residual[case : case + 1]


VM = pl.BlockSpec(memory_space=pltpu.VMEM)
SM = pl.BlockSpec(memory_space=pltpu.SMEM)
HB = pl.BlockSpec(memory_space=pltpu.HBM)


def call(kernel, outs, given, specs, scratch=(), moved_bytes=None, stored=0):
    specs = specs + [VM] * (len(given) - len(specs))
    given = [
        pltpu.with_memory_space_constraint(x, pltpu.HBM) if spec is HB else x
        for x, spec in zip(given, specs)
    ]
    return pl.pallas_call(
        kernel,
        out_shape=[jax.ShapeDtypeStruct(shape, kind) for shape, kind in outs],
        in_specs=specs,
        out_specs=[HB] * stored + [VM] * (len(outs) - stored),
        scratch_shapes=list(scratch),
        cost_estimate=moved_bytes
        and pl.CostEstimate(flops=int(4e10) if moved_bytes<0 else 0, bytes_accessed=abs(moved_bytes), transcendentals=0),
        compiler_params=pltpu.CompilerParams(vmem_limit_bytes=VMEM_LIMIT),
    )(*given)


def passed_along(value, axis, steps):
    count = lax.axis_size(axis)
    pairs = [(source, (source + steps) % count) for source in range(count)]
    return lax.ppermute(value, axis, pairs)


def exchanged(value, axis, bit):
    pairs = [(source, source ^ bit) for source in range(lax.axis_size(axis))]
    return lax.ppermute(value, axis, pairs)


def per_device(
    jump_data,
    lumped_scale,
    schur_inverse,
    coarse_coupling,
    corner_inverse,
    own_dof,
    nbr_dof,
    live_count,
    corner_index,
):
    cases, records = jump_data.shape[2:]
    held, iface = coarse_coupling.shape[2:]
    corners, width = corner_inverse.shape
    chain, slabs = lax.axis_size("sub"), lax.axis_size("crs")
    devices = chain * slabs

    def buffers(*arrays):
        return [pltpu.VMEM(a.shape, a.dtype) for a in arrays] + [
            pltpu.SemaphoreType.DMA((len(arrays),))
        ]

    jump = jump_data.reshape(cases, 1, records)
    first = (jump, lumped_scale, nbr_dof)
    pack, half = call(
        pack_kernel,
        [((ROWS, records), F32), ((2 * width, width), F32)],
        (live_count, *first, corner_inverse),
        [SM] + [HB] * 4,
        [*buffers(*first)[:-1], pltpu.SemaphoreType.DMA((4,))],
    )
    if is_paired(width):
        far = exchanged(half, "crs", 2)
    left = passed_along(pack, "sub", 1)
    fetched_here = (schur_inverse, coarse_coupling, own_dof, corner_index)
    s_high, s_low, c_high, c_low, own_coupling, load, index, own = call(
        functools.partial(prepare_kernel, cases),
        [
            ((iface, iface), BF16),
            ((iface, iface), BF16),
            ((SLOT, iface), BF16),
            ((SLOT, iface), BF16),
            ((held, records), F32),
            ((ROWS, iface), F32),
            ((1, LANES), F32),
            ((1, records), jnp.int32),
        ],
        (pack, *fetched_here),
        [VM] + [HB] * 4,
        buffers(*fetched_here),
        32 << 20,
    )
    inv_high, inv_low = call(
        inverse_kernel,
        [((corners, width), BF16)] * 2,
        (corner_inverse,),
        [HB],
        [pltpu.VMEM((corners, width), F32), pltpu.SemaphoreType.DMA((slabs,))],
    )
    outgoing = [pltpu.VMEM((devices, FOLD, LANES), F32), pltpu.SemaphoreType.DMA((1,))]
    send, right, back, one, two, left_index = call(
        functools.partial(first_kernel, cases),
        [((devices, FOLD, LANES), F32)]
        + [((ROWS + held, records), F32)] * 4
        + [((1, records), jnp.int32)],
        (left, pack, load, own_coupling, index, s_high, s_low, c_high, c_low, own),
        [],
        outgoing,
        -1,
        stored=1,
    )

    top = (iface // 16 * 8, iface)

    def gathered(send, beside, ahead):
        everyone = lax.all_to_all(send, ("sub", "crs"), 0, 0)
        row = (ROWS, corners)
        outs = [(row, F32), ((ROWS, LANES), F32), ((ROWS, LANES), jnp.int32)]
        if is_paired(width):
            x, total, sums, near, *fetched = call(
                functools.partial(pair_kernel, cases),
                [(row, F32), *outs] + [(top, F32)] * ahead,
                (everyone, far, inv_high, inv_low, schur_inverse),
                [VM] * 4 + [HB],
                [pltpu.SemaphoreType.DMA((1,))] * ahead,
            )
            if beside is not None:
                x, _ = lax.optimization_barrier((x, beside))
            return (
                (x, exchanged(x, "crs", 1), total, sums, near),
                [VM] * 5,
                [],
                functools.partial(paired_coarse, cases, width),
                *fetched,
            )
        x, *others = call(
            functools.partial(coarse_kernel, cases),
            [((ROWS, width), F32), *outs],
            (everyone, inv_high, inv_low),
            [],
        )
        pieces = [x] + [passed_along(x, "crs", -m) for m in range(1, slabs)]
        return (
            (*pieces, *others),
            [VM] * (len(pieces) + len(others)),
            [pltpu.VMEM(row, F32)],
            functools.partial(shared_coarse, cases, width),
            *[schur_inverse[0, 0, : top[0]]] * ahead,
        )

    if by_turns(chain):
        rounds = [[(c, (c + 1) % chain) for c in range(start, chain, 2)] for start in (0, 1)]
        rounds = [pairs + [(b, a) for a, b in pairs] for pairs in rounds]
        two = lax.ppermute(two, "sub", rounds[1])
        one = lax.ppermute(one, "sub", rounds[0])
    else:
        one, two = passed_along(two, "sub", -1), passed_along(one, "sub", 1)
    given, specs, scratch, coarse, first_rows = gathered(send, None, 1)
    terms = call(
        terms_kernel,
        [((iface, iface), BF16)] * 2 + [((iface, records), BF16)] * 2,
        (first_rows, left_index, own, schur_inverse),
        [VM] * 3 + [HB],
        [pltpu.VMEM((iface - top[0], iface), F32), pltpu.SemaphoreType.DMA((1,))],
    )
    send, out, keep, spread, scalars = call(
        functools.partial(second_kernel, cases, coarse, len(given)),
        [
            ((devices, FOLD, LANES), F32),
            ((ROWS, records), F32),
            ((2 * ROWS, records), F32),
            ((LANES, records), F32),
            ((ROWS, LANES), F32),
        ],
        (
            *given, pack, left, right, back, one, two,
            *terms, c_high, c_low, index,
        ),
        specs,
        outgoing + scratch,
        stored=1,
    )
    from_right = passed_along(out, "sub", -1)
    given, specs, scratch, coarse = gathered(send, from_right, 0)
    outs = call(
        functools.partial(last_kernel, cases, coarse, len(given)),
        [(jump.shape, F32), (jump.shape, F32)],
        (*given, pack, from_right, keep, spread, scalars),
        specs,
        scratch,
    )
    return tuple(out.reshape(jump_data.shape) for out in outs)


def solution(mesh):
    return jax.shard_map(
        per_device,
        mesh=mesh,
        in_specs=(
            P("sub", "crs", None, None),
            P("sub", "crs", None),
            P("sub", "crs", None, None),
            P("sub", "crs", None, None),
            P(None, "crs"),
            P("sub", "crs", None),
            P("sub", "crs", None),
            P("sub", "crs"),
            P("sub", "crs", None),
        ),
        out_specs=(P("sub", "crs", None, None), P("sub", "crs", None, None)),
        check_vma=False,
    )
```

```python
import functools

import jax
import jax.numpy as jnp
from jax import lax
from jax.experimental import pallas as pl
from jax.experimental.pallas import tpu as pltpu
from jax.sharding import PartitionSpec as P

F32 = jnp.float32
BF16 = jnp.bfloat16
ROWS = 8
LANES = 128
SLOT = 32
GROUP = LANES // SLOT
FOLD = ROWS // GROUP
VMEM_LIMIT = 24 << 20


def parts(x, count):
    out = []
    for _ in range(count):
        out.append(x.astype(BF16))
        x = x - out[-1].astype(F32)
    return out


def dot(a, b, transposed=False):
    dims = (((1,), (1 if transposed else 0,)), ((), ()))
    return lax.dot_general(a, b, dims, preferred_element_type=F32)


def exact(a, chosen, count, transposed=False):
    rows = a.shape[0]
    all_parts = dot(jnp.concatenate(parts(a, count), axis=0), chosen, transposed)
    return sum(all_parts[i * rows : (i + 1) * rows] for i in range(count))


def lows(index):
    rows = lax.broadcasted_iota(jnp.int32, (LANES, index.shape[1]), 0)
    return jnp.where(rows == (index & (LANES - 1)), 1.0, 0.0).astype(BF16)


def added_up(a, index, size):
    rows = a.shape[0]
    high = index >> 7
    stacked = [jnp.where(high == h, a, 0.0) for h in range(size // LANES)]
    out = exact(jnp.concatenate(stacked, axis=0), lows(index), 2, True)
    return jnp.concatenate([out[h * rows : (h + 1) * rows] for h in range(size // LANES)], axis=1)


def taken(a, index):
    rows, size = a.shape
    high = index >> 7
    stacked = [a[:, h * LANES : (h + 1) * LANES] for h in range(size // LANES)]
    out = exact(jnp.concatenate(stacked, axis=0), lows(index), 2)
    return sum(jnp.where(high == h, out[h * rows : (h + 1) * rows], 0.0) for h in range(size // LANES))


def product(a, high, low, transposed=False):
    rows = a.shape[0]
    top, rest = parts(a, 2)
    both = dot(jnp.concatenate([top, rest], axis=0), high, transposed)
    return both[:rows] + both[rows:] + dot(top, low, transposed)


def row_sum(x):
    return jnp.sum(x, axis=1, keepdims=True)


def padded(x, rows):
    return jnp.concatenate([x, jnp.zeros((rows - x.shape[0], x.shape[1]), x.dtype)], axis=0)


def fetched(pairs, sems):
    copies = [
        pltpu.make_async_copy(source, target, sems.at[i]) for i, (source, target) in enumerate(pairs)
    ]
    for copy in copies:
        copy.start()
    return copies


def always(body):
    pl.when(lax.axis_index("crs") >= 0)(body)


def pack_kernel(
    live_ref, jump_hbm, scale_hbm, nbr_hbm, inverse_hbm, out_ref, half_ref, jump, scale, nbr, sems,
):
    cases, _, records = jump.shape
    copies = fetched(
        [
            (jump_hbm, jump),
            (scale_hbm, scale),
            (nbr_hbm, nbr),
            (half_of(lax.axis_index("crs"), inverse_hbm), half_ref),
        ],
        sems,
    )
    for copy in copies:
        copy.wait()
    live = lax.broadcasted_iota(jnp.int32, (1, records), 1) < live_ref[0, 0]
    live = live.astype(F32)
    for case in range(cases):
        out_ref[case : case + 1] = jump[case] * live
    out_ref[cases : cases + 1] = scale[0] * live
    out_ref[cases + 1 : cases + 2] = nbr[0].astype(F32)


def unpacked(pack, cases):
    rows = lax.broadcasted_iota(jnp.int32, pack.shape, 0)
    residual = jnp.where(rows < cases, pack, 0.0)
    return residual, pack[cases : cases + 1], pack[cases + 1 : cases + 2].astype(jnp.int32)


def near_devices():
    chain, slabs = lax.axis_size("sub"), lax.axis_size("crs")
    here, slab = lax.axis_index("sub"), lax.axis_index("crs")
    return [lax.rem(here + step, chain) * slabs + slab for step in (chain - 1, 0, 1)]


def is_paired(width):
    return lax.axis_size("crs") == 4 and width & (width - 1) == 0


def block_at(slab, j, width):
    return slab ^ j if is_paired(width) else j


def by_turns(count):
    return count % 2 == 0


def dealt(right, left):
    if not by_turns(lax.axis_size("sub")):
        return right, left
    even = lax.rem(lax.axis_index("sub"), 2) == 0
    return jnp.where(even, right, left), jnp.where(even, left, right)


PIECES = 6


def pieces(source, target, count):
    rows = source.shape[2] // count
    at = [(0, 0, pl.ds(i * rows, rows)) for i in range(count)]
    return [(source.at[i], target.at[i]) for i in at]


def split_as_it_comes(copies, whole, high, low, first):
    rows = whole.shape[2] // len(copies)
    for i in range(first // rows, (first + high.shape[0]) // rows):
        copies[i].wait()
        at = slice(i * rows - first, (i + 1) * rows - first)
        high[at], low[at] = parts(whole[0, 0, i * rows : (i + 1) * rows], 2)


def half_of(slab, inverse_hbm):
    rows = 2 * inverse_hbm.shape[1]
    first = jnp.minimum(slab // 2 * rows, inverse_hbm.shape[0] - rows)
    return inverse_hbm.at[pl.ds(pl.multiple_of(first, 8), rows)]


def prepare_kernel(
    cases, pack_ref, schur_hbm, coupling_hbm, own_hbm, corner_hbm,
    top_high, top_low, s_high, s_low, c_high, c_low, own_coupling, load_ref, index_ref, own_ref,
    schur, coupling, own, corner, sems,
):
    copies = fetched(
        [
            (own_hbm, own),
            (coupling_hbm, coupling),
            (corner_hbm, corner),
            *pieces(schur_hbm, schur, PIECES),
        ],
        sems,
    )
    for copy in copies[:3]:
        copy.wait()
    held, iface = coupling.shape[2:]
    block = padded(coupling[0, 0], SLOT)
    c_high[...], c_low[...] = parts(block, 2)
    own_ref[...] = own[0]
    own_coupling[...] = taken(block, own[0])[:held]
    residual, scale, _ = unpacked(pack_ref[...], cases)
    load_ref[...] = added_up(residual * scale, own[0], iface)
    lane = lax.broadcasted_iota(jnp.int32, (held, LANES), 1) % SLOT
    tiles = jnp.where(lane == lax.broadcasted_iota(jnp.int32, (held, LANES), 0), 1.0, 0.0)
    index = jnp.broadcast_to(corner[0].astype(F32), (ROWS, held))
    index_ref[...] = jnp.where(lane[:1] < held, exact(index, tiles.astype(BF16), 2)[:1], -1.0)
    split_as_it_comes(copies[3:], schur, top_high, top_low, 0)
    split_as_it_comes(copies[3:], schur, s_high, s_low, top_high.shape[0])


def inverse_kernel(inverse_hbm, inv_high, inv_low, inverse, sems):
    blocks, width = lax.axis_size("crs"), inverse.shape[1]
    pairs = []
    for j in range(blocks):
        rows = pl.ds(pl.multiple_of(block_at(lax.axis_index("crs"), j, width) * width, width), width)
        pairs.append((inverse_hbm.at[rows], inverse.at[pl.ds(j * width, width)]))
    for copy in fetched(pairs, sems):
        copy.wait()
    inv_high[...], inv_low[...] = parts(inverse[...], 2)


def terms_kernel(rows_ref, schur_hbm, s_high, s_low, rest, sems):
    rows, left = rows_ref.shape[0], rest.shape[0]
    size = schur_hbm.shape[2]
    (copy,) = fetched([(schur_hbm.at[0, 0, pl.ds(size - left, left)], rest)], sems)

    @always
    def _():
        s_high[:rows], s_low[:rows] = parts(rows_ref[...], 2)

    copy.wait()
    s_high[rows:], s_low[rows:] = parts(rest[...], 2)


def schur_product(load, top_high, top_low, s_high, s_low):
    rows = top_high.shape[0]
    top = product(load[:, :rows], top_high[...], top_low[...])
    return top + product(load[:, rows:], s_high[...], s_low[...])


def forces(load, through, first, c_high, c_low, index_ref, cases, send_hbm, send, sems):
    high, low = [jnp.concatenate([c[...]] * GROUP, axis=0) for c in (c_high, c_low)]
    force = product(load, high, low, True)
    lane = lax.broadcasted_iota(jnp.int32, force.shape, 1) % SLOT
    row = lax.broadcasted_iota(jnp.int32, force.shape, 0)
    force = jnp.where(lane == SLOT - 2, first, force)
    force = jnp.where(lane == SLOT - 1, row_sum(load * through), force)
    force = jnp.where(row == cases, index_ref[...], force)
    block = lax.broadcasted_iota(jnp.int32, force.shape, 1) // SLOT
    force = jnp.where(row // FOLD == block, force, 0.0)
    folded = sum(force[b * FOLD : (b + 1) * FOLD] for b in range(GROUP))
    send[...] = jnp.broadcast_to(folded[None], send.shape)
    (copy,) = fetched([(send, send_hbm)], sems)
    return copy


def unfolded(four):
    block = lax.broadcasted_iota(jnp.int32, four.shape, 1) // SLOT
    place = lax.broadcasted_iota(jnp.int32, four.shape, 0) // FOLD
    out = four
    for k in range(1, GROUP):
        turned = pltpu.roll(pltpu.roll(four, SLOT * k, 1), ROWS - FOLD * k, 0)
        out = jnp.where((block - place) % GROUP == k, turned, out)
    return out


def first_kernel(
    cases, left_ref, pack_ref, load_ref, own_coupling, index_ref,
    top_high, top_low, s_high, s_low, c_high, c_low, own_ref,
    send_hbm, one_ref, two_ref, index_out, send, sems,
):
    left_residual, left_scale, left_index = unpacked(left_ref[...], cases)
    index_out[...] = left_index
    iface = load_ref.shape[1]
    load = load_ref[...] - added_up(left_residual * left_scale, left_index, iface)
    through = schur_product(load, top_high, top_low, s_high, s_low)
    residual, scale, _ = unpacked(pack_ref[...], cases)
    norm = row_sum(residual * residual * scale)
    copy = forces(load, through, norm, c_high, c_low, index_ref, cases, send_hbm, send, sems)

    @always
    def _():
        held = own_coupling.shape[0]
        one_ref[:ROWS], two_ref[:ROWS] = dealt(
            taken(through, own_ref[...]), taken(through, left_index)
        )
        coupling = c_high[...].astype(F32) + c_low[...].astype(F32)
        one_ref[ROWS:], two_ref[ROWS:] = dealt(
            own_coupling[...], taken(coupling, left_index)[:held]
        )

    copy.wait()


def gathered_forces(cases, all_ref, corners, flip, sums_ref, total_ref):
    devices = all_ref.shape[0]
    chunk = min(devices, LANES // GROUP)
    row = lax.broadcasted_iota(jnp.int32, (ROWS, 1), 0)

    def add(at):
        pieces = [
            unfolded(jnp.concatenate([all_ref[at + group + e] for e in range(GROUP)], axis=0))
            for group in range(0, chunk, GROUP)
        ]
        sums = sum(pieces)
        for turn in (SLOT, 2 * SLOT):
            sums = sums + pltpu.roll(sums, turn, 1)
        flat = jnp.concatenate(pieces, axis=1)
        index = flat[cases : cases + 1].astype(jnp.int32) ^ flip
        force = jnp.where(row < cases, flat, 0.0)
        return sums, added_up(force, index, corners)

    sums_ref[...], total_ref[...] = add(0)
    if devices > chunk:

        @pl.loop(1, devices // chunk)
        def _(i):
            sums, total = add(i * chunk)
            sums_ref[...] += sums
            total_ref[...] += total


def near_index(cases, all_ref):
    lane = lax.broadcasted_iota(jnp.int32, (1, LANES), 1) // SLOT
    index = jnp.zeros((1, LANES), F32)
    for e, device in enumerate(near_devices()):
        rows = jnp.concatenate([all_ref[device]] * GROUP, axis=0)
        rows = pltpu.roll(rows, SLOT * (e - cases // FOLD) % LANES, 1)
        index = jnp.where(lane == e, rows[cases % FOLD : cases % FOLD + 1], index)
    return index.astype(jnp.int32)


def coarse_kernel(cases, all_ref, inv_high, inv_low, x_ref, total_ref, sums_ref, index_ref):
    gathered_forces(cases, all_ref, total_ref.shape[1], 0, sums_ref, total_ref)
    index_ref[...] = jnp.broadcast_to(near_index(cases, all_ref), index_ref.shape)
    x_ref[...] = product(total_ref[...], inv_high[...], inv_low[...])


def shared_coarse(cases, width, refs):
    *pieces, total_ref, sums_ref, index_ref, whole = refs
    for m, piece in enumerate(pieces):
        base = lax.rem(lax.axis_index("crs") + m, len(pieces)) * width
        whole[:, pl.ds(pl.multiple_of(base, width), width)] = piece[...]
    return whole[...], total_ref[...], sums_ref[...], index_ref[:1]


def pair_kernel(
    cases, first_row, all_ref, far_ref, inv_high, inv_low, schur_hbm, x_ref, total_ref, sums_ref, index_ref, *later,
):
    copies = []
    if later:
        rows, sems = later
        copies = fetched([(schur_hbm.at[0, 0, pl.ds(first_row, rows.shape[0])], rows)], sems)
    width = inv_high.shape[1]
    slab = lax.axis_index("crs")
    flip = slab * width

    @always
    def _():
        gathered_forces(cases, all_ref, 4 * width, flip, sums_ref, total_ref)
        index = near_index(cases, all_ref) ^ flip
        index_ref[...] = jnp.broadcast_to(index, index_ref.shape)
        total = total_ref[...]
        last = [
            far_ref[pl.ds(pl.multiple_of((slab % 2 ^ j) * width, width), width)] for j in range(2)
        ]
        third = product(total[:, 2 * width :], *parts(jnp.concatenate(last, axis=0), 2))
        x_ref[:, :width] = product(total, inv_high[...], inv_low[...])
        x_ref[:, width : 2 * width] = jnp.zeros((ROWS, width), F32)
        across = product(total[:, :width], inv_high[2 * width :], inv_low[2 * width :], True)
        x_ref[:, 2 * width : 3 * width] = across[:, :width] + third
        x_ref[:, 3 * width :] = across[:, width:]

    for copy in copies:
        copy.wait()


def paired_coarse(cases, width, refs):
    x_ref, other_ref, total_ref, sums_ref, index_ref = refs
    other = [other_ref[:, (j ^ 1) * width : (j ^ 1) * width + width] for j in range(4)]
    solution = x_ref[...] + jnp.concatenate(other, axis=1)
    return solution, total_ref[...], sums_ref[...], index_ref[:1]


def column(x, lane):
    return x[:, lane : lane + 1]


def second_kernel(cases, coarse, given, *refs):
    (
        pack_ref, left_ref, one_sent, two_sent, one_ref, two_ref,
        top_high, top_low, s_high, s_low, own_ref, left_index, c_high, c_low, corner_ref,
        send_hbm, out_ref, keep_ref, spread_ref, scalar_ref, send, sems,
    ) = refs[given : given + 22]
    solution, total, sums, index = coarse(refs[:given] + refs[given + 22 :])
    picked = taken(solution, index)
    right, back = dealt(one_sent[...], two_sent[...])
    from_right, from_left = dealt(one_ref[...], two_ref[...])
    blank = jnp.zeros((SLOT - (right.shape[0] - ROWS), right.shape[1]), F32)
    none = jnp.zeros((SLOT, right.shape[1]), F32)
    own = jnp.concatenate([none, right[ROWS:], blank, -from_right[ROWS:], blank, none], axis=0)
    other = jnp.concatenate([from_left[ROWS:], blank, -back[ROWS:], blank, none, none], axis=0)
    spread_ref[...] = own
    both = product(picked, *parts(jnp.concatenate([own, other], axis=1), 2))
    records = right.shape[1]
    residual, scale, _ = unpacked(pack_ref[...], cases)
    left_residual, left_scale, _ = unpacked(left_ref[...], cases)
    live = (scale > 0.0).astype(F32)
    left_live = (left_scale > 0.0).astype(F32)
    image = (right[:ROWS] - from_right[:ROWS] + both[:, :records]) * live
    left_image = (from_left[:ROWS] - back[:ROWS] + both[:, records:]) * left_live
    norm = column(sums, SLOT - 2)
    curvature = column(sums, SLOT - 1) + row_sum(total * solution)
    row = lax.broadcasted_iota(jnp.int32, (ROWS, 1), 0)
    alpha = jnp.where(row < cases, norm / curvature, 0.0)
    residual = residual - alpha * image
    left_residual = left_residual - alpha * left_image
    precon = scale * residual
    left_precon = left_scale * left_residual
    iface = c_high.shape[1]
    load = added_up(precon, own_ref[...], iface) - added_up(left_precon, left_index[...], iface)
    through = schur_product(load, top_high, top_low, s_high, s_low)
    norm_here = row_sum(residual * precon)
    copy = forces(load, through, norm_here, c_high, c_low, corner_ref, cases, send_hbm, send, sems)

    @always
    def _():
        out_ref[...] = taken(through, left_index[...])
        keep_ref[:ROWS] = taken(through, own_ref[...])
        keep_ref[ROWS:] = image
        lane = lax.broadcasted_iota(jnp.int32, scalar_ref.shape, 1)
        scalar_ref[...] = jnp.where(lane == 0, norm, alpha)

    copy.wait()


def last_kernel(cases, coarse, given, *refs):
    (
        pack_ref, from_right, keep_ref, spread_ref, scalar_ref, multipliers_ref, residual_ref,
    ) = refs[given : given + 7]
    solution, total, sums, index = coarse(refs[:given] + refs[given + 7 :])
    picked = taken(solution, index)
    residual, scale, _ = unpacked(pack_ref[...], cases)
    live = (scale > 0.0).astype(F32)
    spread = product(picked, *parts(spread_ref[...], 2))
    image = (keep_ref[:ROWS] - from_right[...] + spread) * live
    along = keep_ref[ROWS:]
    first_norm = column(scalar_ref[...], 0)
    first_alpha = column(scalar_ref[...], 1)
    norm = column(sums, SLOT - 2)
    curvature = column(sums, SLOT - 1) + row_sum(total * solution)
    ratio = norm / first_norm
    alpha = norm / (curvature - ratio * norm / first_alpha)
    direction = scale * residual
    multipliers = first_alpha * direction
    residual = residual - first_alpha * along
    direction = scale * residual + ratio * direction
    along = image + ratio * along
    multipliers = multipliers + alpha * direction
    residual = residual - alpha * along
    for case in range(cases):
        multipliers_ref[case] = multipliers[case : case + 1]
        residual_ref[case] = residual[case : case + 1]


VM = pl.BlockSpec(memory_space=pltpu.VMEM)
SM = pl.BlockSpec(memory_space=pltpu.SMEM)
HB = pl.BlockSpec(memory_space=pltpu.HBM)


def call(kernel, outs, given, specs, scratch=(), moved_bytes=None, stored=0):
    specs = specs + [VM] * (len(given) - len(specs))
    given = [
        pltpu.with_memory_space_constraint(x, pltpu.HBM) if spec is HB else x
        for x, spec in zip(given, specs)
    ]
    return pl.pallas_call(
        kernel,
        out_shape=[jax.ShapeDtypeStruct(shape, kind) for shape, kind in outs],
        in_specs=specs,
        out_specs=[HB] * stored + [VM] * (len(outs) - stored),
        scratch_shapes=list(scratch),
        cost_estimate=moved_bytes
        and pl.CostEstimate(flops=int(4e10) if moved_bytes<0 else 0, bytes_accessed=abs(moved_bytes), transcendentals=0),
        compiler_params=pltpu.CompilerParams(vmem_limit_bytes=VMEM_LIMIT),
    )(*given)


def passed_along(value, axis, steps):
    count = lax.axis_size(axis)
    pairs = [(source, (source + steps) % count) for source in range(count)]
    return lax.ppermute(value, axis, pairs)


def exchanged(value, axis, bit):
    pairs = [(source, source ^ bit) for source in range(lax.axis_size(axis))]
    return lax.ppermute(value, axis, pairs)


def per_device(
    jump_data,
    lumped_scale,
    schur_inverse,
    coarse_coupling,
    corner_inverse,
    own_dof,
    nbr_dof,
    live_count,
    corner_index,
):
    cases, records = jump_data.shape[2:]
    held, iface = coarse_coupling.shape[2:]
    corners, width = corner_inverse.shape
    chain, slabs = lax.axis_size("sub"), lax.axis_size("crs")
    devices = chain * slabs

    def buffers(*arrays):
        return [pltpu.VMEM(a.shape, a.dtype) for a in arrays] + [
            pltpu.SemaphoreType.DMA((len(arrays),))
        ]

    jump = jump_data.reshape(cases, 1, records)
    first = (jump, lumped_scale, nbr_dof)
    pack, half = call(
        pack_kernel,
        [((ROWS, records), F32), ((2 * width, width), F32)],
        (live_count, *first, corner_inverse),
        [SM] + [HB] * 4,
        [*buffers(*first)[:-1], pltpu.SemaphoreType.DMA((4,))],
    )
    if is_paired(width):
        far = exchanged(half, "crs", 2)
    left = passed_along(pack, "sub", 1)
    fetched_here = (schur_inverse, coarse_coupling, own_dof, corner_index)
    top = iface // 3 // LANES * LANES
    *tops, s_high, s_low, c_high, c_low, own_coupling, load, index, own = call(
        functools.partial(prepare_kernel, cases),
        [
            ((top, iface), BF16),
            ((top, iface), BF16),
            ((iface - top, iface), BF16),
            ((iface - top, iface), BF16),
            ((SLOT, iface), BF16),
            ((SLOT, iface), BF16),
            ((held, records), F32),
            ((ROWS, iface), F32),
            ((1, LANES), F32),
            ((1, records), jnp.int32),
        ],
        (pack, *fetched_here),
        [VM] + [HB] * 4,
        [*buffers(*fetched_here)[:-1], pltpu.SemaphoreType.DMA((3 + PIECES,))],
        32 << 20,
    )
    inv_high, inv_low = call(
        inverse_kernel,
        [((corners, width), BF16)] * 2,
        (corner_inverse,),
        [HB],
        [pltpu.VMEM((corners, width), F32), pltpu.SemaphoreType.DMA((slabs,))],
    )
    outgoing = [pltpu.VMEM((devices, FOLD, LANES), F32), pltpu.SemaphoreType.DMA((1,))]
    send, one_sent, two_sent, left_index = call(
        functools.partial(first_kernel, cases),
        [((devices, FOLD, LANES), F32)]
        + [((ROWS + held, records), F32)] * 2
        + [((1, records), jnp.int32)],
        (left, pack, load, own_coupling, index, *tops, s_high, s_low, c_high, c_low, own),
        [],
        outgoing,
        -1,
        stored=1,
    )

    more = iface // 64 * 16

    def gathered(send, beside, ahead):
        everyone = lax.all_to_all(send, ("sub", "crs"), 0, 0)
        row = (ROWS, corners)
        outs = [(row, F32), ((ROWS, LANES), F32), ((ROWS, LANES), jnp.int32)]
        if is_paired(width):
            x, total, sums, near, *fetched = call(
                functools.partial(pair_kernel, cases, top),
                [(row, F32), *outs] + [((more, iface), F32)] * ahead,
                (everyone, far, inv_high, inv_low, schur_inverse),
                [VM] * 4 + [HB],
                [pltpu.SemaphoreType.DMA((1,))] * ahead,
            )
            if beside is not None:
                x, _ = lax.optimization_barrier((x, beside))
            return (
                (x, exchanged(x, "crs", 1), total, sums, near),
                [VM] * 5,
                [],
                functools.partial(paired_coarse, cases, width),
                *fetched,
            )
        x, *others = call(
            functools.partial(coarse_kernel, cases),
            [((ROWS, width), F32), *outs],
            (everyone, inv_high, inv_low),
            [],
        )
        pieces = [x] + [passed_along(x, "crs", -m) for m in range(1, slabs)]
        return (
            (*pieces, *others),
            [VM] * (len(pieces) + len(others)),
            [pltpu.VMEM(row, F32)],
            functools.partial(shared_coarse, cases, width),
            *[schur_inverse[0, 0, top : top + more]] * ahead,
        )

    if by_turns(chain):
        rounds = [[(c, (c + 1) % chain) for c in range(start, chain, 2)] for start in (0, 1)]
        rounds = [pairs + [(b, a) for a, b in pairs] for pairs in rounds]
        two = lax.ppermute(two_sent, "sub", rounds[1])
        one = lax.ppermute(one_sent, "sub", rounds[0])
    else:
        one, two = passed_along(two_sent, "sub", -1), passed_along(one_sent, "sub", 1)
    given, specs, scratch, coarse, first_rows = gathered(send, None, 1)
    terms = call(
        terms_kernel,
        [((iface - top, iface), BF16)] * 2,
        (first_rows, schur_inverse),
        [VM, HB],
        [pltpu.VMEM((iface - top - more, iface), F32), pltpu.SemaphoreType.DMA((1,))],
    )
    send, out, keep, spread, scalars = call(
        functools.partial(second_kernel, cases, coarse, len(given)),
        [
            ((devices, FOLD, LANES), F32),
            ((ROWS, records), F32),
            ((2 * ROWS, records), F32),
            ((LANES, records), F32),
            ((ROWS, LANES), F32),
        ],
        (
            *given, pack, left, one_sent, two_sent, one, two,
            *tops, *terms, own, left_index, c_high, c_low, index,
        ),
        specs,
        outgoing + scratch,
        stored=1,
    )
    from_right = passed_along(out, "sub", -1)
    given, specs, scratch, coarse = gathered(send, from_right, 0)
    outs = call(
        functools.partial(last_kernel, cases, coarse, len(given)),
        [(jump.shape, F32), (jump.shape, F32)],
        (*given, pack, from_right, keep, spread, scalars),
        specs,
        scratch,
    )
    return tuple(out.reshape(jump_data.shape) for out in outs)


def solution(mesh):
    return jax.shard_map(
        per_device,
        mesh=mesh,
        in_specs=(
            P("sub", "crs", None, None),
            P("sub", "crs", None),
            P("sub", "crs", None, None),
            P("sub", "crs", None, None),
            P(None, "crs"),
            P("sub", "crs", None),
            P("sub", "crs", None),
            P("sub", "crs"),
            P("sub", "crs", None),
        ),
        out_specs=(P("sub", "crs", None, None), P("sub", "crs", None, None)),
        check_vma=False,
    )
```

```python
import functools

import jax
import jax.numpy as jnp
from jax import lax
from jax.experimental import pallas as pl
from jax.experimental.pallas import tpu as pltpu
from jax.sharding import PartitionSpec as P

F32 = jnp.float32
BF16 = jnp.bfloat16
ROWS = 8
LANES = 128
SLOT = 32
GROUP = LANES // SLOT
FOLD = ROWS // GROUP
VMEM_LIMIT = 24 << 20


def parts(x, count):
    out = []
    for _ in range(count):
        out.append(x.astype(BF16))
        x = x - out[-1].astype(F32)
    return out


def dot(a, b, transposed=False):
    dims = (((1,), (1 if transposed else 0,)), ((), ()))
    return lax.dot_general(a, b, dims, preferred_element_type=F32)


def exact(a, chosen, count, transposed=False):
    rows = a.shape[0]
    all_parts = dot(jnp.concatenate(parts(a, count), axis=0), chosen, transposed)
    return sum(all_parts[i * rows : (i + 1) * rows] for i in range(count))


def lows(index):
    rows = lax.broadcasted_iota(jnp.int32, (LANES, index.shape[1]), 0)
    return jnp.where(rows == (index & (LANES - 1)), 1.0, 0.0).astype(BF16)


def added_up(a, index, size):
    rows = a.shape[0]
    high = index >> 7
    stacked = [jnp.where(high == h, a, 0.0) for h in range(size // LANES)]
    out = exact(jnp.concatenate(stacked, axis=0), lows(index), 2, True)
    return jnp.concatenate([out[h * rows : (h + 1) * rows] for h in range(size // LANES)], axis=1)


def taken(a, index):
    rows, size = a.shape
    high = index >> 7
    stacked = [a[:, h * LANES : (h + 1) * LANES] for h in range(size // LANES)]
    out = exact(jnp.concatenate(stacked, axis=0), lows(index), 2)
    return sum(jnp.where(high == h, out[h * rows : (h + 1) * rows], 0.0) for h in range(size // LANES))


def product(a, high, low, transposed=False):
    rows = a.shape[0]
    top, rest = parts(a, 2)
    both = dot(jnp.concatenate([top, rest], axis=0), high, transposed)
    return both[:rows] + both[rows:] + dot(top, low, transposed)


def row_sum(x):
    return jnp.sum(x, axis=1, keepdims=True)


def padded(x, rows):
    return jnp.concatenate([x, jnp.zeros((rows - x.shape[0], x.shape[1]), x.dtype)], axis=0)


def fetched(pairs, sems):
    copies = [
        pltpu.make_async_copy(source, target, sems.at[i]) for i, (source, target) in enumerate(pairs)
    ]
    for copy in copies:
        copy.start()
    return copies


def always(body):
    pl.when(lax.axis_index("crs") >= 0)(body)


def pack_kernel(live_ref, jump_hbm, scale_hbm, nbr_hbm, out_ref, jump, scale, nbr, sems):
    for copy in fetched([(jump_hbm, jump), (scale_hbm, scale), (nbr_hbm, nbr)], sems):
        copy.wait()
    cases, _, records = jump.shape
    live = lax.broadcasted_iota(jnp.int32, (1, records), 1) < live_ref[0, 0]
    live = live.astype(F32)
    for case in range(cases):
        out_ref[case : case + 1] = jump[case] * live
    out_ref[cases : cases + 1] = scale[0] * live
    out_ref[cases + 1 : cases + 2] = nbr[0].astype(F32)


def unpacked(pack, cases):
    rows = lax.broadcasted_iota(jnp.int32, pack.shape, 0)
    residual = jnp.where(rows < cases, pack, 0.0)
    return residual, pack[cases : cases + 1], pack[cases + 1 : cases + 2].astype(jnp.int32)


def near_devices():
    chain, slabs = lax.axis_size("sub"), lax.axis_size("crs")
    here, slab = lax.axis_index("sub"), lax.axis_index("crs")
    return [lax.rem(here + step, chain) * slabs + slab for step in (chain - 1, 0, 1)]


def is_paired(width):
    return lax.axis_size("crs") == 4 and width & (width - 1) == 0


def block_at(slab, j, width):
    return slab ^ j if is_paired(width) else j


def by_turns(count):
    return count % 2 == 0


def dealt(right, left):
    if not by_turns(lax.axis_size("sub")):
        return right, left
    even = lax.rem(lax.axis_index("sub"), 2) == 0
    return jnp.where(even, right, left), jnp.where(even, left, right)


PIECES = 6


def pieces(source, target, count):
    rows = source.shape[2] // count
    at = [(0, 0, pl.ds(i * rows, rows)) for i in range(count)]
    return [(source.at[i], target.at[i]) for i in at]


def split_as_it_comes(copies, whole, high, low, first):
    rows = whole.shape[2] // len(copies)
    for i in range(first // rows, (first + high.shape[0]) // rows):
        copies[i].wait()
        at = slice(i * rows - first, (i + 1) * rows - first)
        high[at], low[at] = parts(whole[0, 0, i * rows : (i + 1) * rows], 2)


def half_of(slab, inverse_hbm):
    rows = 2 * inverse_hbm.shape[1]
    first = jnp.minimum(slab // 2 * rows, inverse_hbm.shape[0] - rows)
    return inverse_hbm.at[pl.ds(pl.multiple_of(first, 8), rows)]


def share_of_half(core, half):
    width = half.shape[1]
    own, other = [half[pl.ds(pl.multiple_of(c * width, width), width)] for c in (core, 1 - core)]
    rows = width // 2
    return jnp.concatenate(
        [own, jnp.where(core == 0, other[:rows], jnp.transpose(other[:, rows:]))], axis=0
    )


def far_solution(core, total, share):
    width = share.shape[1]
    rows = width // 2
    near, far = total[:, :width], total[:, width:]
    first = core == 0
    block = parts(share[:width], 2)
    across = parts(share[width:], 2)
    whole = product(jnp.where(first, far[:, :rows], near[:, rows:]), *across)
    piece = product(jnp.where(first, near, far), *across, True)
    none = jnp.zeros_like(piece)
    near = product(near, *block) + jnp.where(first, whole, jnp.concatenate([none, piece], axis=1))
    far = jnp.where(first, jnp.concatenate([piece, none], axis=1), whole)
    return jnp.concatenate([near, far], axis=1)


def prepare_kernel(
    cases, pack_ref, schur_hbm, coupling_hbm, own_hbm, corner_hbm, inverse_hbm,
    top_high, top_low, s_high, s_low, c_high, c_low, own_coupling, load_ref, index_ref, own_ref, share_ref,
    schur, coupling, own, corner, half, sems,
):
    copies = fetched(
        [
            (own_hbm, own),
            (coupling_hbm, coupling),
            (corner_hbm, corner),
            (half_of(lax.axis_index("crs"), inverse_hbm), half),
            *pieces(schur_hbm, schur, PIECES),
        ],
        sems,
    )
    for copy in copies[:3]:
        copy.wait()
    held, iface = coupling.shape[2:]
    block = padded(coupling[0, 0], SLOT)
    c_high[...], c_low[...] = parts(block, 2)
    own_ref[...] = own[0]
    own_coupling[...] = taken(block, own[0])[:held]
    residual, scale, _ = unpacked(pack_ref[...], cases)
    load_ref[...] = added_up(residual * scale, own[0], iface)
    lane = lax.broadcasted_iota(jnp.int32, (held, LANES), 1) % SLOT
    tiles = jnp.where(lane == lax.broadcasted_iota(jnp.int32, (held, LANES), 0), 1.0, 0.0)
    index = jnp.broadcast_to(corner[0].astype(F32), (ROWS, held))
    index_ref[...] = jnp.where(lane[:1] < held, exact(index, tiles.astype(BF16), 2)[:1], -1.0)
    copies[3].wait()
    share_ref[...] = share_of_half(lax.axis_index("crs") % 2, half)
    split_as_it_comes(copies[4:], schur, top_high, top_low, 0)
    split_as_it_comes(copies[4:], schur, s_high, s_low, top_high.shape[0])


def inverse_kernel(inverse_hbm, inv_high, inv_low, inverse, sems):
    blocks, width = lax.axis_size("crs"), inverse.shape[1]
    pairs = []
    for j in range(blocks):
        rows = pl.ds(pl.multiple_of(block_at(lax.axis_index("crs"), j, width) * width, width), width)
        pairs.append((inverse_hbm.at[rows], inverse.at[pl.ds(j * width, width)]))
    for copy in fetched(pairs, sems):
        copy.wait()
    inv_high[...], inv_low[...] = parts(inverse[...], 2)


def terms_kernel(rows_ref, schur_hbm, s_high, s_low, rest, sems):
    rows, left = rows_ref.shape[0], rest.shape[0]
    size = schur_hbm.shape[2]
    (copy,) = fetched([(schur_hbm.at[0, 0, pl.ds(size - left, left)], rest)], sems)

    @always
    def _():
        s_high[:rows], s_low[:rows] = parts(rows_ref[...], 2)

    copy.wait()
    s_high[rows:], s_low[rows:] = parts(rest[...], 2)


def schur_product(load, top_high, top_low, s_high, s_low):
    rows = top_high.shape[0]
    top = product(load[:, :rows], top_high[...], top_low[...])
    return top + product(load[:, rows:], s_high[...], s_low[...])


def forces(load, through, first, c_high, c_low, index_ref, cases, send_hbm, send, sems):
    force = product(load, c_high[...], c_low[...], True)
    force = jnp.concatenate([force] * GROUP, axis=1)
    lane = lax.broadcasted_iota(jnp.int32, force.shape, 1) % SLOT
    row = lax.broadcasted_iota(jnp.int32, force.shape, 0)
    force = jnp.where(lane == SLOT - 2, first, force)
    force = jnp.where(lane == SLOT - 1, row_sum(load * through), force)
    force = jnp.where(row == cases, index_ref[...], force)
    block = lax.broadcasted_iota(jnp.int32, force.shape, 1) // SLOT
    force = jnp.where(row // FOLD == block, force, 0.0)
    folded = sum(force[b * FOLD : (b + 1) * FOLD] for b in range(GROUP))
    send[...] = jnp.broadcast_to(folded[None], send.shape)
    (copy,) = fetched([(send, send_hbm)], sems)
    return copy


def unfolded(four):
    block = lax.broadcasted_iota(jnp.int32, four.shape, 1) // SLOT
    place = lax.broadcasted_iota(jnp.int32, four.shape, 0) // FOLD
    out = four
    for k in range(1, GROUP):
        turned = pltpu.roll(pltpu.roll(four, SLOT * k, 1), ROWS - FOLD * k, 0)
        out = jnp.where((block - place) % GROUP == k, turned, out)
    return out


def first_kernel(
    cases, left_ref, pack_ref, load_ref, own_coupling, index_ref,
    top_high, top_low, s_high, s_low, c_high, c_low, own_ref,
    send_hbm, one_ref, two_ref, index_out, send, sems,
):
    left_residual, left_scale, left_index = unpacked(left_ref[...], cases)
    index_out[...] = left_index
    iface = load_ref.shape[1]
    load = load_ref[...] - added_up(left_residual * left_scale, left_index, iface)
    through = schur_product(load, top_high, top_low, s_high, s_low)
    residual, scale, _ = unpacked(pack_ref[...], cases)
    norm = row_sum(residual * residual * scale)
    copy = forces(load, through, norm, c_high, c_low, index_ref, cases, send_hbm, send, sems)

    @always
    def _():
        held = own_coupling.shape[0]
        one_ref[:ROWS], two_ref[:ROWS] = dealt(
            taken(through, own_ref[...]), taken(through, left_index)
        )
        coupling = c_high[...].astype(F32) + c_low[...].astype(F32)
        one_ref[ROWS:], two_ref[ROWS:] = dealt(
            own_coupling[...], taken(coupling, left_index)[:held]
        )

    copy.wait()


def gathered_forces(cases, all_ref, corners, flip, sums_ref, total_ref):
    devices = all_ref.shape[0]
    chunk = min(devices, LANES // GROUP)
    row = lax.broadcasted_iota(jnp.int32, (ROWS, 1), 0)

    def add(at):
        pieces = [
            unfolded(jnp.concatenate([all_ref[at + group + e] for e in range(GROUP)], axis=0))
            for group in range(0, chunk, GROUP)
        ]
        sums = sum(pieces)
        for turn in (SLOT, 2 * SLOT):
            sums = sums + pltpu.roll(sums, turn, 1)
        flat = jnp.concatenate(pieces, axis=1)
        index = flat[cases : cases + 1].astype(jnp.int32) ^ flip
        force = jnp.where(row < cases, flat, 0.0)
        return sums, added_up(force, index, corners)

    sums_ref[...], total_ref[...] = add(0)
    if devices > chunk:

        @pl.loop(1, devices // chunk)
        def _(i):
            sums, total = add(i * chunk)
            sums_ref[...] += sums
            total_ref[...] += total


def near_index(cases, all_ref):
    lane = lax.broadcasted_iota(jnp.int32, (1, LANES), 1) // SLOT
    index = jnp.zeros((1, LANES), F32)
    for e, device in enumerate(near_devices()):
        rows = jnp.concatenate([all_ref[device]] * GROUP, axis=0)
        rows = pltpu.roll(rows, SLOT * (e - cases // FOLD) % LANES, 1)
        index = jnp.where(lane == e, rows[cases % FOLD : cases % FOLD + 1], index)
    return index.astype(jnp.int32)


def coarse_kernel(cases, all_ref, inv_high, inv_low, x_ref, total_ref, sums_ref, index_ref):
    gathered_forces(cases, all_ref, total_ref.shape[1], 0, sums_ref, total_ref)
    index_ref[...] = jnp.broadcast_to(near_index(cases, all_ref), index_ref.shape)
    x_ref[...] = product(total_ref[...], inv_high[...], inv_low[...])


def shared_coarse(cases, width, refs):
    *pieces, total_ref, sums_ref, index_ref, whole = refs
    for m, piece in enumerate(pieces):
        base = lax.rem(lax.axis_index("crs") + m, len(pieces)) * width
        whole[:, pl.ds(pl.multiple_of(base, width), width)] = piece[...]
    return whole[...], total_ref[...], sums_ref[...], index_ref[:1]


def pair_kernel(
    cases, first_row, all_ref, far_ref, inv_high, inv_low, schur_hbm, x_ref, total_ref, sums_ref, index_ref, *later,
):
    copies = []
    if later:
        rows, sems = later
        copies = fetched([(schur_hbm.at[0, 0, pl.ds(first_row, rows.shape[0])], rows)], sems)
    width = inv_high.shape[1]
    slab = lax.axis_index("crs")
    flip = slab * width

    @always
    def _():
        gathered_forces(cases, all_ref, 4 * width, flip, sums_ref, total_ref)
        index = near_index(cases, all_ref) ^ flip
        index_ref[...] = jnp.broadcast_to(index, index_ref.shape)
        total = total_ref[...]
        x_ref[:, :width] = product(total, inv_high[...], inv_low[...])
        x_ref[:, width : 2 * width] = jnp.zeros((ROWS, width), F32)
        across = product(total[:, :width], inv_high[2 * width :], inv_low[2 * width :], True)
        x_ref[:, 2 * width :] = across + far_solution(slab % 2, total[:, 2 * width :], far_ref[...])

    for copy in copies:
        copy.wait()


def paired_coarse(cases, width, refs):
    x_ref, other_ref, total_ref, sums_ref, index_ref = refs
    other = [other_ref[:, (j ^ 1) * width : (j ^ 1) * width + width] for j in range(4)]
    solution = x_ref[...] + jnp.concatenate(other, axis=1)
    return solution, total_ref[...], sums_ref[...], index_ref[:1]


def column(x, lane):
    return x[:, lane : lane + 1]


def second_kernel(cases, coarse, given, *refs):
    (
        pack_ref, left_ref, one_sent, two_sent, one_ref, two_ref,
        top_high, top_low, s_high, s_low, own_ref, left_index, c_high, c_low, corner_ref,
        send_hbm, out_ref, keep_ref, spread_ref, scalar_ref, send, sems,
    ) = refs[given : given + 22]
    solution, total, sums, index = coarse(refs[:given] + refs[given + 22 :])
    picked = taken(solution, index)
    right, back = dealt(one_sent[...], two_sent[...])
    from_right, from_left = dealt(one_ref[...], two_ref[...])
    blank = jnp.zeros((SLOT - (right.shape[0] - ROWS), right.shape[1]), F32)
    none = jnp.zeros((SLOT, right.shape[1]), F32)
    own = jnp.concatenate([none, right[ROWS:], blank, -from_right[ROWS:], blank, none], axis=0)
    other = jnp.concatenate([from_left[ROWS:], blank, -back[ROWS:], blank, none, none], axis=0)
    spread_ref[...] = own
    both = product(picked, *parts(jnp.concatenate([own, other], axis=1), 2))
    records = right.shape[1]
    residual, scale, _ = unpacked(pack_ref[...], cases)
    left_residual, left_scale, _ = unpacked(left_ref[...], cases)
    live = (scale > 0.0).astype(F32)
    left_live = (left_scale > 0.0).astype(F32)
    image = (right[:ROWS] - from_right[:ROWS] + both[:, :records]) * live
    left_image = (from_left[:ROWS] - back[:ROWS] + both[:, records:]) * left_live
    norm = column(sums, SLOT - 2)
    curvature = column(sums, SLOT - 1) + row_sum(total * solution)
    row = lax.broadcasted_iota(jnp.int32, (ROWS, 1), 0)
    alpha = jnp.where(row < cases, norm / curvature, 0.0)
    residual = residual - alpha * image
    left_residual = left_residual - alpha * left_image
    precon = scale * residual
    left_precon = left_scale * left_residual
    iface = c_high.shape[1]
    load = added_up(precon, own_ref[...], iface) - added_up(left_precon, left_index[...], iface)
    through = schur_product(load, top_high, top_low, s_high, s_low)
    norm_here = row_sum(residual * precon)
    copy = forces(load, through, norm_here, c_high, c_low, corner_ref, cases, send_hbm, send, sems)

    @always
    def _():
        out_ref[...] = taken(through, left_index[...])
        keep_ref[:ROWS] = taken(through, own_ref[...])
        keep_ref[ROWS:] = image
        lane = lax.broadcasted_iota(jnp.int32, scalar_ref.shape, 1)
        scalar_ref[...] = jnp.where(lane == 0, norm, alpha)

    copy.wait()


def last_kernel(cases, coarse, given, *refs):
    (
        pack_ref, from_right, keep_ref, spread_ref, scalar_ref, multipliers_ref, residual_ref,
    ) = refs[given : given + 7]
    solution, total, sums, index = coarse(refs[:given] + refs[given + 7 :])
    picked = taken(solution, index)
    residual, scale, _ = unpacked(pack_ref[...], cases)
    live = (scale > 0.0).astype(F32)
    spread = product(picked, *parts(spread_ref[...], 2))
    image = (keep_ref[:ROWS] - from_right[...] + spread) * live
    along = keep_ref[ROWS:]
    first_norm = column(scalar_ref[...], 0)
    first_alpha = column(scalar_ref[...], 1)
    norm = column(sums, SLOT - 2)
    curvature = column(sums, SLOT - 1) + row_sum(total * solution)
    ratio = norm / first_norm
    alpha = norm / (curvature - ratio * norm / first_alpha)
    direction = scale * residual
    multipliers = first_alpha * direction
    residual = residual - first_alpha * along
    direction = scale * residual + ratio * direction
    along = image + ratio * along
    multipliers = multipliers + alpha * direction
    residual = residual - alpha * along
    for case in range(cases):
        multipliers_ref[case] = multipliers[case : case + 1]
        residual_ref[case] = residual[case : case + 1]


VM = pl.BlockSpec(memory_space=pltpu.VMEM)
SM = pl.BlockSpec(memory_space=pltpu.SMEM)
HB = pl.BlockSpec(memory_space=pltpu.HBM)


def call(kernel, outs, given, specs, scratch=(), moved_bytes=None, stored=0):
    specs = specs + [VM] * (len(given) - len(specs))
    given = [
        pltpu.with_memory_space_constraint(x, pltpu.HBM) if spec is HB else x
        for x, spec in zip(given, specs)
    ]
    return pl.pallas_call(
        kernel,
        out_shape=[jax.ShapeDtypeStruct(shape, kind) for shape, kind in outs],
        in_specs=specs,
        out_specs=[HB] * stored + [VM] * (len(outs) - stored),
        scratch_shapes=list(scratch),
        cost_estimate=moved_bytes
        and pl.CostEstimate(flops=int(4e10) if moved_bytes<0 else 0, bytes_accessed=abs(moved_bytes), transcendentals=0),
        compiler_params=pltpu.CompilerParams(vmem_limit_bytes=VMEM_LIMIT),
    )(*given)


def passed_along(value, axis, steps):
    count = lax.axis_size(axis)
    pairs = [(source, (source + steps) % count) for source in range(count)]
    return lax.ppermute(value, axis, pairs)


def exchanged(value, axis, bit):
    pairs = [(source, source ^ bit) for source in range(lax.axis_size(axis))]
    return lax.ppermute(value, axis, pairs)


def per_device(
    jump_data,
    lumped_scale,
    schur_inverse,
    coarse_coupling,
    corner_inverse,
    own_dof,
    nbr_dof,
    live_count,
    corner_index,
):
    cases, records = jump_data.shape[2:]
    held, iface = coarse_coupling.shape[2:]
    corners, width = corner_inverse.shape
    chain, slabs = lax.axis_size("sub"), lax.axis_size("crs")
    devices = chain * slabs

    def buffers(*arrays):
        return [pltpu.VMEM(a.shape, a.dtype) for a in arrays] + [
            pltpu.SemaphoreType.DMA((len(arrays),))
        ]

    jump = jump_data.reshape(cases, 1, records)
    first = (jump, lumped_scale, nbr_dof)
    (pack,) = call(
        pack_kernel,
        [((ROWS, records), F32)],
        (live_count, *first),
        [SM] + [HB] * 3,
        buffers(*first),
    )
    left = passed_along(pack, "sub", 1)
    fetched_here = (schur_inverse, coarse_coupling, own_dof, corner_index)
    half = (2 * width, width)
    share = (width + width // 2, width)
    top = iface // 3 // LANES * LANES
    *tops, s_high, s_low, c_high, c_low, own_coupling, load, index, own, share = call(
        functools.partial(prepare_kernel, cases),
        [
            ((top, iface), BF16),
            ((top, iface), BF16),
            ((iface - top, iface), BF16),
            ((iface - top, iface), BF16),
            ((SLOT, iface), BF16),
            ((SLOT, iface), BF16),
            ((held, records), F32),
            ((ROWS, iface), F32),
            ((1, LANES), F32),
            ((1, records), jnp.int32),
            (share, F32),
        ],
        (pack, *fetched_here, corner_inverse),
        [VM] + [HB] * 5,
        [
            *buffers(*fetched_here)[:-1],
            pltpu.VMEM(half, F32),
            pltpu.SemaphoreType.DMA((4 + PIECES,)),
        ],
        32 << 20,
    )
    if is_paired(width):
        far = exchanged(share, "crs", 2)
    inv_high, inv_low = call(
        inverse_kernel,
        [((corners, width), BF16)] * 2,
        (corner_inverse,),
        [HB],
        [pltpu.VMEM((corners, width), F32), pltpu.SemaphoreType.DMA((slabs,))],
    )
    outgoing = [pltpu.VMEM((devices, FOLD, LANES), F32), pltpu.SemaphoreType.DMA((1,))]
    send, one_sent, two_sent, left_index = call(
        functools.partial(first_kernel, cases),
        [((devices, FOLD, LANES), F32)]
        + [((ROWS + held, records), F32)] * 2
        + [((1, records), jnp.int32)],
        (left, pack, load, own_coupling, index, *tops, s_high, s_low, c_high, c_low, own),
        [],
        outgoing,
        -1,
        stored=1,
    )

    more = iface // 64 * 16

    def gathered(send, beside, ahead):
        everyone = lax.all_to_all(send, ("sub", "crs"), 0, 0)
        row = (ROWS, corners)
        outs = [(row, F32), ((ROWS, LANES), F32), ((ROWS, LANES), jnp.int32)]
        if is_paired(width):
            x, total, sums, near, *fetched = call(
                functools.partial(pair_kernel, cases, top),
                [(row, F32), *outs] + [((more, iface), F32)] * ahead,
                (everyone, far, inv_high, inv_low, schur_inverse),
                [VM] * 4 + [HB],
                [pltpu.SemaphoreType.DMA((1,))] * ahead,
            )
            if beside is not None:
                x, _ = lax.optimization_barrier((x, beside))
            return (
                (x, exchanged(x, "crs", 1), total, sums, near),
                [VM] * 5,
                [],
                functools.partial(paired_coarse, cases, width),
                *fetched,
            )
        x, *others = call(
            functools.partial(coarse_kernel, cases),
            [((ROWS, width), F32), *outs],
            (everyone, inv_high, inv_low),
            [],
        )
        pieces = [x] + [passed_along(x, "crs", -m) for m in range(1, slabs)]
        return (
            (*pieces, *others),
            [VM] * (len(pieces) + len(others)),
            [pltpu.VMEM(row, F32)],
            functools.partial(shared_coarse, cases, width),
            *[schur_inverse[0, 0, top : top + more]] * ahead,
        )

    if by_turns(chain):
        rounds = [[(c, (c + 1) % chain) for c in range(start, chain, 2)] for start in (0, 1)]
        rounds = [pairs + [(b, a) for a, b in pairs] for pairs in rounds]
        two = lax.ppermute(two_sent, "sub", rounds[1])
        one = lax.ppermute(one_sent, "sub", rounds[0])
    else:
        one, two = passed_along(two_sent, "sub", -1), passed_along(one_sent, "sub", 1)
    given, specs, scratch, coarse, first_rows = gathered(send, None, 1)
    terms = call(
        terms_kernel,
        [((iface - top, iface), BF16)] * 2,
        (first_rows, schur_inverse),
        [VM, HB],
        [pltpu.VMEM((iface - top - more, iface), F32), pltpu.SemaphoreType.DMA((1,))],
    )
    send, out, keep, spread, scalars = call(
        functools.partial(second_kernel, cases, coarse, len(given)),
        [
            ((devices, FOLD, LANES), F32),
            ((ROWS, records), F32),
            ((2 * ROWS, records), F32),
            ((LANES, records), F32),
            ((ROWS, LANES), F32),
        ],
        (
            *given, pack, left, one_sent, two_sent, one, two,
            *tops, *terms, own, left_index, c_high, c_low, index,
        ),
        specs,
        outgoing + scratch,
        stored=1,
    )
    from_right = passed_along(out, "sub", -1)
    given, specs, scratch, coarse = gathered(send, from_right, 0)
    outs = call(
        functools.partial(last_kernel, cases, coarse, len(given)),
        [(jump.shape, F32), (jump.shape, F32)],
        (*given, pack, from_right, keep, spread, scalars),
        specs,
        scratch,
    )
    return tuple(out.reshape(jump_data.shape) for out in outs)


def solution(mesh):
    return jax.shard_map(
        per_device,
        mesh=mesh,
        in_specs=(
            P("sub", "crs", None, None),
            P("sub", "crs", None),
            P("sub", "crs", None, None),
            P("sub", "crs", None, None),
            P(None, "crs"),
            P("sub", "crs", None),
            P("sub", "crs", None),
            P("sub", "crs"),
            P("sub", "crs", None),
        ),
        out_specs=(P("sub", "crs", None, None), P("sub", "crs", None, None)),
        check_vma=False,
    )
```

```python
import functools

import jax
import jax.numpy as jnp
from jax import lax
from jax.experimental import pallas as pl
from jax.experimental.pallas import tpu as pltpu
from jax.sharding import PartitionSpec as P

F32 = jnp.float32
BF16 = jnp.bfloat16
ROWS = 8
LANES = 128
SLOT = 32
GROUP = LANES // SLOT
FOLD = ROWS // GROUP
VMEM_LIMIT = 24 << 20


def parts(x, count):
    out = []
    for _ in range(count):
        out.append(x.astype(BF16))
        x = x - out[-1].astype(F32)
    return out


def dot(a, b, transposed=False):
    dims = (((1,), (1 if transposed else 0,)), ((), ()))
    return lax.dot_general(a, b, dims, preferred_element_type=F32)


def exact(a, chosen, count, transposed=False):
    rows = a.shape[0]
    all_parts = dot(jnp.concatenate(parts(a, count), axis=0), chosen, transposed)
    return sum(all_parts[i * rows : (i + 1) * rows] for i in range(count))


def lows(index):
    rows = lax.broadcasted_iota(jnp.int32, (LANES, index.shape[1]), 0)
    return jnp.where(rows == (index & (LANES - 1)), 1.0, 0.0).astype(BF16)


def added_up(a, index, size):
    rows = a.shape[0]
    high = index >> 7
    stacked = [jnp.where(high == h, a, 0.0) for h in range(size // LANES)]
    out = exact(jnp.concatenate(stacked, axis=0), lows(index), 2, True)
    return jnp.concatenate([out[h * rows : (h + 1) * rows] for h in range(size // LANES)], axis=1)


def taken(a, index):
    rows, size = a.shape
    high = index >> 7
    stacked = [a[:, h * LANES : (h + 1) * LANES] for h in range(size // LANES)]
    out = exact(jnp.concatenate(stacked, axis=0), lows(index), 2)
    return sum(jnp.where(high == h, out[h * rows : (h + 1) * rows], 0.0) for h in range(size // LANES))


def product(a, high, low, transposed=False):
    rows = a.shape[0]
    top, rest = parts(a, 2)
    both = dot(jnp.concatenate([top, rest], axis=0), high, transposed)
    return both[:rows] + both[rows:] + dot(top, low, transposed)


def row_sum(x):
    return jnp.sum(x, axis=1, keepdims=True)


def padded(x, rows):
    return jnp.concatenate([x, jnp.zeros((rows - x.shape[0], x.shape[1]), x.dtype)], axis=0)


def fetched(pairs, sems):
    copies = [
        pltpu.make_async_copy(source, target, sems.at[i]) for i, (source, target) in enumerate(pairs)
    ]
    for copy in copies:
        copy.start()
    return copies


def always(body):
    pl.when(lax.axis_index("crs") >= 0)(body)


def pack_kernel(live_ref, jump_hbm, scale_hbm, nbr_hbm, out_ref, jump, scale, nbr, sems):
    for copy in fetched([(jump_hbm, jump), (scale_hbm, scale), (nbr_hbm, nbr)], sems):
        copy.wait()
    cases, _, records = jump.shape
    live = lax.broadcasted_iota(jnp.int32, (1, records), 1) < live_ref[0, 0]
    live = live.astype(F32)
    for case in range(cases):
        out_ref[case : case + 1] = jump[case] * live
    out_ref[cases : cases + 1] = scale[0] * live
    out_ref[cases + 1 : cases + 2] = nbr[0].astype(F32)


def unpacked(pack, cases):
    rows = lax.broadcasted_iota(jnp.int32, pack.shape, 0)
    residual = jnp.where(rows < cases, pack, 0.0)
    return residual, pack[cases : cases + 1], pack[cases + 1 : cases + 2].astype(jnp.int32)


def near_devices():
    chain, slabs = lax.axis_size("sub"), lax.axis_size("crs")
    here, slab = lax.axis_index("sub"), lax.axis_index("crs")
    return [lax.rem(here + step, chain) * slabs + slab for step in (chain - 1, 0, 1)]


def is_paired(width):
    return lax.axis_size("crs") == 4 and width & (width - 1) == 0


def block_at(slab, j, width):
    return slab ^ j if is_paired(width) else j


def by_turns(count):
    return count % 2 == 0


def dealt(right, left):
    if not by_turns(lax.axis_size("sub")):
        return right, left
    even = lax.rem(lax.axis_index("sub"), 2) == 0
    return jnp.where(even, right, left), jnp.where(even, left, right)


PIECES = 6


def pieces(source, target, count):
    rows = source.shape[2] // count
    at = [(0, 0, pl.ds(i * rows, rows)) for i in range(count)]
    return [(source.at[i], target.at[i]) for i in at]


def split_as_it_comes(copies, whole, high, low, first):
    rows = whole.shape[2] // len(copies)
    for i in range(first // rows, (first + high.shape[0]) // rows):
        copies[i].wait()
        at = slice(i * rows - first, (i + 1) * rows - first)
        high[at], low[at] = parts(whole[0, 0, i * rows : (i + 1) * rows], 2)


def half_of(slab, inverse_hbm):
    rows = 2 * inverse_hbm.shape[1]
    first = jnp.minimum(slab // 2 * rows, inverse_hbm.shape[0] - rows)
    return inverse_hbm.at[pl.ds(pl.multiple_of(first, 8), rows)]


def share_of_half(core, half):
    width = half.shape[1]
    own, other = [half[pl.ds(pl.multiple_of(c * width, width), width)] for c in (core, 1 - core)]
    rows = width // 2
    return jnp.concatenate(
        [own, jnp.where(core == 0, other[:rows], jnp.transpose(other[:, rows:]))], axis=0
    )


def far_solution(core, total, share):
    width = share.shape[1]
    rows = width // 2
    near, far = total[:, :width], total[:, width:]
    first = core == 0
    block = parts(share[:width], 2)
    across = parts(share[width:], 2)
    whole = product(jnp.where(first, far[:, :rows], near[:, rows:]), *across)
    piece = product(jnp.where(first, near, far), *across, True)
    none = jnp.zeros_like(piece)
    near = product(near, *block) + jnp.where(first, whole, jnp.concatenate([none, piece], axis=1))
    far = jnp.where(first, jnp.concatenate([piece, none], axis=1), whole)
    return jnp.concatenate([near, far], axis=1)


def prepare_kernel(
    cases, pack_ref, schur_hbm, coupling_hbm, own_hbm, corner_hbm, inverse_hbm,
    top_high, top_low, s_high, s_low, c_high, c_low, own_coupling, load_ref, index_ref, own_ref, share_ref,
    schur, coupling, own, corner, half, sems,
):
    copies = fetched(
        [
            (own_hbm, own),
            (coupling_hbm, coupling),
            (corner_hbm, corner),
            (half_of(lax.axis_index("crs"), inverse_hbm), half),
            *pieces(schur_hbm, schur, PIECES),
        ],
        sems,
    )
    for copy in copies[:3]:
        copy.wait()
    held, iface = coupling.shape[2:]
    block = padded(coupling[0, 0], SLOT)
    c_high[...], c_low[...] = parts(block, 2)
    own_ref[...] = own[0]
    own_coupling[...] = taken(block, own[0])[:held]
    residual, scale, _ = unpacked(pack_ref[...], cases)
    load_ref[...] = added_up(residual * scale, own[0], iface)
    lane = lax.broadcasted_iota(jnp.int32, (held, LANES), 1) % SLOT
    tiles = jnp.where(lane == lax.broadcasted_iota(jnp.int32, (held, LANES), 0), 1.0, 0.0)
    index = jnp.broadcast_to(corner[0].astype(F32), (ROWS, held))
    index_ref[...] = jnp.where(lane[:1] < held, exact(index, tiles.astype(BF16), 2)[:1], -1.0)
    copies[3].wait()
    share_ref[...] = share_of_half(lax.axis_index("crs") % 2, half)
    split_as_it_comes(copies[4:], schur, top_high, top_low, 0)
    split_as_it_comes(copies[4:], schur, s_high, s_low, top_high.shape[0])


def inverse_kernel(inverse_hbm, inv_high, inv_low, inverse, sems):
    blocks, width = lax.axis_size("crs"), inverse.shape[1]
    pairs = []
    for j in range(blocks):
        rows = pl.ds(pl.multiple_of(block_at(lax.axis_index("crs"), j, width) * width, width), width)
        pairs.append((inverse_hbm.at[rows], inverse.at[pl.ds(j * width, width)]))
    for copy in fetched(pairs, sems):
        copy.wait()
    inv_high[...], inv_low[...] = parts(inverse[...], 2)


def terms_kernel(rows_ref, schur_hbm, s_high, s_low, rest, sems):
    rows, left = rows_ref.shape[0], rest.shape[0]
    size = schur_hbm.shape[2]
    (copy,) = fetched([(schur_hbm.at[0, 0, pl.ds(size - left, left)], rest)], sems)

    @always
    def _():
        s_high[:rows], s_low[:rows] = parts(rows_ref[...], 2)

    copy.wait()
    s_high[rows:], s_low[rows:] = parts(rest[...], 2)


def schur_product(load, top_high, top_low, s_high, s_low):
    rows = top_high.shape[0]
    top = product(load[:, :rows], top_high[...], top_low[...])
    return top + product(load[:, rows:], s_high[...], s_low[...])


def forces(load, through, first, c_high, c_low, index_ref, cases, send_hbm, send, sems):
    force = product(load, c_high[...], c_low[...], True)
    force = jnp.concatenate([force] * GROUP, axis=1)
    lane = lax.broadcasted_iota(jnp.int32, force.shape, 1) % SLOT
    row = lax.broadcasted_iota(jnp.int32, force.shape, 0)
    force = jnp.where(lane == SLOT - 2, first, force)
    force = jnp.where(lane == SLOT - 1, row_sum(load * through), force)
    force = jnp.where(row == cases, index_ref[...], force)
    block = lax.broadcasted_iota(jnp.int32, force.shape, 1) // SLOT
    force = jnp.where(row // FOLD == block, force, 0.0)
    folded = sum(force[b * FOLD : (b + 1) * FOLD] for b in range(GROUP))
    send[...] = jnp.broadcast_to(folded[None], send.shape)
    (copy,) = fetched([(send, send_hbm)], sems)
    return copy


def unfolded(four):
    block = lax.broadcasted_iota(jnp.int32, four.shape, 1) // SLOT
    place = lax.broadcasted_iota(jnp.int32, four.shape, 0) // FOLD
    out = four
    for k in range(1, GROUP):
        turned = pltpu.roll(pltpu.roll(four, SLOT * k, 1), ROWS - FOLD * k, 0)
        out = jnp.where((block - place) % GROUP == k, turned, out)
    return out


def first_kernel(
    cases, left_ref, pack_ref, load_ref, own_coupling, index_ref,
    top_high, top_low, s_high, s_low, c_high, c_low, own_ref,
    send_hbm, one_ref, two_ref, index_out, send, sems,
):
    left_residual, left_scale, left_index = unpacked(left_ref[...], cases)
    index_out[...] = left_index
    iface = load_ref.shape[1]
    load = load_ref[...] - added_up(left_residual * left_scale, left_index, iface)
    through = schur_product(load, top_high, top_low, s_high, s_low)
    residual, scale, _ = unpacked(pack_ref[...], cases)
    norm = row_sum(residual * residual * scale)
    copy = forces(load, through, norm, c_high, c_low, index_ref, cases, send_hbm, send, sems)

    @always
    def _():
        held = own_coupling.shape[0]
        one_ref[:ROWS], two_ref[:ROWS] = dealt(
            taken(through, own_ref[...]), taken(through, left_index)
        )
        coupling = c_high[...].astype(F32) + c_low[...].astype(F32)
        one_ref[ROWS:], two_ref[ROWS:] = dealt(
            own_coupling[...], taken(coupling, left_index)[:held]
        )

    copy.wait()


def gathered_forces(cases, all_ref, corners, flip, sums_ref, total_ref):
    devices = all_ref.shape[0]
    chunk = min(devices, LANES // GROUP)
    row = lax.broadcasted_iota(jnp.int32, (ROWS, 1), 0)

    def add(at):
        pieces = [
            unfolded(jnp.concatenate([all_ref[at + group + e] for e in range(GROUP)], axis=0))
            for group in range(0, chunk, GROUP)
        ]
        sums = sum(pieces)
        for turn in (SLOT, 2 * SLOT):
            sums = sums + pltpu.roll(sums, turn, 1)
        flat = jnp.concatenate(pieces, axis=1)
        index = flat[cases : cases + 1].astype(jnp.int32) ^ flip
        force = jnp.where(row < cases, flat, 0.0)
        return sums, added_up(force, index, corners)

    sums_ref[...], total_ref[...] = add(0)
    if devices > chunk:

        @pl.loop(1, devices // chunk)
        def _(i):
            sums, total = add(i * chunk)
            sums_ref[...] += sums
            total_ref[...] += total


def near_index(cases, all_ref):
    lane = lax.broadcasted_iota(jnp.int32, (1, LANES), 1) // SLOT
    index = jnp.zeros((1, LANES), F32)
    for e, device in enumerate(near_devices()):
        rows = jnp.concatenate([all_ref[device]] * GROUP, axis=0)
        rows = pltpu.roll(rows, SLOT * (e - cases // FOLD) % LANES, 1)
        index = jnp.where(lane == e, rows[cases % FOLD : cases % FOLD + 1], index)
    return index.astype(jnp.int32)


def coarse_kernel(cases, all_ref, inv_high, inv_low, x_ref, total_ref, sums_ref, index_ref):
    gathered_forces(cases, all_ref, total_ref.shape[1], 0, sums_ref, total_ref)
    index_ref[...] = jnp.broadcast_to(near_index(cases, all_ref), index_ref.shape)
    x_ref[...] = product(total_ref[...], inv_high[...], inv_low[...])


def shared_coarse(cases, width, refs):
    *pieces, total_ref, sums_ref, index_ref, whole = refs
    for m, piece in enumerate(pieces):
        base = lax.rem(lax.axis_index("crs") + m, len(pieces)) * width
        whole[:, pl.ds(pl.multiple_of(base, width), width)] = piece[...]
    return whole[...], total_ref[...], sums_ref[...], index_ref[:1]


def pair_kernel(
    cases, first_row, all_ref, far_ref, inv_high, inv_low, schur_hbm, x_ref, total_ref, sums_ref, index_ref, *later,
):
    copies = []
    if later:
        rows, sems = later
        copies = fetched([(schur_hbm.at[0, 0, pl.ds(first_row, rows.shape[0])], rows)], sems)
    width = inv_high.shape[1]
    slab = lax.axis_index("crs")
    flip = slab * width

    @always
    def _():
        gathered_forces(cases, all_ref, 4 * width, flip, sums_ref, total_ref)
        index = near_index(cases, all_ref) ^ flip
        index_ref[...] = jnp.broadcast_to(index, index_ref.shape)
        total = total_ref[...]
        x_ref[:, :width] = product(total, inv_high[...], inv_low[...])
        x_ref[:, width : 2 * width] = jnp.zeros((ROWS, width), F32)
        across = product(total[:, :width], inv_high[2 * width :], inv_low[2 * width :], True)
        x_ref[:, 2 * width :] = across + far_solution(slab % 2, total[:, 2 * width :], far_ref[...])

    for copy in copies:
        copy.wait()


def paired_coarse(cases, width, refs):
    x_ref, other_ref, total_ref, sums_ref, index_ref = refs
    other = [other_ref[:, (j ^ 1) * width : (j ^ 1) * width + width] for j in range(4)]
    solution = x_ref[...] + jnp.concatenate(other, axis=1)
    return solution, total_ref[...], sums_ref[...], index_ref[:1]


def column(x, lane):
    return x[:, lane : lane + 1]


def second_kernel(cases, coarse, given, *refs):
    (
        pack_ref, left_ref, one_sent, two_sent, two_ref, one_ref,
        top_high, top_low, s_high, s_low, own_ref, left_index, c_high, c_low, corner_ref,
        send_hbm, out_ref, keep_ref, spread_ref, scalar_ref, send, sems,
    ) = refs[given : given + 22]
    solution, total, sums, index = coarse(refs[:given] + refs[given + 22 :])
    picked = taken(solution, index)
    right, back = dealt(one_sent[...], two_sent[...])
    from_right, from_left = dealt(one_ref[...], two_ref[...])
    blank = jnp.zeros((SLOT - (right.shape[0] - ROWS), right.shape[1]), F32)
    none = jnp.zeros((SLOT, right.shape[1]), F32)
    own = jnp.concatenate([none, right[ROWS:], blank, -from_right[ROWS:], blank, none], axis=0)
    other = jnp.concatenate([from_left[ROWS:], blank, -back[ROWS:], blank, none, none], axis=0)
    spread_ref[...] = own
    both = product(picked, *parts(jnp.concatenate([own, other], axis=1), 2))
    records = right.shape[1]
    residual, scale, _ = unpacked(pack_ref[...], cases)
    left_residual, left_scale, _ = unpacked(left_ref[...], cases)
    live = (scale > 0.0).astype(F32)
    left_live = (left_scale > 0.0).astype(F32)
    image = (right[:ROWS] - from_right[:ROWS] + both[:, :records]) * live
    left_image = (from_left[:ROWS] - back[:ROWS] + both[:, records:]) * left_live
    norm = column(sums, SLOT - 2)
    curvature = column(sums, SLOT - 1) + row_sum(total * solution)
    row = lax.broadcasted_iota(jnp.int32, (ROWS, 1), 0)
    alpha = jnp.where(row < cases, norm / curvature, 0.0)
    residual = residual - alpha * image
    left_residual = left_residual - alpha * left_image
    precon = scale * residual
    left_precon = left_scale * left_residual
    iface = c_high.shape[1]
    load = added_up(precon, own_ref[...], iface) - added_up(left_precon, left_index[...], iface)
    through = schur_product(load, top_high, top_low, s_high, s_low)
    norm_here = row_sum(residual * precon)
    copy = forces(load, through, norm_here, c_high, c_low, corner_ref, cases, send_hbm, send, sems)

    @always
    def _():
        out_ref[...] = taken(through, left_index[...])
        keep_ref[:ROWS] = taken(through, own_ref[...])
        keep_ref[ROWS:] = image
        lane = lax.broadcasted_iota(jnp.int32, scalar_ref.shape, 1)
        scalar_ref[...] = jnp.where(lane == 0, norm, alpha)

    copy.wait()


def last_kernel(cases, coarse, given, *refs):
    (
        pack_ref, from_right, keep_ref, spread_ref, scalar_ref, multipliers_ref, residual_ref,
    ) = refs[given : given + 7]
    solution, total, sums, index = coarse(refs[:given] + refs[given + 7 :])
    picked = taken(solution, index)
    residual, scale, _ = unpacked(pack_ref[...], cases)
    live = (scale > 0.0).astype(F32)
    spread = product(picked, *parts(spread_ref[...], 2))
    image = (keep_ref[:ROWS] - from_right[...] + spread) * live
    along = keep_ref[ROWS:]
    first_norm = column(scalar_ref[...], 0)
    first_alpha = column(scalar_ref[...], 1)
    norm = column(sums, SLOT - 2)
    curvature = column(sums, SLOT - 1) + row_sum(total * solution)
    ratio = norm / first_norm
    alpha = norm / (curvature - ratio * norm / first_alpha)
    direction = scale * residual
    multipliers = first_alpha * direction
    residual = residual - first_alpha * along
    direction = scale * residual + ratio * direction
    along = image + ratio * along
    multipliers = multipliers + alpha * direction
    residual = residual - alpha * along
    for case in range(cases):
        multipliers_ref[case] = multipliers[case : case + 1]
        residual_ref[case] = residual[case : case + 1]


VM = pl.BlockSpec(memory_space=pltpu.VMEM)
SM = pl.BlockSpec(memory_space=pltpu.SMEM)
HB = pl.BlockSpec(memory_space=pltpu.HBM)


def call(kernel, outs, given, specs, scratch=(), moved_bytes=None, stored=0):
    specs = specs + [VM] * (len(given) - len(specs))
    given = [
        pltpu.with_memory_space_constraint(x, pltpu.HBM) if spec is HB else x
        for x, spec in zip(given, specs)
    ]
    return pl.pallas_call(
        kernel,
        out_shape=[jax.ShapeDtypeStruct(shape, kind) for shape, kind in outs],
        in_specs=specs,
        out_specs=[HB] * stored + [VM] * (len(outs) - stored),
        scratch_shapes=list(scratch),
        cost_estimate=moved_bytes
        and pl.CostEstimate(flops=int(4e10) if moved_bytes<0 else 0, bytes_accessed=abs(moved_bytes), transcendentals=0),
        compiler_params=pltpu.CompilerParams(vmem_limit_bytes=VMEM_LIMIT),
    )(*given)


def passed_along(value, axis, steps):
    count = lax.axis_size(axis)
    pairs = [(source, (source + steps) % count) for source in range(count)]
    return lax.ppermute(value, axis, pairs)


def exchanged(value, axis, bit):
    pairs = [(source, source ^ bit) for source in range(lax.axis_size(axis))]
    return lax.ppermute(value, axis, pairs)


def per_device(
    jump_data,
    lumped_scale,
    schur_inverse,
    coarse_coupling,
    corner_inverse,
    own_dof,
    nbr_dof,
    live_count,
    corner_index,
):
    cases, records = jump_data.shape[2:]
    held, iface = coarse_coupling.shape[2:]
    corners, width = corner_inverse.shape
    chain, slabs = lax.axis_size("sub"), lax.axis_size("crs")
    devices = chain * slabs

    def buffers(*arrays):
        return [pltpu.VMEM(a.shape, a.dtype) for a in arrays] + [
            pltpu.SemaphoreType.DMA((len(arrays),))
        ]

    jump = jump_data.reshape(cases, 1, records)
    first = (jump, lumped_scale, nbr_dof)
    (pack,) = call(
        pack_kernel,
        [((ROWS, records), F32)],
        (live_count, *first),
        [SM] + [HB] * 3,
        buffers(*first),
    )
    left = passed_along(pack, "sub", 1)
    fetched_here = (schur_inverse, coarse_coupling, own_dof, corner_index)
    half = (2 * width, width)
    share = (width + width // 2, width)
    top = iface // 3 // LANES * LANES
    *tops, s_high, s_low, c_high, c_low, own_coupling, load, index, own, share = call(
        functools.partial(prepare_kernel, cases),
        [
            ((top, iface), BF16),
            ((top, iface), BF16),
            ((iface - top, iface), BF16),
            ((iface - top, iface), BF16),
            ((SLOT, iface), BF16),
            ((SLOT, iface), BF16),
            ((held, records), F32),
            ((ROWS, iface), F32),
            ((1, LANES), F32),
            ((1, records), jnp.int32),
            (share, F32),
        ],
        (pack, *fetched_here, corner_inverse),
        [VM] + [HB] * 5,
        [
            *buffers(*fetched_here)[:-1],
            pltpu.VMEM(half, F32),
            pltpu.SemaphoreType.DMA((4 + PIECES,)),
        ],
        32 << 20,
    )
    if is_paired(width):
        far = exchanged(share, "crs", 2)
    inv_high, inv_low = call(
        inverse_kernel,
        [((corners, width), BF16)] * 2,
        (corner_inverse,),
        [HB],
        [pltpu.VMEM((corners, width), F32), pltpu.SemaphoreType.DMA((slabs,))],
    )
    outgoing = [pltpu.VMEM((devices, FOLD, LANES), F32), pltpu.SemaphoreType.DMA((1,))]
    send, one_sent, two_sent, left_index = call(
        functools.partial(first_kernel, cases),
        [((devices, FOLD, LANES), F32)]
        + [((ROWS + held, records), F32)] * 2
        + [((1, records), jnp.int32)],
        (left, pack, load, own_coupling, index, *tops, s_high, s_low, c_high, c_low, own),
        [],
        outgoing,
        -1,
        stored=1,
    )

    more = iface // 64 * 16

    def gathered(send, beside, ahead):
        everyone = lax.all_to_all(send, ("sub", "crs"), 0, 0)
        row = (ROWS, corners)
        outs = [(row, F32), ((ROWS, LANES), F32), ((ROWS, LANES), jnp.int32)]
        if is_paired(width):
            x, total, sums, near, *fetched = call(
                functools.partial(pair_kernel, cases, top),
                [(row, F32), *outs] + [((more, iface), F32)] * ahead,
                (everyone, far, inv_high, inv_low, schur_inverse),
                [VM] * 4 + [HB],
                [pltpu.SemaphoreType.DMA((1,))] * ahead,
            )
            if beside is not None:
                x, _ = lax.optimization_barrier((x, beside))
            return (
                (x, exchanged(x, "crs", 1), total, sums, near),
                [VM] * 5,
                [],
                functools.partial(paired_coarse, cases, width),
                *fetched,
            )
        x, *others = call(
            functools.partial(coarse_kernel, cases),
            [((ROWS, width), F32), *outs],
            (everyone, inv_high, inv_low),
            [],
        )
        pieces = [x] + [passed_along(x, "crs", -m) for m in range(1, slabs)]
        return (
            (*pieces, *others),
            [VM] * (len(pieces) + len(others)),
            [pltpu.VMEM(row, F32)],
            functools.partial(shared_coarse, cases, width),
            *[schur_inverse[0, 0, top : top + more]] * ahead,
        )

    if by_turns(chain):
        rounds = [[(c, (c + 1) % chain) for c in range(start, chain, 2)] for start in (0, 1)]
        rounds = [pairs + [(b, a) for a, b in pairs] for pairs in rounds]
        two = lax.ppermute(two_sent, "sub", rounds[1])
        one = lax.ppermute(one_sent, "sub", rounds[0])
    else:
        one, two = passed_along(two_sent, "sub", -1), passed_along(one_sent, "sub", 1)
    given, specs, scratch, coarse, first_rows = gathered(send, None, 1)
    terms = call(
        terms_kernel,
        [((iface - top, iface), BF16)] * 2,
        (first_rows, schur_inverse),
        [VM, HB],
        [pltpu.VMEM((iface - top - more, iface), F32), pltpu.SemaphoreType.DMA((1,))],
    )
    send, out, keep, spread, scalars = call(
        functools.partial(second_kernel, cases, coarse, len(given)),
        [
            ((devices, FOLD, LANES), F32),
            ((ROWS, records), F32),
            ((2 * ROWS, records), F32),
            ((LANES, records), F32),
            ((ROWS, LANES), F32),
        ],
        (
            *given, pack, left, one_sent, two_sent, two, one,
            *tops, *terms, own, left_index, c_high, c_low, index,
        ),
        specs,
        outgoing + scratch,
        stored=1,
    )
    from_right = passed_along(out, "sub", -1)
    given, specs, scratch, coarse = gathered(send, from_right, 0)
    outs = call(
        functools.partial(last_kernel, cases, coarse, len(given)),
        [(jump.shape, F32), (jump.shape, F32)],
        (*given, pack, from_right, keep, spread, scalars),
        specs,
        scratch,
    )
    return tuple(out.reshape(jump_data.shape) for out in outs)


def solution(mesh):
    return jax.shard_map(
        per_device,
        mesh=mesh,
        in_specs=(
            P("sub", "crs", None, None),
            P("sub", "crs", None),
            P("sub", "crs", None, None),
            P("sub", "crs", None, None),
            P(None, "crs"),
            P("sub", "crs", None),
            P("sub", "crs", None),
            P("sub", "crs"),
            P("sub", "crs", None),
        ),
        out_specs=(P("sub", "crs", None, None), P("sub", "crs", None, None)),
        check_vma=False,
    )
```

```python
import functools

import jax
import jax.numpy as jnp
from jax import lax
from jax.experimental import pallas as pl
from jax.experimental.pallas import tpu as pltpu
from jax.sharding import PartitionSpec as P

F32 = jnp.float32
BF16 = jnp.bfloat16
ROWS = 8
LANES = 128
SLOT = 32
GROUP = LANES // SLOT
FOLD = ROWS // GROUP
VMEM_LIMIT = 24 << 20


def parts(x, count):
    out = []
    for _ in range(count):
        out.append(x.astype(BF16))
        x = x - out[-1].astype(F32)
    return out


def dot(a, b, transposed=False):
    dims = (((1,), (1 if transposed else 0,)), ((), ()))
    return lax.dot_general(a, b, dims, preferred_element_type=F32)


def exact(a, chosen, count, transposed=False):
    rows = a.shape[0]
    all_parts = dot(jnp.concatenate(parts(a, count), axis=0), chosen, transposed)
    return sum(all_parts[i * rows : (i + 1) * rows] for i in range(count))


def lows(index):
    rows = lax.broadcasted_iota(jnp.int32, (LANES, index.shape[1]), 0)
    return jnp.where(rows == (index & (LANES - 1)), 1.0, 0.0).astype(BF16)


def added_up(a, index, size):
    rows = a.shape[0]
    high = index >> 7
    stacked = [jnp.where(high == h, a, 0.0) for h in range(size // LANES)]
    out = exact(jnp.concatenate(stacked, axis=0), lows(index), 2, True)
    return jnp.concatenate([out[h * rows : (h + 1) * rows] for h in range(size // LANES)], axis=1)


def taken(a, index):
    rows, size = a.shape
    high = index >> 7
    stacked = [a[:, h * LANES : (h + 1) * LANES] for h in range(size // LANES)]
    out = exact(jnp.concatenate(stacked, axis=0), lows(index), 2)
    return sum(jnp.where(high == h, out[h * rows : (h + 1) * rows], 0.0) for h in range(size // LANES))


def product(a, high, low, transposed=False):
    rows = a.shape[0]
    top, rest = parts(a, 2)
    both = dot(jnp.concatenate([top, rest], axis=0), high, transposed)
    return both[:rows] + both[rows:] + dot(top, low, transposed)


def row_sum(x):
    return jnp.sum(x, axis=1, keepdims=True)


def padded(x, rows):
    return jnp.concatenate([x, jnp.zeros((rows - x.shape[0], x.shape[1]), x.dtype)], axis=0)


def fetched(pairs, sems):
    copies = [
        pltpu.make_async_copy(source, target, sems.at[i]) for i, (source, target) in enumerate(pairs)
    ]
    for copy in copies:
        copy.start()
    return copies


def always(body):
    pl.when(lax.axis_index("crs") >= 0)(body)


def pack_kernel(live_ref, jump_hbm, scale_hbm, nbr_hbm, out_ref, jump, scale, nbr, sems):
    for copy in fetched([(jump_hbm, jump), (scale_hbm, scale), (nbr_hbm, nbr)], sems):
        copy.wait()
    cases, _, records = jump.shape
    live = lax.broadcasted_iota(jnp.int32, (1, records), 1) < live_ref[0, 0]
    live = live.astype(F32)
    for case in range(cases):
        out_ref[case : case + 1] = jump[case] * live
    out_ref[cases : cases + 1] = scale[0] * live
    out_ref[cases + 1 : cases + 2] = nbr[0].astype(F32)


def unpacked(pack, cases):
    rows = lax.broadcasted_iota(jnp.int32, pack.shape, 0)
    residual = jnp.where(rows < cases, pack, 0.0)
    return residual, pack[cases : cases + 1], pack[cases + 1 : cases + 2].astype(jnp.int32)


def near_devices():
    chain, slabs = lax.axis_size("sub"), lax.axis_size("crs")
    here, slab = lax.axis_index("sub"), lax.axis_index("crs")
    return [lax.rem(here + step, chain) * slabs + slab for step in (chain - 1, 0, 1)]


def is_paired(width):
    return lax.axis_size("crs") == 4 and width & (width - 1) == 0


def block_at(slab, j, width):
    return slab ^ j if is_paired(width) else j


def by_turns(count):
    return count % 2 == 0


def dealt(right, left):
    if not by_turns(lax.axis_size("sub")):
        return right, left
    even = lax.rem(lax.axis_index("sub"), 2) == 0
    return jnp.where(even, right, left), jnp.where(even, left, right)


PIECES = 6


def pieces(source, target, count):
    rows = source.shape[2] // count
    at = [(0, 0, pl.ds(i * rows, rows)) for i in range(count)]
    return [(source.at[i], target.at[i]) for i in at]


def split_as_it_comes(copies, whole, high, low, first):
    rows = whole.shape[2] // len(copies)
    for i in range(first // rows, (first + high.shape[0]) // rows):
        copies[i].wait()
        at = slice(i * rows - first, (i + 1) * rows - first)
        high[at], low[at] = parts(whole[0, 0, i * rows : (i + 1) * rows], 2)


def half_of(slab, inverse_hbm):
    rows = 2 * inverse_hbm.shape[1]
    first = jnp.minimum(slab // 2 * rows, inverse_hbm.shape[0] - rows)
    return inverse_hbm.at[pl.ds(pl.multiple_of(first, 8), rows)]


def share_of_half(core, half):
    width = half.shape[1]
    own, other = [half[pl.ds(pl.multiple_of(c * width, width), width)] for c in (core, 1 - core)]
    rows = width // 2
    return jnp.concatenate(
        [own, jnp.where(core == 0, other[:rows], jnp.transpose(other[:, rows:]))], axis=0
    )


def far_solution(core, total, *share):
    width = share[0].shape[1]
    rows = width // 2
    near, far = total[:, :width], total[:, width:]
    first = core == 0
    block = [part[:width] for part in share]
    across = [part[width:] for part in share]
    whole = product(jnp.where(first, far[:, :rows], near[:, rows:]), *across)
    piece = product(jnp.where(first, near, far), *across, True)
    none = jnp.zeros_like(piece)
    near = product(near, *block) + jnp.where(first, whole, jnp.concatenate([none, piece], axis=1))
    far = jnp.where(first, jnp.concatenate([piece, none], axis=1), whole)
    return jnp.concatenate([near, far], axis=1)


def prepare_kernel(
    cases, pack_ref, schur_hbm, coupling_hbm, own_hbm, corner_hbm, inverse_hbm,
    top_high, top_low, s_high, s_low, c_high, c_low, own_coupling, load_ref, index_ref, own_ref, share_ref,
    schur, coupling, own, corner, half, sems,
):
    copies = fetched(
        [
            (own_hbm, own),
            (coupling_hbm, coupling),
            (corner_hbm, corner),
            (half_of(lax.axis_index("crs"), inverse_hbm), half),
            *pieces(schur_hbm, schur, PIECES),
        ],
        sems,
    )
    for copy in copies[:3]:
        copy.wait()
    held, iface = coupling.shape[2:]
    block = padded(coupling[0, 0], SLOT)
    c_high[...], c_low[...] = parts(block, 2)
    own_ref[...] = own[0]
    own_coupling[...] = taken(block, own[0])[:held]
    residual, scale, _ = unpacked(pack_ref[...], cases)
    load_ref[...] = added_up(residual * scale, own[0], iface)
    lane = lax.broadcasted_iota(jnp.int32, (held, LANES), 1) % SLOT
    tiles = jnp.where(lane == lax.broadcasted_iota(jnp.int32, (held, LANES), 0), 1.0, 0.0)
    index = jnp.broadcast_to(corner[0].astype(F32), (ROWS, held))
    index_ref[...] = jnp.where(lane[:1] < held, exact(index, tiles.astype(BF16), 2)[:1], -1.0)
    copies[3].wait()
    share_ref[...] = share_of_half(lax.axis_index("crs") % 2, half)
    split_as_it_comes(copies[4:], schur, top_high, top_low, 0)
    split_as_it_comes(copies[4:], schur, s_high, s_low, top_high.shape[0])


def inverse_kernel(far_ref, inverse_hbm, inv_high, inv_low, far_high, far_low, inverse, sems):
    blocks, width = lax.axis_size("crs"), inverse.shape[1]
    pairs = []
    for j in range(blocks):
        rows = pl.ds(pl.multiple_of(block_at(lax.axis_index("crs"), j, width) * width, width), width)
        pairs.append((inverse_hbm.at[rows], inverse.at[pl.ds(j * width, width)]))
    copies = fetched(pairs, sems)
    if far_ref is not None:

        @always
        def _():
            far_high[...], far_low[...] = parts(far_ref[...], 2)

    for copy in copies:
        copy.wait()
    inv_high[...], inv_low[...] = parts(inverse[...], 2)


def terms_kernel(rows_ref, schur_hbm, s_high, s_low, rest, sems):
    rows, left = rows_ref.shape[0], rest.shape[0]
    size = schur_hbm.shape[2]
    (copy,) = fetched([(schur_hbm.at[0, 0, pl.ds(size - left, left)], rest)], sems)

    @always
    def _():
        s_high[:rows], s_low[:rows] = parts(rows_ref[...], 2)

    copy.wait()
    s_high[rows:], s_low[rows:] = parts(rest[...], 2)


def schur_product(load, top_high, top_low, s_high, s_low):
    rows = top_high.shape[0]
    top = product(load[:, :rows], top_high[...], top_low[...])
    return top + product(load[:, rows:], s_high[...], s_low[...])


def forces(load, through, first, c_high, c_low, index_ref, cases, send_hbm, send, sems):
    force = product(load, c_high[...], c_low[...], True)
    force = jnp.concatenate([force] * GROUP, axis=1)
    lane = lax.broadcasted_iota(jnp.int32, force.shape, 1) % SLOT
    row = lax.broadcasted_iota(jnp.int32, force.shape, 0)
    force = jnp.where(lane == SLOT - 2, first, force)
    force = jnp.where(lane == SLOT - 1, row_sum(load * through), force)
    force = jnp.where(row == cases, index_ref[...], force)
    block = lax.broadcasted_iota(jnp.int32, force.shape, 1) // SLOT
    force = jnp.where(row // FOLD == block, force, 0.0)
    folded = sum(force[b * FOLD : (b + 1) * FOLD] for b in range(GROUP))
    send[...] = jnp.broadcast_to(folded[None], send.shape)
    (copy,) = fetched([(send, send_hbm)], sems)
    return copy


def unfolded(four):
    block = lax.broadcasted_iota(jnp.int32, four.shape, 1) // SLOT
    place = lax.broadcasted_iota(jnp.int32, four.shape, 0) // FOLD
    out = four
    for k in range(1, GROUP):
        turned = pltpu.roll(pltpu.roll(four, SLOT * k, 1), ROWS - FOLD * k, 0)
        out = jnp.where((block - place) % GROUP == k, turned, out)
    return out


def first_kernel(
    cases, left_ref, pack_ref, load_ref, own_coupling, index_ref,
    top_high, top_low, s_high, s_low, c_high, c_low, own_ref,
    send_hbm, one_ref, two_ref, index_out, send, sems,
):
    left_residual, left_scale, left_index = unpacked(left_ref[...], cases)
    index_out[...] = left_index
    iface = load_ref.shape[1]
    load = load_ref[...] - added_up(left_residual * left_scale, left_index, iface)
    through = schur_product(load, top_high, top_low, s_high, s_low)
    residual, scale, _ = unpacked(pack_ref[...], cases)
    norm = row_sum(residual * residual * scale)
    copy = forces(load, through, norm, c_high, c_low, index_ref, cases, send_hbm, send, sems)

    @always
    def _():
        held = own_coupling.shape[0]
        one_ref[:ROWS], two_ref[:ROWS] = dealt(
            taken(through, own_ref[...]), taken(through, left_index)
        )
        coupling = c_high[...].astype(F32) + c_low[...].astype(F32)
        one_ref[ROWS:], two_ref[ROWS:] = dealt(
            own_coupling[...], taken(coupling, left_index)[:held]
        )

    copy.wait()


def gathered_forces(cases, all_ref, corners, flip, sums_ref, total_ref):
    devices = all_ref.shape[0]
    chunk = min(devices, LANES // GROUP)
    row = lax.broadcasted_iota(jnp.int32, (ROWS, 1), 0)

    def add(at):
        pieces = [
            unfolded(jnp.concatenate([all_ref[at + group + e] for e in range(GROUP)], axis=0))
            for group in range(0, chunk, GROUP)
        ]
        sums = sum(pieces)
        for turn in (SLOT, 2 * SLOT):
            sums = sums + pltpu.roll(sums, turn, 1)
        flat = jnp.concatenate(pieces, axis=1)
        index = flat[cases : cases + 1].astype(jnp.int32) ^ flip
        force = jnp.where(row < cases, flat, 0.0)
        return sums, added_up(force, index, corners)

    sums_ref[...], total_ref[...] = add(0)
    if devices > chunk:

        @pl.loop(1, devices // chunk)
        def _(i):
            sums, total = add(i * chunk)
            sums_ref[...] += sums
            total_ref[...] += total


def near_index(cases, all_ref):
    lane = lax.broadcasted_iota(jnp.int32, (1, LANES), 1) // SLOT
    index = jnp.zeros((1, LANES), F32)
    for e, device in enumerate(near_devices()):
        rows = jnp.concatenate([all_ref[device]] * GROUP, axis=0)
        rows = pltpu.roll(rows, SLOT * (e - cases // FOLD) % LANES, 1)
        index = jnp.where(lane == e, rows[cases % FOLD : cases % FOLD + 1], index)
    return index.astype(jnp.int32)


def coarse_kernel(cases, all_ref, inv_high, inv_low, x_ref, total_ref, sums_ref, index_ref):
    gathered_forces(cases, all_ref, total_ref.shape[1], 0, sums_ref, total_ref)
    index_ref[...] = jnp.broadcast_to(near_index(cases, all_ref), index_ref.shape)
    x_ref[...] = product(total_ref[...], inv_high[...], inv_low[...])


def shared_coarse(cases, width, refs):
    *pieces, total_ref, sums_ref, index_ref, whole = refs
    for m, piece in enumerate(pieces):
        base = lax.rem(lax.axis_index("crs") + m, len(pieces)) * width
        whole[:, pl.ds(pl.multiple_of(base, width), width)] = piece[...]
    return whole[...], total_ref[...], sums_ref[...], index_ref[:1]


def pair_kernel(
    cases, first_row, all_ref, far_high, far_low, inv_high, inv_low, schur_hbm, x_ref, total_ref, sums_ref, index_ref, *later,
):
    copies = []
    if later:
        rows, sems = later
        copies = fetched([(schur_hbm.at[0, 0, pl.ds(first_row, rows.shape[0])], rows)], sems)
    width = inv_high.shape[1]
    slab = lax.axis_index("crs")
    flip = slab * width

    @always
    def _():
        gathered_forces(cases, all_ref, 4 * width, flip, sums_ref, total_ref)
        index = near_index(cases, all_ref) ^ flip
        index_ref[...] = jnp.broadcast_to(index, index_ref.shape)
        total = total_ref[...]
        x_ref[:, :width] = product(total, inv_high[...], inv_low[...])
        x_ref[:, width : 2 * width] = jnp.zeros((ROWS, width), F32)
        across = product(total[:, :width], inv_high[2 * width :], inv_low[2 * width :], True)
        x_ref[:, 2 * width :] = across + far_solution(slab % 2, total[:, 2 * width :], far_high, far_low)

    for copy in copies:
        copy.wait()


def paired_coarse(cases, width, refs):
    x_ref, other_ref, total_ref, sums_ref, index_ref = refs
    other = [other_ref[:, (j ^ 1) * width : (j ^ 1) * width + width] for j in range(4)]
    solution = x_ref[...] + jnp.concatenate(other, axis=1)
    return solution, total_ref[...], sums_ref[...], index_ref[:1]


def column(x, lane):
    return x[:, lane : lane + 1]


def second_kernel(cases, coarse, given, *refs):
    (
        pack_ref, left_ref, one_sent, two_sent, two_ref, one_ref,
        top_high, top_low, s_high, s_low, own_ref, left_index, c_high, c_low, corner_ref,
        send_hbm, out_ref, keep_ref, spread_ref, scalar_ref, send, sems,
    ) = refs[given : given + 22]
    solution, total, sums, index = coarse(refs[:given] + refs[given + 22 :])
    picked = taken(solution, index)
    right, back = dealt(one_sent[...], two_sent[...])
    from_right, from_left = dealt(one_ref[...], two_ref[...])
    blank = jnp.zeros((SLOT - (right.shape[0] - ROWS), right.shape[1]), F32)
    none = jnp.zeros((SLOT, right.shape[1]), F32)
    own = jnp.concatenate([none, right[ROWS:], blank, -from_right[ROWS:], blank, none], axis=0)
    other = jnp.concatenate([from_left[ROWS:], blank, -back[ROWS:], blank, none, none], axis=0)
    spread_ref[...] = own
    both = product(picked, *parts(jnp.concatenate([own, other], axis=1), 2))
    records = right.shape[1]
    residual, scale, _ = unpacked(pack_ref[...], cases)
    left_residual, left_scale, _ = unpacked(left_ref[...], cases)
    live = (scale > 0.0).astype(F32)
    left_live = (left_scale > 0.0).astype(F32)
    image = (right[:ROWS] - from_right[:ROWS] + both[:, :records]) * live
    left_image = (from_left[:ROWS] - back[:ROWS] + both[:, records:]) * left_live
    norm = column(sums, SLOT - 2)
    curvature = column(sums, SLOT - 1) + row_sum(total * solution)
    row = lax.broadcasted_iota(jnp.int32, (ROWS, 1), 0)
    alpha = jnp.where(row < cases, norm / curvature, 0.0)
    residual = residual - alpha * image
    left_residual = left_residual - alpha * left_image
    precon = scale * residual
    left_precon = left_scale * left_residual
    iface = c_high.shape[1]
    both_index = jnp.concatenate([own_ref[...], left_index[...]], axis=1)
    load = added_up(jnp.concatenate([precon, -left_precon], axis=1), both_index, iface)
    through = schur_product(load, top_high, top_low, s_high, s_low)
    norm_here = row_sum(residual * precon)
    copy = forces(load, through, norm_here, c_high, c_low, corner_ref, cases, send_hbm, send, sems)

    @always
    def _():
        out_ref[...] = taken(through, left_index[...])
        keep_ref[:ROWS] = taken(through, own_ref[...])
        keep_ref[ROWS:] = image
        lane = lax.broadcasted_iota(jnp.int32, scalar_ref.shape, 1)
        scalar_ref[...] = jnp.where(lane == 0, norm, alpha)

    copy.wait()


def last_kernel(cases, coarse, given, *refs):
    (
        pack_ref, from_right, keep_ref, spread_ref, scalar_ref, multipliers_ref, residual_ref,
    ) = refs[given : given + 7]
    solution, total, sums, index = coarse(refs[:given] + refs[given + 7 :])
    picked = taken(solution, index)
    residual, scale, _ = unpacked(pack_ref[...], cases)
    live = (scale > 0.0).astype(F32)
    spread = product(picked, *parts(spread_ref[...], 2))
    image = (keep_ref[:ROWS] - from_right[...] + spread) * live
    along = keep_ref[ROWS:]
    first_norm = column(scalar_ref[...], 0)
    first_alpha = column(scalar_ref[...], 1)
    norm = column(sums, SLOT - 2)
    curvature = column(sums, SLOT - 1) + row_sum(total * solution)
    ratio = norm / first_norm
    alpha = norm / (curvature - ratio * norm / first_alpha)
    direction = scale * residual
    multipliers = first_alpha * direction
    residual = residual - first_alpha * along
    direction = scale * residual + ratio * direction
    along = image + ratio * along
    multipliers = multipliers + alpha * direction
    residual = residual - alpha * along
    for case in range(cases):
        multipliers_ref[case] = multipliers[case : case + 1]
        residual_ref[case] = residual[case : case + 1]


VM = pl.BlockSpec(memory_space=pltpu.VMEM)
SM = pl.BlockSpec(memory_space=pltpu.SMEM)
HB = pl.BlockSpec(memory_space=pltpu.HBM)


def call(kernel, outs, given, specs, scratch=(), moved_bytes=None, stored=0):
    specs = specs + [VM] * (len(given) - len(specs))
    given = [
        pltpu.with_memory_space_constraint(x, pltpu.HBM) if spec is HB else x
        for x, spec in zip(given, specs)
    ]
    return pl.pallas_call(
        kernel,
        out_shape=[jax.ShapeDtypeStruct(shape, kind) for shape, kind in outs],
        in_specs=specs,
        out_specs=[HB] * stored + [VM] * (len(outs) - stored),
        scratch_shapes=list(scratch),
        cost_estimate=moved_bytes
        and pl.CostEstimate(flops=int(4e10) if moved_bytes<0 else 0, bytes_accessed=abs(moved_bytes), transcendentals=0),
        compiler_params=pltpu.CompilerParams(vmem_limit_bytes=VMEM_LIMIT),
    )(*given)


def passed_along(value, axis, steps):
    count = lax.axis_size(axis)
    pairs = [(source, (source + steps) % count) for source in range(count)]
    return lax.ppermute(value, axis, pairs)


def exchanged(value, axis, bit):
    pairs = [(source, source ^ bit) for source in range(lax.axis_size(axis))]
    return lax.ppermute(value, axis, pairs)


def per_device(
    jump_data,
    lumped_scale,
    schur_inverse,
    coarse_coupling,
    corner_inverse,
    own_dof,
    nbr_dof,
    live_count,
    corner_index,
):
    cases, records = jump_data.shape[2:]
    held, iface = coarse_coupling.shape[2:]
    corners, width = corner_inverse.shape
    chain, slabs = lax.axis_size("sub"), lax.axis_size("crs")
    devices = chain * slabs

    def buffers(*arrays):
        return [pltpu.VMEM(a.shape, a.dtype) for a in arrays] + [
            pltpu.SemaphoreType.DMA((len(arrays),))
        ]

    jump = jump_data.reshape(cases, 1, records)
    first = (jump, lumped_scale, nbr_dof)
    (pack,) = call(
        pack_kernel,
        [((ROWS, records), F32)],
        (live_count, *first),
        [SM] + [HB] * 3,
        buffers(*first),
    )
    left = passed_along(pack, "sub", 1)
    fetched_here = (schur_inverse, coarse_coupling, own_dof, corner_index)
    half = (2 * width, width)
    share = (width + width // 2, width)
    top = iface // 2 // LANES * LANES
    *tops, s_high, s_low, c_high, c_low, own_coupling, load, index, own, share = call(
        functools.partial(prepare_kernel, cases),
        [
            ((top, iface), BF16),
            ((top, iface), BF16),
            ((iface - top, iface), BF16),
            ((iface - top, iface), BF16),
            ((SLOT, iface), BF16),
            ((SLOT, iface), BF16),
            ((held, records), F32),
            ((ROWS, iface), F32),
            ((1, LANES), F32),
            ((1, records), jnp.int32),
            (share, F32),
        ],
        (pack, *fetched_here, corner_inverse),
        [VM] + [HB] * 5,
        [
            *buffers(*fetched_here)[:-1],
            pltpu.VMEM(half, F32),
            pltpu.SemaphoreType.DMA((4 + PIECES,)),
        ],
        32 << 20,
    )
    if is_paired(width):
        far = exchanged(share, "crs", 2)
    inverse_parts = [((corners, width), BF16)] * 2
    inverse_scratch = [pltpu.VMEM((corners, width), F32), pltpu.SemaphoreType.DMA((slabs,))]
    if is_paired(width):
        inv_high, inv_low, far_high, far_low = call(
            inverse_kernel,
            inverse_parts + [(far.shape, BF16)] * 2,
            (far, corner_inverse),
            [VM, HB],
            inverse_scratch,
        )
    else:
        inv_high, inv_low = call(
            lambda source, high, low, *rest: inverse_kernel(None, source, high, low, None, None, *rest),
            inverse_parts,
            (corner_inverse,),
            [HB],
            inverse_scratch,
        )
    outgoing = [pltpu.VMEM((devices, FOLD, LANES), F32), pltpu.SemaphoreType.DMA((1,))]
    send, one_sent, two_sent, left_index = call(
        functools.partial(first_kernel, cases),
        [((devices, FOLD, LANES), F32)]
        + [((ROWS + held, records), F32)] * 2
        + [((1, records), jnp.int32)],
        (left, pack, load, own_coupling, index, *tops, s_high, s_low, c_high, c_low, own),
        [],
        outgoing,
        -1,
        stored=1,
    )

    more = iface // 96 * 16

    def gathered(send, beside, ahead):
        everyone = lax.all_to_all(send, ("sub", "crs"), 0, 0)
        row = (ROWS, corners)
        outs = [(row, F32), ((ROWS, LANES), F32), ((ROWS, LANES), jnp.int32)]
        if is_paired(width):
            x, total, sums, near, *fetched = call(
                functools.partial(pair_kernel, cases, top),
                [(row, F32), *outs] + [((more, iface), F32)] * ahead,
                (everyone, far_high, far_low, inv_high, inv_low, schur_inverse),
                [VM] * 5 + [HB],
                [pltpu.SemaphoreType.DMA((1,))] * ahead,
            )
            if beside is not None:
                x, _ = lax.optimization_barrier((x, beside))
            return (
                (x, exchanged(x, "crs", 1), total, sums, near),
                [VM] * 5,
                [],
                functools.partial(paired_coarse, cases, width),
                *fetched,
            )
        x, *others = call(
            functools.partial(coarse_kernel, cases),
            [((ROWS, width), F32), *outs],
            (everyone, inv_high, inv_low),
            [],
        )
        pieces = [x] + [passed_along(x, "crs", -m) for m in range(1, slabs)]
        return (
            (*pieces, *others),
            [VM] * (len(pieces) + len(others)),
            [pltpu.VMEM(row, F32)],
            functools.partial(shared_coarse, cases, width),
            *[schur_inverse[0, 0, top : top + more]] * ahead,
        )

    if by_turns(chain):
        rounds = [[(c, (c + 1) % chain) for c in range(start, chain, 2)] for start in (0, 1)]
        rounds = [pairs + [(b, a) for a, b in pairs] for pairs in rounds]
        two = lax.ppermute(two_sent, "sub", rounds[1])
        one = lax.ppermute(one_sent, "sub", rounds[0])
    else:
        one, two = passed_along(two_sent, "sub", -1), passed_along(one_sent, "sub", 1)
    given, specs, scratch, coarse, first_rows = gathered(send, None, 1)
    terms = call(
        terms_kernel,
        [((iface - top, iface), BF16)] * 2,
        (first_rows, schur_inverse),
        [VM, HB],
        [pltpu.VMEM((iface - top - more, iface), F32), pltpu.SemaphoreType.DMA((1,))],
    )
    send, out, keep, spread, scalars = call(
        functools.partial(second_kernel, cases, coarse, len(given)),
        [
            ((devices, FOLD, LANES), F32),
            ((ROWS, records), F32),
            ((2 * ROWS, records), F32),
            ((LANES, records), F32),
            ((ROWS, LANES), F32),
        ],
        (
            *given, pack, left, one_sent, two_sent, two, one,
            *tops, *terms, own, left_index, c_high, c_low, index,
        ),
        specs,
        outgoing + scratch,
        stored=1,
    )
    from_right = passed_along(out, "sub", -1)
    given, specs, scratch, coarse = gathered(send, from_right, 0)
    outs = call(
        functools.partial(last_kernel, cases, coarse, len(given)),
        [(jump.shape, F32), (jump.shape, F32)],
        (*given, pack, from_right, keep, spread, scalars),
        specs,
        scratch,
    )
    return tuple(out.reshape(jump_data.shape) for out in outs)


def solution(mesh):
    return jax.shard_map(
        per_device,
        mesh=mesh,
        in_specs=(
            P("sub", "crs", None, None),
            P("sub", "crs", None),
            P("sub", "crs", None, None),
            P("sub", "crs", None, None),
            P(None, "crs"),
            P("sub", "crs", None),
            P("sub", "crs", None),
            P("sub", "crs"),
            P("sub", "crs", None),
        ),
        out_specs=(P("sub", "crs", None, None), P("sub", "crs", None, None)),
        check_vma=False,
    )
```

```python
import functools

import jax
import jax.numpy as jnp
from jax import lax
from jax.experimental import pallas as pl
from jax.experimental.pallas import tpu as pltpu
from jax.sharding import PartitionSpec as P

F32 = jnp.float32
BF16 = jnp.bfloat16
ROWS = 8
LANES = 128
SLOT = 32
GROUP = LANES // SLOT
FOLD = ROWS // GROUP
VMEM_LIMIT = 24 << 20


def parts(x, count):
    out = []
    for _ in range(count):
        out.append(x.astype(BF16))
        x = x - out[-1].astype(F32)
    return out


def dot(a, b, transposed=False):
    dims = (((1,), (1 if transposed else 0,)), ((), ()))
    return lax.dot_general(a, b, dims, preferred_element_type=F32)


def exact(a, chosen, count, transposed=False):
    rows = a.shape[0]
    all_parts = dot(jnp.concatenate(parts(a, count), axis=0), chosen, transposed)
    return sum(all_parts[i * rows : (i + 1) * rows] for i in range(count))


def lows(index):
    rows = lax.broadcasted_iota(jnp.int32, (LANES, index.shape[1]), 0)
    return jnp.where(rows == (index & (LANES - 1)), 1.0, 0.0).astype(BF16)


def added_up(a, index, size):
    rows = a.shape[0]
    high = index >> 7
    stacked = [jnp.where(high == h, a, 0.0) for h in range(size // LANES)]
    out = exact(jnp.concatenate(stacked, axis=0), lows(index), 2, True)
    return jnp.concatenate([out[h * rows : (h + 1) * rows] for h in range(size // LANES)], axis=1)


def taken(a, index):
    rows, size = a.shape
    high = index >> 7
    stacked = [a[:, h * LANES : (h + 1) * LANES] for h in range(size // LANES)]
    out = exact(jnp.concatenate(stacked, axis=0), lows(index), 2)
    return sum(jnp.where(high == h, out[h * rows : (h + 1) * rows], 0.0) for h in range(size // LANES))


def product(a, high, low, transposed=False):
    rows = a.shape[0]
    top, rest = parts(a, 2)
    both = dot(jnp.concatenate([top, rest], axis=0), high, transposed)
    return both[:rows] + both[rows:] + dot(top, low, transposed)


def row_sum(x):
    return jnp.sum(x, axis=1, keepdims=True)


def padded(x, rows):
    return jnp.concatenate([x, jnp.zeros((rows - x.shape[0], x.shape[1]), x.dtype)], axis=0)


def fetched(pairs, sems):
    copies = [
        pltpu.make_async_copy(source, target, sems.at[i]) for i, (source, target) in enumerate(pairs)
    ]
    for copy in copies:
        copy.start()
    return copies


def always(body):
    pl.when(lax.axis_index("crs") >= 0)(body)


def pack_kernel(live_ref, jump_hbm, scale_hbm, nbr_hbm, out_ref, jump, scale, nbr, sems):
    for copy in fetched([(jump_hbm, jump), (scale_hbm, scale), (nbr_hbm, nbr)], sems):
        copy.wait()
    cases, _, records = jump.shape
    live = lax.broadcasted_iota(jnp.int32, (1, records), 1) < live_ref[0, 0]
    live = live.astype(F32)
    for case in range(cases):
        out_ref[case : case + 1] = jump[case] * live
    out_ref[cases : cases + 1] = scale[0] * live
    out_ref[cases + 1 : cases + 2] = nbr[0].astype(F32)


def unpacked(pack, cases):
    rows = lax.broadcasted_iota(jnp.int32, pack.shape, 0)
    residual = jnp.where(rows < cases, pack, 0.0)
    return residual, pack[cases : cases + 1], pack[cases + 1 : cases + 2].astype(jnp.int32)


def near_devices():
    chain, slabs = lax.axis_size("sub"), lax.axis_size("crs")
    here, slab = lax.axis_index("sub"), lax.axis_index("crs")
    return [lax.rem(here + step, chain) * slabs + slab for step in (chain - 1, 0, 1)]


def is_paired(width):
    return lax.axis_size("crs") == 4 and width & (width - 1) == 0


def block_at(slab, j, width):
    return slab ^ j if is_paired(width) else j


def by_turns(count):
    return count % 2 == 0


def dealt(right, left):
    if not by_turns(lax.axis_size("sub")):
        return right, left
    even = lax.rem(lax.axis_index("sub"), 2) == 0
    return jnp.where(even, right, left), jnp.where(even, left, right)


PIECES = 6


def pieces(source, target, count):
    rows = source.shape[2] // count
    at = [(0, 0, pl.ds(i * rows, rows)) for i in range(count)]
    return [(source.at[i], target.at[i]) for i in at]


def split_as_it_comes(copies, whole, high, low, first):
    rows = whole.shape[2] // len(copies)
    for i in range(first // rows, (first + high.shape[0]) // rows):
        copies[i].wait()
        at = slice(i * rows - first, (i + 1) * rows - first)
        high[at], low[at] = parts(whole[0, 0, i * rows : (i + 1) * rows], 2)


def half_of(slab, inverse_hbm):
    rows = 2 * inverse_hbm.shape[1]
    first = jnp.minimum(slab // 2 * rows, inverse_hbm.shape[0] - rows)
    return inverse_hbm.at[pl.ds(pl.multiple_of(first, 8), rows)]


def share_of_half(core, half):
    width = half.shape[1]
    own, other = [half[pl.ds(pl.multiple_of(c * width, width), width)] for c in (core, 1 - core)]
    rows = width // 2
    return jnp.concatenate(
        [own, jnp.where(core == 0, other[:rows], jnp.transpose(other[:, rows:]))], axis=0
    )


def far_solution(core, total, *share):
    width = share[0].shape[1]
    rows = width // 2
    near, far = total[:, :width], total[:, width:]
    first = core == 0
    block = [part[:width] for part in share]
    across = [part[width:] for part in share]
    whole = product(jnp.where(first, far[:, :rows], near[:, rows:]), *across)
    piece = product(jnp.where(first, near, far), *across, True)
    none = jnp.zeros_like(piece)
    near = product(near, *block) + jnp.where(first, whole, jnp.concatenate([none, piece], axis=1))
    far = jnp.where(first, jnp.concatenate([piece, none], axis=1), whole)
    return jnp.concatenate([near, far], axis=1)


def prepare_kernel(
    cases, pack_ref, schur_hbm, coupling_hbm, own_hbm, corner_hbm, inverse_hbm,
    top_high, top_low, s_high, s_low, c_high, c_low, own_coupling, load_ref, index_ref, own_ref, share_ref,
    schur, coupling, own, corner, half, sems,
):
    copies = fetched(
        [
            (own_hbm, own),
            (coupling_hbm, coupling),
            (corner_hbm, corner),
            (half_of(lax.axis_index("crs"), inverse_hbm), half),
            *pieces(schur_hbm, schur, PIECES),
        ],
        sems,
    )
    for copy in copies[:3]:
        copy.wait()
    held, iface = coupling.shape[2:]
    block = padded(coupling[0, 0], SLOT)
    c_high[...], c_low[...] = parts(block, 2)
    own_ref[...] = own[0]
    own_coupling[...] = taken(block, own[0])[:held]
    residual, scale, _ = unpacked(pack_ref[...], cases)
    load_ref[...] = added_up(residual * scale, own[0], iface)
    lane = lax.broadcasted_iota(jnp.int32, (held, LANES), 1) % SLOT
    tiles = jnp.where(lane == lax.broadcasted_iota(jnp.int32, (held, LANES), 0), 1.0, 0.0)
    index = jnp.broadcast_to(corner[0].astype(F32), (ROWS, held))
    index_ref[...] = jnp.where(lane[:1] < held, exact(index, tiles.astype(BF16), 2)[:1], -1.0)
    copies[3].wait()
    share_ref[...] = share_of_half(lax.axis_index("crs") % 2, half)
    split_as_it_comes(copies[4:], schur, top_high, top_low, 0)
    split_as_it_comes(copies[4:], schur, s_high, s_low, top_high.shape[0])


def inverse_kernel(far_ref, inverse_hbm, inv_high, inv_low, far_high, far_low, inverse, sems):
    blocks, width = lax.axis_size("crs"), inverse.shape[1]
    pairs = []
    for j in range(blocks):
        rows = pl.ds(pl.multiple_of(block_at(lax.axis_index("crs"), j, width) * width, width), width)
        pairs.append((inverse_hbm.at[rows], inverse.at[pl.ds(j * width, width)]))
    copies = fetched(pairs, sems)
    if far_ref is not None:

        @always
        def _():
            far_high[...], far_low[...] = parts(far_ref[...], 2)

    for copy in copies:
        copy.wait()
    inv_high[...], inv_low[...] = parts(inverse[...], 2)


def terms_kernel(rows_ref, schur_hbm, s_high, s_low, rest, sems):
    rows, left = rows_ref.shape[0], rest.shape[0]
    size = schur_hbm.shape[2]
    (copy,) = fetched([(schur_hbm.at[0, 0, pl.ds(size - left, left)], rest)], sems)

    @always
    def _():
        s_high[:rows], s_low[:rows] = parts(rows_ref[...], 2)

    copy.wait()
    s_high[rows:], s_low[rows:] = parts(rest[...], 2)


def schur_product(load, top_high, top_low, s_high, s_low):
    rows = top_high.shape[0]
    top = product(load[:, :rows], top_high[...], top_low[...])
    return top + product(load[:, rows:], s_high[...], s_low[...])


def forces(load, through, first, c_high, c_low, index_ref, cases, send_hbm, send, sems):
    force = product(load, c_high[...], c_low[...], True)
    force = jnp.concatenate([force] * GROUP, axis=1)
    lane = lax.broadcasted_iota(jnp.int32, force.shape, 1) % SLOT
    row = lax.broadcasted_iota(jnp.int32, force.shape, 0)
    force = jnp.where(lane == SLOT - 2, first, force)
    force = jnp.where(lane == SLOT - 1, row_sum(load * through), force)
    force = jnp.where(row == cases, index_ref[...], force)
    block = lax.broadcasted_iota(jnp.int32, force.shape, 1) // SLOT
    force = jnp.where(row // FOLD == block, force, 0.0)
    folded = sum(force[b * FOLD : (b + 1) * FOLD] for b in range(GROUP))
    send[...] = jnp.broadcast_to(folded[None], send.shape)
    (copy,) = fetched([(send, send_hbm)], sems)
    return copy


def unfolded(four):
    block = lax.broadcasted_iota(jnp.int32, four.shape, 1) // SLOT
    place = lax.broadcasted_iota(jnp.int32, four.shape, 0) // FOLD
    out = four
    for k in range(1, GROUP):
        turned = pltpu.roll(pltpu.roll(four, SLOT * k, 1), ROWS - FOLD * k, 0)
        out = jnp.where((block - place) % GROUP == k, turned, out)
    return out


def first_kernel(
    cases, left_ref, pack_ref, load_ref, own_coupling, index_ref,
    top_high, top_low, s_high, s_low, c_high, c_low, own_ref,
    send_hbm, one_ref, two_ref, index_out, send, sems,
):
    left_residual, left_scale, left_index = unpacked(left_ref[...], cases)
    index_out[...] = left_index
    iface = load_ref.shape[1]
    load = load_ref[...] - added_up(left_residual * left_scale, left_index, iface)
    through = schur_product(load, top_high, top_low, s_high, s_low)
    residual, scale, _ = unpacked(pack_ref[...], cases)
    norm = row_sum(residual * residual * scale)
    copy = forces(load, through, norm, c_high, c_low, index_ref, cases, send_hbm, send, sems)

    @always
    def _():
        held = own_coupling.shape[0]
        slots = taken(through, jnp.concatenate([own_ref[...], left_index], axis=1))
        records = left_index.shape[1]
        one_ref[:ROWS], two_ref[:ROWS] = dealt(slots[:, :records], slots[:, records:])
        coupling = c_high[...].astype(F32) + c_low[...].astype(F32)
        one_ref[ROWS:], two_ref[ROWS:] = dealt(
            own_coupling[...], taken(coupling, left_index)[:held]
        )

    copy.wait()


def gathered_forces(cases, all_ref, corners, flip, sums_ref, total_ref):
    devices = all_ref.shape[0]
    chunk = min(devices, LANES // GROUP)
    row = lax.broadcasted_iota(jnp.int32, (ROWS, 1), 0)

    def add(at):
        pieces = [
            unfolded(jnp.concatenate([all_ref[at + group + e] for e in range(GROUP)], axis=0))
            for group in range(0, chunk, GROUP)
        ]
        sums = sum(pieces)
        for turn in (SLOT, 2 * SLOT):
            sums = sums + pltpu.roll(sums, turn, 1)
        flat = jnp.concatenate(pieces, axis=1)
        index = flat[cases : cases + 1].astype(jnp.int32) ^ flip
        force = jnp.where(row < cases, flat, 0.0)
        return sums, added_up(force, index, corners)

    sums_ref[...], total_ref[...] = add(0)
    if devices > chunk:

        @pl.loop(1, devices // chunk)
        def _(i):
            sums, total = add(i * chunk)
            sums_ref[...] += sums
            total_ref[...] += total


def near_index(cases, all_ref):
    lane = lax.broadcasted_iota(jnp.int32, (1, LANES), 1) // SLOT
    index = jnp.zeros((1, LANES), F32)
    for e, device in enumerate(near_devices()):
        rows = jnp.concatenate([all_ref[device]] * GROUP, axis=0)
        rows = pltpu.roll(rows, SLOT * (e - cases // FOLD) % LANES, 1)
        index = jnp.where(lane == e, rows[cases % FOLD : cases % FOLD + 1], index)
    return index.astype(jnp.int32)


def coarse_kernel(cases, all_ref, inv_high, inv_low, x_ref, total_ref, sums_ref, index_ref):
    gathered_forces(cases, all_ref, total_ref.shape[1], 0, sums_ref, total_ref)
    index_ref[...] = jnp.broadcast_to(near_index(cases, all_ref), index_ref.shape)
    x_ref[...] = product(total_ref[...], inv_high[...], inv_low[...])


def shared_coarse(cases, width, refs):
    *pieces, total_ref, sums_ref, index_ref, whole = refs
    for m, piece in enumerate(pieces):
        base = lax.rem(lax.axis_index("crs") + m, len(pieces)) * width
        whole[:, pl.ds(pl.multiple_of(base, width), width)] = piece[...]
    return whole[...], total_ref[...], sums_ref[...], index_ref[:1]


def pair_kernel(
    cases, first_row, all_ref, far_high, far_low, inv_high, inv_low, schur_hbm, x_ref, total_ref, sums_ref, index_ref, *later,
):
    copies = []
    if later:
        rows, sems = later
        copies = fetched([(schur_hbm.at[0, 0, pl.ds(first_row, rows.shape[0])], rows)], sems)
    width = inv_high.shape[1]
    slab = lax.axis_index("crs")
    flip = slab * width

    @always
    def _():
        gathered_forces(cases, all_ref, 4 * width, flip, sums_ref, total_ref)
        index = near_index(cases, all_ref) ^ flip
        index_ref[...] = jnp.broadcast_to(index, index_ref.shape)
        total = total_ref[...]
        x_ref[:, :width] = product(total, inv_high[...], inv_low[...])
        x_ref[:, width : 2 * width] = jnp.zeros((ROWS, width), F32)
        across = product(total[:, :width], inv_high[2 * width :], inv_low[2 * width :], True)
        x_ref[:, 2 * width :] = across + far_solution(slab % 2, total[:, 2 * width :], far_high, far_low)

    for copy in copies:
        copy.wait()


def paired_coarse(cases, width, refs):
    x_ref, other_ref, total_ref, sums_ref, index_ref = refs
    other = [other_ref[:, (j ^ 1) * width : (j ^ 1) * width + width] for j in range(4)]
    solution = x_ref[...] + jnp.concatenate(other, axis=1)
    return solution, total_ref[...], sums_ref[...], index_ref[:1]


def column(x, lane):
    return x[:, lane : lane + 1]


def second_kernel(cases, coarse, given, *refs):
    (
        pack_ref, left_ref, one_sent, two_sent, two_ref, one_ref,
        top_high, top_low, s_high, s_low, own_ref, left_index, c_high, c_low, corner_ref,
        send_hbm, out_ref, keep_ref, spread_ref, scalar_ref, send, sems,
    ) = refs[given : given + 22]
    solution, total, sums, index = coarse(refs[:given] + refs[given + 22 :])
    picked = taken(solution, index)
    right, back = dealt(one_sent[...], two_sent[...])
    from_right, from_left = dealt(one_ref[...], two_ref[...])
    blank = jnp.zeros((SLOT - (right.shape[0] - ROWS), right.shape[1]), F32)
    none = jnp.zeros((SLOT, right.shape[1]), F32)
    own = jnp.concatenate([none, right[ROWS:], blank, -from_right[ROWS:], blank, none], axis=0)
    other = jnp.concatenate([from_left[ROWS:], blank, -back[ROWS:], blank, none, none], axis=0)
    spread_ref[...] = own
    both = product(picked, *parts(jnp.concatenate([own, other], axis=1), 2))
    records = right.shape[1]
    residual, scale, _ = unpacked(pack_ref[...], cases)
    left_residual, left_scale, _ = unpacked(left_ref[...], cases)
    live = (scale > 0.0).astype(F32)
    left_live = (left_scale > 0.0).astype(F32)
    image = (right[:ROWS] - from_right[:ROWS] + both[:, :records]) * live
    left_image = (from_left[:ROWS] - back[:ROWS] + both[:, records:]) * left_live
    norm = column(sums, SLOT - 2)
    curvature = column(sums, SLOT - 1) + row_sum(total * solution)
    row = lax.broadcasted_iota(jnp.int32, (ROWS, 1), 0)
    alpha = jnp.where(row < cases, norm / curvature, 0.0)
    residual = residual - alpha * image
    left_residual = left_residual - alpha * left_image
    precon = scale * residual
    left_precon = left_scale * left_residual
    iface = c_high.shape[1]
    both_index = jnp.concatenate([own_ref[...], left_index[...]], axis=1)
    load = added_up(jnp.concatenate([precon, -left_precon], axis=1), both_index, iface)
    through = schur_product(load, top_high, top_low, s_high, s_low)
    norm_here = row_sum(residual * precon)
    copy = forces(load, through, norm_here, c_high, c_low, corner_ref, cases, send_hbm, send, sems)

    @always
    def _():
        out_ref[...] = taken(through, left_index[...])
        keep_ref[:ROWS] = taken(through, own_ref[...])
        keep_ref[ROWS:] = image
        lane = lax.broadcasted_iota(jnp.int32, scalar_ref.shape, 1)
        scalar_ref[...] = jnp.where(lane == 0, norm, alpha)

    copy.wait()


def last_kernel(cases, coarse, given, *refs):
    (
        pack_ref, from_right, keep_ref, spread_ref, scalar_ref, multipliers_ref, residual_ref,
    ) = refs[given : given + 7]
    solution, total, sums, index = coarse(refs[:given] + refs[given + 7 :])
    picked = taken(solution, index)
    residual, scale, _ = unpacked(pack_ref[...], cases)
    live = (scale > 0.0).astype(F32)
    spread = product(picked, *parts(spread_ref[...], 2))
    image = (keep_ref[:ROWS] - from_right[...] + spread) * live
    along = keep_ref[ROWS:]
    first_norm = column(scalar_ref[...], 0)
    first_alpha = column(scalar_ref[...], 1)
    norm = column(sums, SLOT - 2)
    curvature = column(sums, SLOT - 1) + row_sum(total * solution)
    ratio = norm / first_norm
    alpha = norm / (curvature - ratio * norm / first_alpha)
    direction = scale * residual
    multipliers = first_alpha * direction
    residual = residual - first_alpha * along
    direction = scale * residual + ratio * direction
    along = image + ratio * along
    multipliers = multipliers + alpha * direction
    residual = residual - alpha * along
    for case in range(cases):
        multipliers_ref[case] = multipliers[case : case + 1]
        residual_ref[case] = residual[case : case + 1]


VM = pl.BlockSpec(memory_space=pltpu.VMEM)
SM = pl.BlockSpec(memory_space=pltpu.SMEM)
HB = pl.BlockSpec(memory_space=pltpu.HBM)


def call(kernel, outs, given, specs, scratch=(), moved_bytes=None, stored=0):
    specs = specs + [VM] * (len(given) - len(specs))
    given = [
        pltpu.with_memory_space_constraint(x, pltpu.HBM) if spec is HB else x
        for x, spec in zip(given, specs)
    ]
    return pl.pallas_call(
        kernel,
        out_shape=[jax.ShapeDtypeStruct(shape, kind) for shape, kind in outs],
        in_specs=specs,
        out_specs=[HB] * stored + [VM] * (len(outs) - stored),
        scratch_shapes=list(scratch),
        cost_estimate=moved_bytes
        and pl.CostEstimate(flops=int(4e10) if moved_bytes<0 else 0, bytes_accessed=abs(moved_bytes), transcendentals=0),
        compiler_params=pltpu.CompilerParams(vmem_limit_bytes=VMEM_LIMIT),
    )(*given)


def passed_along(value, axis, steps):
    count = lax.axis_size(axis)
    pairs = [(source, (source + steps) % count) for source in range(count)]
    return lax.ppermute(value, axis, pairs)


def exchanged(value, axis, bit):
    pairs = [(source, source ^ bit) for source in range(lax.axis_size(axis))]
    return lax.ppermute(value, axis, pairs)


def per_device(
    jump_data,
    lumped_scale,
    schur_inverse,
    coarse_coupling,
    corner_inverse,
    own_dof,
    nbr_dof,
    live_count,
    corner_index,
):
    cases, records = jump_data.shape[2:]
    held, iface = coarse_coupling.shape[2:]
    corners, width = corner_inverse.shape
    chain, slabs = lax.axis_size("sub"), lax.axis_size("crs")
    devices = chain * slabs

    def buffers(*arrays):
        return [pltpu.VMEM(a.shape, a.dtype) for a in arrays] + [
            pltpu.SemaphoreType.DMA((len(arrays),))
        ]

    jump = jump_data.reshape(cases, 1, records)
    first = (jump, lumped_scale, nbr_dof)
    (pack,) = call(
        pack_kernel,
        [((ROWS, records), F32)],
        (live_count, *first),
        [SM] + [HB] * 3,
        buffers(*first),
    )
    left = passed_along(pack, "sub", 1)
    fetched_here = (schur_inverse, coarse_coupling, own_dof, corner_index)
    half = (2 * width, width)
    share = (width + width // 2, width)
    top = iface // 2 // LANES * LANES
    *tops, s_high, s_low, c_high, c_low, own_coupling, load, index, own, share = call(
        functools.partial(prepare_kernel, cases),
        [
            ((top, iface), BF16),
            ((top, iface), BF16),
            ((iface - top, iface), BF16),
            ((iface - top, iface), BF16),
            ((SLOT, iface), BF16),
            ((SLOT, iface), BF16),
            ((held, records), F32),
            ((ROWS, iface), F32),
            ((1, LANES), F32),
            ((1, records), jnp.int32),
            (share, F32),
        ],
        (pack, *fetched_here, corner_inverse),
        [VM] + [HB] * 5,
        [
            *buffers(*fetched_here)[:-1],
            pltpu.VMEM(half, F32),
            pltpu.SemaphoreType.DMA((4 + PIECES,)),
        ],
        32 << 20,
    )
    if is_paired(width):
        far = exchanged(share, "crs", 2)
    inverse_parts = [((corners, width), BF16)] * 2
    inverse_scratch = [pltpu.VMEM((corners, width), F32), pltpu.SemaphoreType.DMA((slabs,))]
    if is_paired(width):
        inv_high, inv_low, far_high, far_low = call(
            inverse_kernel,
            inverse_parts + [(far.shape, BF16)] * 2,
            (far, corner_inverse),
            [VM, HB],
            inverse_scratch,
        )
    else:
        inv_high, inv_low = call(
            lambda source, high, low, *rest: inverse_kernel(None, source, high, low, None, None, *rest),
            inverse_parts,
            (corner_inverse,),
            [HB],
            inverse_scratch,
        )
    outgoing = [pltpu.VMEM((devices, FOLD, LANES), F32), pltpu.SemaphoreType.DMA((1,))]
    send, one_sent, two_sent, left_index = call(
        functools.partial(first_kernel, cases),
        [((devices, FOLD, LANES), F32)]
        + [((ROWS + held, records), F32)] * 2
        + [((1, records), jnp.int32)],
        (left, pack, load, own_coupling, index, *tops, s_high, s_low, c_high, c_low, own),
        [],
        outgoing,
        -1,
        stored=1,
    )

    more = iface // 96 * 16

    def gathered(send, beside, ahead):
        everyone = lax.all_to_all(send, ("sub", "crs"), 0, 0)
        row = (ROWS, corners)
        outs = [(row, F32), ((ROWS, LANES), F32), ((ROWS, LANES), jnp.int32)]
        if is_paired(width):
            x, total, sums, near, *fetched = call(
                functools.partial(pair_kernel, cases, top),
                [(row, F32), *outs] + [((more, iface), F32)] * ahead,
                (everyone, far_high, far_low, inv_high, inv_low, schur_inverse),
                [VM] * 5 + [HB],
                [pltpu.SemaphoreType.DMA((1,))] * ahead,
            )
            if beside is not None:
                x, _ = lax.optimization_barrier((x, beside))
            return (
                (x, exchanged(x, "crs", 1), total, sums, near),
                [VM] * 5,
                [],
                functools.partial(paired_coarse, cases, width),
                *fetched,
            )
        x, *others = call(
            functools.partial(coarse_kernel, cases),
            [((ROWS, width), F32), *outs],
            (everyone, inv_high, inv_low),
            [],
        )
        pieces = [x] + [passed_along(x, "crs", -m) for m in range(1, slabs)]
        return (
            (*pieces, *others),
            [VM] * (len(pieces) + len(others)),
            [pltpu.VMEM(row, F32)],
            functools.partial(shared_coarse, cases, width),
            *[schur_inverse[0, 0, top : top + more]] * ahead,
        )

    if by_turns(chain):
        rounds = [[(c, (c + 1) % chain) for c in range(start, chain, 2)] for start in (0, 1)]
        rounds = [pairs + [(b, a) for a, b in pairs] for pairs in rounds]
        two = lax.ppermute(two_sent, "sub", rounds[1])
        one = lax.ppermute(one_sent, "sub", rounds[0])
    else:
        one, two = passed_along(two_sent, "sub", -1), passed_along(one_sent, "sub", 1)
    given, specs, scratch, coarse, first_rows = gathered(send, None, 1)
    terms = call(
        terms_kernel,
        [((iface - top, iface), BF16)] * 2,
        (first_rows, schur_inverse),
        [VM, HB],
        [pltpu.VMEM((iface - top - more, iface), F32), pltpu.SemaphoreType.DMA((1,))],
    )
    send, out, keep, spread, scalars = call(
        functools.partial(second_kernel, cases, coarse, len(given)),
        [
            ((devices, FOLD, LANES), F32),
            ((ROWS, records), F32),
            ((2 * ROWS, records), F32),
            ((LANES, records), F32),
            ((ROWS, LANES), F32),
        ],
        (
            *given, pack, left, one_sent, two_sent, two, one,
            *tops, *terms, own, left_index, c_high, c_low, index,
        ),
        specs,
        outgoing + scratch,
        stored=1,
    )
    from_right = passed_along(out, "sub", -1)
    given, specs, scratch, coarse = gathered(send, from_right, 0)
    outs = call(
        functools.partial(last_kernel, cases, coarse, len(given)),
        [(jump.shape, F32), (jump.shape, F32)],
        (*given, pack, from_right, keep, spread, scalars),
        specs,
        scratch,
    )
    return tuple(out.reshape(jump_data.shape) for out in outs)


def solution(mesh):
    return jax.shard_map(
        per_device,
        mesh=mesh,
        in_specs=(
            P("sub", "crs", None, None),
            P("sub", "crs", None),
            P("sub", "crs", None, None),
            P("sub", "crs", None, None),
            P(None, "crs"),
            P("sub", "crs", None),
            P("sub", "crs", None),
            P("sub", "crs"),
            P("sub", "crs", None),
        ),
        out_specs=(P("sub", "crs", None, None), P("sub", "crs", None, None)),
        check_vma=False,
    )
```
